32 devices in a mesh: dp: 4 (over z), row: 4 (over y, core), col: 2 (over x).
Axes of the slice: x: 2, y: 2, z: 4, core: 2. Of those that a mesh axis runs over, the one named last changes fastest.
Arguments:
- tokens: bfloat16 [8192, 1152], P('dp', ('row', 'col')), may hold values from -6 to 6
- cotangent: bfloat16 [8192, 1152], P('dp', ('row', 'col')), may hold values from -6 to 6
- weight_query: bfloat16 [1152, 1024], P('row', 'col'), may hold values from -0.1875 to 0.1875
- weight_key: bfloat16 [1152, 256], P('row', 'col'), may hold values from -0.1875 to 0.1875
- weight_value: bfloat16 [1152, 256], P('row', 'col'), may hold values from -0.1875 to 0.1875
- weight_out: bfloat16 [1024, 1152], P('col', 'row'), may hold values from -0.1875 to 0.1875
- weight_gate: bfloat16 [1152, 6912], P('row', 'col'), may hold values from -0.1875 to 0.1875
- weight_up: bfloat16 [1152, 6912], P('row', 'col'), may hold values from -0.1875 to 0.1875
- weight_down: bfloat16 [6912, 1152], P('col', 'row'), may hold values from -0.078125 to 0.078125
- gain_input: float32 [1152], P(('row', 'col')), may hold values from -0.5 to 1
- gain_attn: float32 [1152], P(('row', 'col')), may hold values from -0.5 to 1
- gain_pre: float32 [1152], P(('row', 'col')), may hold values from -0.5 to 1
- gain_post: float32 [1152], P(('row', 'col')), may hold values from -0.5 to 1
- gain_query: float32 [256], replicated, may hold values from -0.5 to 1
- gain_key: float32 [256], replicated, may hold values from -0.5 to 1
- doc_lengths: int32 [4, 3], P('dp'), may hold values from 1 to 1792, 2048 in all within a row
- block_size: int32 [1], replicated, may hold values from 128 to 512
Outputs:
- layer_out: bfloat16 [8192, 1152], P('dp', ('row', 'col'))
- grad_tokens: float32 [8192, 1152], P('dp', ('row', 'col'))
- grad_weight_query: float32 [1152, 1024], P('row', 'col')
- grad_weight_key: float32 [1152, 256], P('row', 'col')
- grad_weight_value: float32 [1152, 256], P('row', 'col')
- grad_weight_out: float32 [1024, 1152], P('col', 'row')
- grad_weight_gate: float32 [1152, 6912], P('row', 'col')
- grad_weight_up: float32 [1152, 6912], P('row', 'col')
- grad_weight_down: float32 [6912, 1152], P('col', 'row')
- grad_gain_input: float32 [1152], P(('row', 'col'))
- grad_gain_attn: float32 [1152], P(('row', 'col'))
- grad_gain_pre: float32 [1152], P(('row', 'col'))
- grad_gain_post: float32 [1152], P(('row', 'col'))
- grad_gain_query: float32 [256], replicated
- grad_gain_key: float32 [256], replicated
The draws below stay inside these ranges and needn't reach their ends.
Inputs may be any that keep to these rules, and one draw needn't show every extreme that they name: `doc_lengths`: each row sums to 2048; its longest document has exactly 1792 tokens. `block_size`: one block size for all documents.
All inputs are finite; a program needn't handle non-finite values.
Results may differ from the reference program's by a relative error of at most 0.017.
Values may be sent and summed in bfloat16 or wider, within the bound.
A program may use at most 192 MiB of HBM per device.

```python
import math
import jax
import jax.numpy as jnp
import numpy as np
from jax import lax

D = 1152
FF = 6912
HEADS = 4
HD = 256
TOK_DEV = 2048
DOCS = 3
BLOCK = 256
QD = 1024
TOKENS = 8192
N_DP = 4


def levels(own_key, shape, pieces, low, high):
    def one(axis_at, parts):
        heights = jax.random.uniform(jax.random.fold_in(jax.random.fold_in(own_key, 6), axis_at), (parts,), jnp.float32, low / len(pieces), high / len(pieces))
        return jnp.repeat(jnp.exp(heights), shape[axis_at] // parts).reshape((-1,) + (1,) * (len(shape) - axis_at - 1))

    level = one(*pieces[0])
    for cut in pieces[1:]:
        level = level * one(*cut)
    return level


def profile(number_of, total, bound, lean):
    weights = [(1 << 20) // math.isqrt(rank ** lean) + 1 for rank in range(2, number_of + 1)]
    spare, given = total - bound - (number_of - 1), [1] * (number_of - 1)
    while spare > 0:
        movable = [i for i in range(number_of - 1) if given[i] < bound]
        whole, left = sum([weights[i] for i in movable]), spare
        for i in movable:
            addition = min(bound - given[i], max(1, left * weights[i] // whole), spare)
            given[i] = given[i] + addition
            spare = spare - addition
    return np.array([bound] + given)


def ragged(own_key, count, total, bound, lean):
    if count == 2:
        one = jax.random.randint(own_key, (), max(1, total - bound), min(bound, total - 1) + 1)
        return jnp.stack([one, total - one])
    sizes = jnp.asarray(profile(count, total, bound, lean), jnp.int32)
    twos = (count - 1) // 2
    donor, taker = sizes[1:1 + 2 * twos:2], sizes[2:2 + 2 * twos:2]
    slack = jnp.minimum(donor - 1, bound - taker)
    shifted = jax.random.randint(jax.random.fold_in(own_key, 1), (twos,), 0, 1 << 20) % (slack + 1)
    sizes = sizes.at[1:1 + 2 * twos:2].set(donor - shifted).at[2:2 + 2 * twos:2].set(taker + shifted)
    return sizes[jax.random.permutation(jax.random.fold_in(own_key, 2), count)]


def centred(key, shape, width, limit, shards=(), kind=jnp.bfloat16):
    loudness = levels(key, shape, shards, -0.22, 0.18) if shards else 1.0
    values = jax.random.normal(key, shape, jnp.float32) * width * loudness
    return jnp.minimum(jnp.maximum(values, -limit), limit).astype(kind)


def setup_inputs(seed: int = 0) -> dict:
    key_list = jax.random.split(jax.random.key(seed), 18)
    tokens = centred(key_list[0], (TOKENS, D), 1.0, 6.0, ((0, 4), (1, 8)))
    cotangent = centred(key_list[1], (TOKENS, D), 1.0, 6.0, ((0, 4), (1, 8)))
    weight_query = centred(key_list[2], (D, QD), D ** -0.5, 0.1875, ((0, 4), (1, 2)))
    weight_key = centred(key_list[3], (D, HD), D ** -0.5, 0.1875, ((0, 4), (1, 2)))
    weight_value = centred(key_list[4], (D, HD), D ** -0.5, 0.1875, ((0, 4), (1, 2)))
    weight_out = centred(key_list[5], (QD, D), QD ** -0.5, 0.1875, ((0, 2), (1, 4)))
    weight_gate = centred(key_list[6], (D, FF), D ** -0.5, 0.1875, ((0, 4), (1, 2)))
    weight_up = centred(key_list[7], (D, FF), D ** -0.5, 0.1875, ((0, 4), (1, 2)))
    weight_down = centred(key_list[8], (FF, D), FF ** -0.5, 0.078125, ((0, 2), (1, 4)))
    gain_input = jnp.clip(-0.5 + 1.5 * jax.random.uniform(key_list[9], (D,), jnp.float32) ** levels(key_list[9], (D,), ((0, 8),), -0.2, 0.2), -0.5, 1.0)
    gain_attn = jnp.clip(-0.5 + 1.5 * jax.random.uniform(key_list[10], (D,), jnp.float32) ** levels(key_list[10], (D,), ((0, 8),), -0.2, 0.2), -0.5, 1.0)
    gain_pre = jnp.clip(-0.5 + 1.5 * jax.random.uniform(key_list[11], (D,), jnp.float32) ** levels(key_list[11], (D,), ((0, 8),), -0.2, 0.2), -0.5, 1.0)
    gain_post = jnp.clip(-0.5 + 1.5 * jax.random.uniform(key_list[12], (D,), jnp.float32) ** levels(key_list[12], (D,), ((0, 8),), -0.2, 0.2), -0.5, 1.0)
    gain_query = jnp.clip(jax.random.uniform(key_list[13], (HD,), jnp.float32, -0.5, 1.0), -0.5, 1.0)
    gain_key = jnp.clip(jax.random.uniform(key_list[14], (HD,), jnp.float32, -0.5, 1.0), -0.5, 1.0)
    doc_lengths = jax.vmap(lambda own: ragged(own, DOCS, TOK_DEV, TOK_DEV - TOK_DEV // 8, 0))(jax.random.split(key_list[15], N_DP)).reshape((N_DP, DOCS)).astype(jnp.int32)
    block_size = jax.random.randint(key_list[16], (1,), BLOCK // 2, 2 * BLOCK + 1).astype(jnp.int32)
    return {"tokens": tokens, "cotangent": cotangent, "weight_query": weight_query, "weight_key": weight_key, "weight_value": weight_value, "weight_out": weight_out, "weight_gate": weight_gate, "weight_up": weight_up, "weight_down": weight_down, "gain_input": gain_input, "gain_attn": gain_attn, "gain_pre": gain_pre, "gain_post": gain_post, "gain_query": gain_query, "gain_key": gain_key, "doc_lengths": doc_lengths, "block_size": block_size}


EPS = 1e-06
ROPE_BASE = 1000000.0
GELU_C = 0.7978845608028654
HIGHEST = lax.Precision.HIGHEST

@jax.custom_vjp
def low(v):
    return lax.optimization_barrier(v.astype(jnp.bfloat16)).astype(jnp.float32)

@jax.custom_vjp
def low_back(v):
    return v

def low_keep(v):
    return (low(v), None)

def low_pass(kept, grad):
    return (grad,)

def back_keep(v):
    return (v, None)

def back_low(kept, grad):
    return (low(grad),)
low.defvjp(low_keep, low_pass)
low_back.defvjp(back_keep, back_low)

def product(left, right):
    return jnp.dot(left, right, precision=HIGHEST, preferred_element_type=jnp.float32)

def rms_norm(values, scales):
    mean_square = lax.optimization_barrier(jnp.mean(values * values, axis=-1, keepdims=True))
    return values * lax.rsqrt(mean_square + EPS) * (1.0 + scales)

def rotate(values, cos_table, sin_table):
    half_width = values.shape[-1] // 2
    first_half = values[..., :half_width]
    second_half = values[..., half_width:]
    return jnp.concatenate([first_half * cos_table - second_half * sin_table, second_half * cos_table + first_half * sin_table], axis=-1)

def gelu_tanh(values):
    return 0.5 * values * (1.0 + jnp.tanh(GELU_C * (values + 0.044715 * values * values * values)))

def positions(lengths, tok_count):
    doc_ends = jnp.cumsum(lengths, dtype=jnp.int32)
    doc_starts = doc_ends - lengths
    token_ids = jnp.arange(tok_count, dtype=jnp.int32)
    document = lax.optimization_barrier(jnp.sum((token_ids[:, None] >= doc_ends[None, :]).astype(jnp.int32), axis=1, dtype=jnp.int32))
    doc_ids = jnp.arange(lengths.shape[0], dtype=jnp.int32)
    doc_first = lax.optimization_barrier(jnp.sum(jnp.where(doc_ids[None, :] == document[:, None], doc_starts[None, :], 0), axis=1, dtype=jnp.int32))
    return (document, token_ids - doc_first)

def angles(places):
    half_width = HD // 2
    frequency = jnp.exp(jnp.arange(half_width, dtype=jnp.float32) * (-2.0 * math.log(ROPE_BASE) / HD))
    phases = places.astype(jnp.float32)[:, None] * frequency[None, :]
    return (jnp.cos(phases), jnp.sin(phases))

def decoder_layer(inputs, weights, cos_table, sin_table, allowed):
    weight_query, weight_key, weight_value, weight_out, weight_gate, weight_up, weight_down, gain_input, gain_attn, gain_pre, gain_post, gain_query, gain_key = weights
    tok_count = inputs.shape[0]
    query_scale = 1.0 / math.sqrt(HD)
    normed = low(rms_norm(inputs, gain_input))
    query_pre = low_back(product(normed, weight_query)).reshape(tok_count, HEADS, HD)
    key_pre = low_back(product(normed, weight_key))
    value_rows = low(low_back(product(normed, weight_value)))
    queries = low(rotate(rms_norm(query_pre, gain_query), cos_table[:, None, :], sin_table[:, None, :]) * query_scale)
    keys_out = low(rotate(rms_norm(key_pre, gain_key), cos_table, sin_table))
    scores = low_back(jnp.einsum('thd,sd->hts', queries, keys_out, precision=HIGHEST))
    scores = jnp.where(allowed[None, :, :], scores, -1e+30)
    attn_probs = low(jax.nn.softmax(scores, axis=-1))
    head_out = low(low_back(jnp.einsum('hts,sd->thd', attn_probs, value_rows, precision=HIGHEST)))
    head_out = head_out.reshape(tok_count, HEADS * HD)
    attn_out = low_back(product(head_out, weight_out))
    residual = inputs + rms_norm(attn_out, gain_attn)
    pre_normed = low(rms_norm(residual, gain_pre))
    gate_rows = low_back(product(pre_normed, weight_gate))
    up_rows = low_back(product(pre_normed, weight_up))
    hidden = low(gelu_tanh(gate_rows) * up_rows)
    mlp_out = low_back(product(hidden, weight_down))
    return residual + rms_norm(mlp_out, gain_post)

def reference(tokens, cotangent, weight_query, weight_key, weight_value, weight_out, weight_gate, weight_up, weight_down, gain_input, gain_attn, gain_pre, gain_post, gain_query, gain_key, doc_lengths, block_size):
    params = (weight_query.astype(jnp.float32), weight_key.astype(jnp.float32), weight_value.astype(jnp.float32), weight_out.astype(jnp.float32), weight_gate.astype(jnp.float32), weight_up.astype(jnp.float32), weight_down.astype(jnp.float32), gain_input.astype(jnp.float32), gain_attn.astype(jnp.float32), gain_pre.astype(jnp.float32), gain_post.astype(jnp.float32), gain_query.astype(jnp.float32), gain_key.astype(jnp.float32))
    block_span = block_size[0]

    def one_pack(totals, pack_index):
        row_start = pack_index * TOK_DEV
        pack_rows = lax.dynamic_slice_in_dim(tokens, row_start, TOK_DEV, 0).astype(jnp.float32)
        grad_pack = lax.dynamic_slice_in_dim(cotangent, row_start, TOK_DEV, 0).astype(jnp.float32)
        document, places = positions(doc_lengths[pack_index], TOK_DEV)
        allowed = (document[None, :] == document[:, None]) & (places[None, :] // block_span <= places[:, None] // block_span)
        cos_table, sin_table = angles(places)

        def forward(pack_in, weights):
            return decoder_layer(pack_in, weights, cos_table, sin_table, allowed)
        result, pull_back = jax.vjp(forward, pack_rows, params)
        grad_input, grad_params = pull_back(grad_pack)
        totals = tuple((running + update for running, update in zip(totals, grad_params)))
        return (totals, (result.astype(jnp.bfloat16), grad_input))
    initial = tuple((jnp.zeros(member.shape, jnp.float32) for member in params))
    totals, (outputs, grad_inputs) = lax.scan(one_pack, initial, jnp.arange(N_DP, dtype=jnp.int32))
    return (outputs.reshape(TOKENS, D), grad_inputs.reshape(TOKENS, D), totals[0], totals[1], totals[2], totals[3], totals[4], totals[5], totals[6], totals[7], totals[8], totals[9], totals[10], totals[11], totals[12])
```

```python
import math

import jax
import jax.numpy as jnp
from jax import lax
from jax.experimental import pallas as pl
from jax.experimental.pallas import tpu as pltpu
from jax.sharding import PartitionSpec as P

HD = 256
EPS = 1e-06
ROPE_BASE = 1000000.0
GELU_C = 0.7978845608028654
BF = jnp.bfloat16
F32 = jnp.float32
PLANE = ("row", "col")


def dot(left, right, dims):
    return lax.dot_general(left, right, (dims, ((), ())), preferred_element_type=F32)


def nn(left, right):
    return dot(left, right, ((1,), (0,)))


def nt(left, right):
    return dot(left, right, ((1,), (1,)))


def tn(left, right):
    return dot(left, right, ((0,), (0,)))


def gelu_tanh(values):
    return 0.5 * values * (1.0 + jnp.tanh(GELU_C * (values + 0.044715 * values * values * values)))


def rotate(values, cos_table, sin_table):
    half_width = values.shape[-1] // 2
    first_half = values[..., :half_width]
    second_half = values[..., half_width:]
    return jnp.concatenate(
        [
            first_half * cos_table - second_half * sin_table,
            second_half * cos_table + first_half * sin_table,
        ],
        axis=-1,
    )


def head_norm(values, scales, cos_table, sin_table):
    mean_square = jnp.mean(values * values, axis=-1, keepdims=True)
    return rotate(values * lax.rsqrt(mean_square + EPS) * (1.0 + scales), cos_table, sin_table)


def positions(lengths, token_ids):
    doc_ends = jnp.cumsum(lengths, dtype=jnp.int32)
    doc_starts = doc_ends - lengths
    document = jnp.sum(
        (token_ids[:, None] >= doc_ends[None, :]).astype(jnp.int32), axis=1, dtype=jnp.int32
    )
    doc_ids = jnp.arange(lengths.shape[0], dtype=jnp.int32)
    doc_first = jnp.sum(
        jnp.where(doc_ids[None, :] == document[:, None], doc_starts[None, :], 0),
        axis=1,
        dtype=jnp.int32,
    )
    return (document, token_ids - doc_first)


def angles(places):
    half_width = HD // 2
    frequency = jnp.exp(
        jnp.arange(half_width, dtype=jnp.float32) * (-2.0 * math.log(ROPE_BASE) / HD)
    )
    phases = places.astype(jnp.float32)[:, None] * frequency[None, :]
    return (jnp.cos(phases), jnp.sin(phases))


def norm(values, scales):
    inverse = lax.rsqrt(jnp.mean(values * values, axis=1, keepdims=True) + EPS)
    return (values * inverse * (1.0 + scales), inverse)


def norm_back(values, scales, inverse, upstream):
    scaled = upstream * (1.0 + scales)
    inner = jnp.mean(scaled * values, axis=1, keepdims=True)
    grad_values = scaled * inverse - values * inverse * inverse * inverse * inner
    return (grad_values, jnp.sum(upstream * values * inverse, axis=0))


MESH = pl.DeviceIdType.MESH
TILE = 256
VMEM_LIMIT = 64 * 1024 * 1024 - 512 * 1024


def whereabouts():
    place, row, col = lax.axis_index("dp"), lax.axis_index("row"), lax.axis_index("col")
    return place, row, col, row // 2, row % 2


def peers():
    place, row, col, high, core = whereabouts()
    far = row + 2 - 4 * high
    return (
        (place, row, 1 - col),
        (place, far, col),
        (place, far, 1 - col),
        (place, row + 1 - 2 * core, col),
    )


def remote(src, dst, send, recv, device):
    return pltpu.make_async_remote_copy(
        src_ref=src, dst_ref=dst, send_sem=send, recv_sem=recv, device_id=device, device_id_type=MESH
    )


def greet(devices):
    barrier = pltpu.get_barrier_semaphore()
    for device in devices:
        pl.semaphore_signal(barrier, inc=1, device_id=device, device_id_type=MESH)
    pl.semaphore_wait(barrier, len(devices))


def any_spec():
    return pl.BlockSpec(memory_space=pl.ANY)


def vmem_spec():
    return pl.BlockSpec(memory_space=pltpu.VMEM)


def params(number):
    return pltpu.CompilerParams(
        collective_id=number, has_side_effects=True, vmem_limit_bytes=VMEM_LIMIT
    )


def entry_kernel(tk, ct, wa, wm, tk_out, ct_out, wa_out, wm_out, tk_s, tk_r, ct_s, ct_r, wa_s, wa_r, wm_s, wm_r, loc):
    place, row, col, high, core = whereabouts()
    depth = wa.shape[0]
    slab = wm_out.shape[2]
    me = 2 * row + col
    px, py, pd, pc = peers()
    others = []
    for step in range(1, 8):
        r2, c2 = (row + step // 2) % 4, (col + step) % 2
        others.append((2 * r2 + c2, (place, r2, c2)))
    greet([device for _, device in others])
    copies = []

    def start(copy):
        copy.start()
        copies.append(copy)
        return copy

    for i, (index, device) in enumerate(others):
        start(remote(tk.at[index], tk_out.at[me], tk_s.at[i], tk_r.at[i], device))
    local = [
        pltpu.make_async_copy(tk.at[me], tk_out.at[me], loc.at[0]),
        pltpu.make_async_copy(ct.at[me], ct_out.at[me], loc.at[1]),
        pltpu.make_async_copy(wa, wa_out.at[col, pl.ds(row * depth, depth)], loc.at[2]),
        pltpu.make_async_copy(
            wm.at[:, :, pl.ds(high * slab, slab)], wm_out.at[:, pl.ds(row * depth, depth)], loc.at[3]
        ),
    ]
    for copy in local:
        copy.start()
    slot = wa_out.at[col, pl.ds(row * depth, depth)]
    first = [start(remote(wa, slot, wa_s.at[i], wa_r.at[i], p)) for i, p in enumerate((px, py, pd, pc))]
    mine = pl.ds(high * slab, slab)
    away = pl.ds((1 - high) * slab, slab)
    rows = pl.ds(row * depth, depth)
    far_row = row + 2 - 4 * high
    far_rows = pl.ds(far_row * depth, depth)
    over = []
    for m in range(3):
        over.append(start(remote(wm.at[m, :, away], wm_out.at[m, rows], wm_s.at[m, 0], wm_r.at[m, 0], py)))
        start(remote(wm.at[m, :, mine], wm_out.at[m, rows], wm_s.at[m, 1], wm_r.at[m, 1], pc))
    for i, (index, device) in enumerate(others):
        start(remote(ct.at[index], ct_out.at[me], ct_s.at[i], ct_r.at[i], device))
    relay = []
    for i, (r2, c2) in enumerate(((row, 1 - col), (far_row, col), (far_row, 1 - col))):
        first[i].wait_recv()
        part = wa_out.at[c2, pl.ds(r2 * depth, depth)]
        relay.append(remote(part, part, wa_s.at[4 + i], wa_r.at[4 + i], pc))
        relay[-1].start()
    for m in range(3):
        over[m].wait_recv()
        part = wm_out.at[m, far_rows]
        relay.append(remote(part, part, wm_s.at[m, 2], wm_r.at[m, 2], pc))
        relay[-1].start()
    waited = first[:3] + over
    for copy in copies:
        copy.wait_send()
        if not any(copy is other for other in waited):
            copy.wait_recv()
    for copy in relay:
        copy.wait()
    for copy in local:
        copy.wait()


def entry(tk, ct, wa, wm):
    depth, feats = wa.shape
    slab = wm.shape[2] // 2
    dma = pltpu.SemaphoreType.DMA
    return pl.pallas_call(
        entry_kernel,
        out_shape=(
            jax.ShapeDtypeStruct(tk.shape, BF),
            jax.ShapeDtypeStruct(ct.shape, BF),
            jax.ShapeDtypeStruct((2, 4 * depth, feats), BF),
            jax.ShapeDtypeStruct((3, 4 * depth, slab), BF),
        ),
        in_specs=[any_spec()] * 4,
        out_specs=[any_spec()] * 4,
        scratch_shapes=[
            dma((7,)), dma((7,)), dma((7,)), dma((7,)), dma((7,)), dma((7,)),
            dma((3, 3)), dma((3, 3)), dma((4,)),
        ],
        compiler_params=params(1),
        name="entry",
    )(tk, ct, wa, wm)


KV_SLOTS = (0, 1, 4, 5)


def kv_kernel(kv, out, send, recv, loc):
    px, py, pd, pc = peers()
    greet((px, py, pd, pc))
    own = pltpu.make_async_copy(kv, out.at[0], loc)
    own.start()
    first = [
        remote(kv, out.at[slot], send.at[i], recv.at[i], device)
        for i, (slot, device) in enumerate(((1, px), (4, py), (5, pd), (2, pc)))
    ]
    for copy in first:
        copy.start()
    relay = []
    for i, slot in enumerate((1, 4, 5)):
        first[i].wait_recv()
        copy = remote(out.at[slot], out.at[slot + 2], send.at[4 + i], recv.at[4 + i], pc)
        copy.start()
        relay.append(copy)
    for copy in first:
        copy.wait_send()
    first[3].wait_recv()
    for copy in relay:
        copy.wait()
    own.wait()


def kv_gather(kv):
    dma = pltpu.SemaphoreType.DMA
    return pl.pallas_call(
        kv_kernel,
        out_shape=jax.ShapeDtypeStruct((8,) + kv.shape, BF),
        in_specs=[any_spec()],
        out_specs=any_spec(),
        scratch_shapes=[dma((7,)), dma((7,)), dma(())],
        compiler_params=params(2),
        name="kv_gather",
    )(kv)


def mlp_kernel(
    pre, res, ct, gpost, wg_h, wu_h, wd_h,
    lo, dgpost, dpre, grads,
    wg, wu, wd, pre_all, pre_t, gm_all, gm_t, aa, bb, hh, acc, own, parts, prc, prc2, dwb, crecv,
    w_sem, ag_s, ag_r, rs_s, rs_r, gs_s, gs_r, bs_s, bs_r, c_s, c_r, y_s, y_r, l_s,
):
    place, row, col, high, core = whereabouts()
    px, py, pd, pc = peers()
    quad = (px, py, pd)
    loc, width = pre.shape
    slab = wg.shape[1]
    tiles = slab // TILE
    depth = crecv.shape[3]
    loads = [
        pltpu.make_async_copy(src, dst, w_sem.at[i])
        for i, (src, dst) in enumerate(((wg_h, wg), (wu_h, wu), (wd_h, wd)))
    ]
    for copy in loads:
        copy.start()
    greet((px, py, pd, pc))

    def spread(src, buffer, send, recv):
        copies = [remote(src, buffer.at[i + 1], send.at[i], recv.at[i], p) for i, p in enumerate(quad)]
        for copy in copies:
            copy.start()
        return copies

    def lanes(n):
        return pl.ds(pl.multiple_of(n * TILE, TILE), TILE)

    gathers = spread(pre, pre_all, ag_s, ag_r)
    pre_all[0] = pre[...]
    for copy in loads:
        copy.wait()

    scatters = []
    for j in range(4):
        if j:
            gathers[j - 1].wait_recv()
        acc[...] = jnp.zeros_like(acc)
        rows = pl.ds(j * loc, loc)

        def forward(n, carry, j=j, rows=rows):
            x = pre_all[j]
            gate = nn(x, wg[:, lanes(n)])
            up = nn(x, wu[:, lanes(n)])
            square = gate * gate
            bend = jnp.tanh(GELU_C * gate * (1.0 + 0.044715 * square))
            half = 0.5 * (1.0 + bend)
            gelu = gate * half
            slope = half + 0.5 * gate * (1.0 - bend * bend) * (GELU_C * (1.0 + 0.134145 * square))
            hidden = (gelu * up).astype(BF)
            aa[rows, lanes(n)] = gelu.astype(BF)
            bb[rows, lanes(n)] = (up * slope).astype(BF)
            hh[rows, lanes(n)] = hidden
            acc[...] += nt(hidden, wd[:, lanes(n)])
            return carry

        lax.fori_loop(0, tiles, forward, 0)
        if j:
            parts[j - 1] = acc[...].astype(BF)
            copy = remote(parts.at[j - 1], prc.at[j - 1], rs_s.at[j - 1], rs_r.at[j - 1], quad[j - 1])
            copy.start()
            scatters.append(copy)
        else:
            own[...] = acc[...]
    for j in range(4):
        pre_t[:, j * loc : (j + 1) * loc] = pre_all[j].T
    for copy in scatters:
        copy.wait()
    out = own[...] + prc[0].astype(F32) + prc[1].astype(F32) + prc[2].astype(F32)
    scale = 1.0 + gpost[...]
    inverse = lax.rsqrt(jnp.mean(out * out, axis=1, keepdims=True) + EPS)
    lo[...] = (res[...] + out * inverse * scale).astype(BF)
    upstream = ct[...].astype(F32)
    scaled = upstream * scale
    inner = jnp.mean(scaled * out, axis=1, keepdims=True)
    gm_all[0] = (scaled * inverse - out * (inverse * inverse * inverse * inner)).astype(BF)
    dgpost[...] = jnp.sum(upstream * out * inverse, axis=0, keepdims=True)

    gathers2 = spread(gm_all.at[0], gm_all, gs_s, gs_r)
    scatters2 = []
    for j in range(4):
        if j:
            gathers2[j - 1].wait_recv()
        acc[...] = jnp.zeros_like(acc)
        rows = pl.ds(j * loc, loc)

        def backward(n, carry, j=j, rows=rows):
            grad_hidden = nn(gm_all[j], wd[:, lanes(n)])
            grad_gate = (grad_hidden * bb[rows, lanes(n)].astype(F32)).astype(BF)
            grad_up = (grad_hidden * aa[rows, lanes(n)].astype(F32)).astype(BF)
            bb[rows, lanes(n)] = grad_gate
            aa[rows, lanes(n)] = grad_up
            acc[...] += nt(grad_gate, wg[:, lanes(n)]) + nt(grad_up, wu[:, lanes(n)])
            return carry

        lax.fori_loop(0, tiles, backward, 0)
        gm_t[:, j * loc : (j + 1) * loc] = gm_all[j].T
        if j:
            parts[j - 1] = acc[...].astype(BF)
            copy = remote(parts.at[j - 1], prc2.at[j - 1], bs_s.at[j - 1], bs_r.at[j - 1], quad[j - 1])
            copy.start()
            scatters2.append(copy)
        else:
            own[...] = acc[...]

    def to_core(n, m, y2):
        return remote(
            dwb.at[n % 2, m, 2 * y2 + 1 - core], crecv.at[m, n, y2], c_s.at[n % 2, m, y2], c_r.at[m, n, y2], pc
        )

    def to_far(n, m):
        return remote(crecv.at[m, n, 1 - high], grads.at[m, n, 1], y_s.at[m, n], y_r.at[m, n], py)

    def to_out(n, m):
        return pltpu.make_async_copy(crecv.at[m, n, high], grads.at[m, n, 0], l_s.at[m, n])

    def produce(n):
        for m, (left, right) in enumerate(((pre_t, bb), (pre_t, aa), (gm_t, hh))):
            product = nn(left[...], right[:, lanes(n)]).astype(BF)
            dwb[n % 2, m] = product.reshape(4, depth, TILE)
            for y2 in range(2):
                to_core(n, m, y2).start()

    def settle(n):
        for m in range(3):
            for y2 in range(2):
                to_core(n, m, y2).wait()
                crecv[m, n, y2] = (
                    crecv[m, n, y2].astype(F32) + dwb[n % 2, m, 2 * y2 + core].astype(F32)
                ).astype(BF)
            to_far(n, m).start()
            to_out(n, m).start()

    produce(0)

    def step(n, carry):
        produce(n)
        settle(n - 1)
        return carry

    lax.fori_loop(1, tiles, step, 0)
    settle(tiles - 1)
    for copy in scatters2:
        copy.wait()
    dpre[...] = own[...] + prc2[0].astype(F32) + prc2[1].astype(F32) + prc2[2].astype(F32)

    def finish(n, carry):
        for m in range(3):
            to_far(n, m).wait()
            to_out(n, m).wait()
        return carry

    lax.fori_loop(0, tiles, finish, 0)
    for copy in gathers + gathers2:
        copy.wait_send()


def mlp(pre, res, ct, gpost, w_gate, w_up, w_down):
    loc, width = pre.shape
    slab = w_gate.shape[1]
    tiles = slab // TILE
    depth = width // 4
    dma = pltpu.SemaphoreType.DMA
    return pl.pallas_call(
        mlp_kernel,
        out_shape=(
            jax.ShapeDtypeStruct((loc, width), BF),
            jax.ShapeDtypeStruct((1, width), F32),
            jax.ShapeDtypeStruct((loc, width), F32),
            jax.ShapeDtypeStruct((3, tiles, 2, depth, TILE), BF),
        ),
        in_specs=[vmem_spec()] * 4 + [any_spec()] * 3,
        out_specs=[vmem_spec()] * 3 + [any_spec()],
        scratch_shapes=[
            pltpu.VMEM((width, slab), BF),
            pltpu.VMEM((width, slab), BF),
            pltpu.VMEM((width, slab), BF),
            pltpu.VMEM((4, loc, width), BF),
            pltpu.VMEM((width, 4 * loc), BF),
            pltpu.VMEM((4, loc, width), BF),
            pltpu.VMEM((width, 4 * loc), BF),
            pltpu.VMEM((4 * loc, slab), BF),
            pltpu.VMEM((4 * loc, slab), BF),
            pltpu.VMEM((4 * loc, slab), BF),
            pltpu.VMEM((loc, width), F32),
            pltpu.VMEM((loc, width), F32),
            pltpu.VMEM((3, loc, width), BF),
            pltpu.VMEM((3, loc, width), BF),
            pltpu.VMEM((3, loc, width), BF),
            pltpu.VMEM((2, 3, 4, depth, TILE), BF),
            pltpu.VMEM((3, tiles, 2, depth, TILE), BF),
            dma((3,)),
            dma((3,)), dma((3,)), dma((3,)), dma((3,)), dma((3,)), dma((3,)), dma((3,)), dma((3,)),
            dma((2, 3, 2)), dma((3, tiles, 2)), dma((3, tiles)), dma((3, tiles)), dma((3, tiles)),
        ],
        compiler_params=params(3),
        name="feed_forward",
    )(pre, res, ct, gpost, w_gate, w_up, w_down)


def kv_sum_kernel(parts, out, cr, summed, qr, c_s, c_r, q_s, q_r):
    px, py, pd, pc = peers()
    greet((px, py, pd, pc))
    core = [
        remote(parts.at[slot + 2], cr.at[i], c_s.at[i], c_r.at[i], pc) for i, slot in enumerate(KV_SLOTS)
    ]
    for copy in core:
        copy.start()
    sends = []
    for i, device in ((3, pd), (1, px), (2, py), (0, None)):
        core[i].wait_recv()
        total = parts[KV_SLOTS[i]].astype(F32) + cr[i].astype(F32)
        if device is None:
            out[...] = total
        else:
            summed[i - 1] = total.astype(BF)
            copy = remote(summed.at[i - 1], qr.at[i - 1], q_s.at[i - 1], q_r.at[i - 1], device)
            copy.start()
            sends.append(copy)
    for copy in sends:
        copy.wait()
    out[...] += qr[0].astype(F32) + qr[1].astype(F32) + qr[2].astype(F32)
    for copy in core:
        copy.wait_send()


def kv_sum(parts):
    shape = parts.shape[1:]
    dma = pltpu.SemaphoreType.DMA
    return pl.pallas_call(
        kv_sum_kernel,
        out_shape=jax.ShapeDtypeStruct(shape, F32),
        in_specs=[vmem_spec()],
        out_specs=vmem_spec(),
        scratch_shapes=[
            pltpu.VMEM((4,) + shape, BF),
            pltpu.VMEM((3,) + shape, BF),
            pltpu.VMEM((3,) + shape, BF),
            dma((4,)), dma((4,)), dma((3,)), dma((3,)),
        ],
        compiler_params=params(4),
        name="kv_sum",
    )(parts)


def attn_sum_kernel(parts, out, cr, summed, qr, c_s, c_r, q_s, q_r):
    place, row, col, high, core = whereabouts()
    px, py, pd, pc = peers()
    greet((px, py, pd, pc))
    wanted = ((1 - col, 1 - high, pd), (1 - col, high, px), (col, 1 - high, py), (col, high, None))
    copies = [
        remote(parts.at[c2, 2 * y2 + 1 - core], cr.at[c2, y2], c_s.at[i], c_r.at[c2, y2], pc)
        for i, (c2, y2, _) in enumerate(wanted)
    ]
    for copy in copies:
        copy.start()
    sends = []
    for i, (c2, y2, device) in enumerate(wanted):
        copies[i].wait_recv()
        total = parts[c2, 2 * y2 + core].astype(F32) + cr[c2, y2].astype(F32)
        if device is None:
            own = total
        else:
            summed[i] = total.astype(BF)
            copy = remote(summed.at[i], qr.at[i], q_s.at[i], q_r.at[i], device)
            copy.start()
            sends.append(copy)
    for copy in sends:
        copy.wait()
    out[...] = (own + qr[0].astype(F32) + qr[1].astype(F32) + qr[2].astype(F32)).astype(BF)
    for copy in copies:
        copy.wait_send()


def attn_sum(parts):
    shape = parts.shape[2:]
    dma = pltpu.SemaphoreType.DMA
    return pl.pallas_call(
        attn_sum_kernel,
        out_shape=jax.ShapeDtypeStruct(shape, BF),
        in_specs=[vmem_spec()],
        out_specs=vmem_spec(),
        scratch_shapes=[
            pltpu.VMEM((2, 2) + shape, BF),
            pltpu.VMEM((3,) + shape, BF),
            pltpu.VMEM((3,) + shape, BF),
            dma((4,)), dma((2, 2)), dma((3,)), dma((3,)),
        ],
        compiler_params=params(5),
        name="attn_sum",
    )(parts)


class Line:
    def __init__(self, mine, inbox, middle, out, sems):
        self.mine, self.inbox, self.middle, self.out = mine, inbox, middle, out
        self.in_s, self.in_r, self.mid_s, self.mid_r, self.x_s, self.x_r, self.o_s, self.o_r, self.l_s = sems
        place, row, col = lax.axis_index("dp"), lax.axis_index("row"), lax.axis_index("col")
        self.end = (place % 3) == 0
        inner = jnp.where(place == 0, 1, 2)
        self.inner = (inner, row, col)
        self.outer = ((place - 1) * 3 % 6, row, col)
        self.across = (3 - place, row, col)
        self.root = jnp.where(place == 1, 0, 1)
        self.place = place

    def inward(self, k, h):
        return remote(self.mine.at[k, h], self.inbox.at[k, h], self.in_s.at[k, h], self.in_r.at[k, h], self.inner)

    def partial(self, k):
        return remote(
            self.mine.at[k, 1 - self.root], self.middle.at[k], self.mid_s.at[k], self.mid_r.at[k], self.across
        )

    def exchange(self, k):
        return remote(
            self.mine.at[k, self.root], self.out.at[k, self.root], self.x_s.at[k], self.x_r.at[k], self.across
        )

    def exchanged(self, k):
        return remote(
            self.mine.at[k, 1 - self.root], self.out.at[k, 1 - self.root], self.x_s.at[k], self.x_r.at[k], self.across
        )

    def outward(self, k, h, source):
        return remote(source.at[k, h], self.out.at[k, h], self.o_s.at[k, h], self.o_r.at[k, h], self.outer)

    def keep(self, k):
        return pltpu.make_async_copy(self.mine.at[k, self.root], self.out.at[k, self.root], self.l_s.at[k])

    def send(self, k):
        @pl.when(self.end)
        def _():
            for h in range(2):
                self.inward(k, h).start()

    def add(self, k):
        @pl.when(jnp.logical_not(self.end))
        def _():
            other = 1 - self.root
            self.inward(k, other).wait_recv()
            self.mine[k, other] = (
                self.mine[k, other].astype(F32) + self.inbox[k, other].astype(F32)
            ).astype(BF)
            self.partial(k).start()

    def total(self, k):
        @pl.when(jnp.logical_not(self.end))
        def _():
            root = self.root
            self.inward(k, root).wait_recv()
            self.partial(k).wait_recv()
            self.mine[k, root] = (
                self.mine[k, root].astype(F32) + self.inbox[k, root].astype(F32) + self.middle[k].astype(F32)
            ).astype(BF)
            self.outward(k, root, self.mine).start()
            self.exchange(k).start()
            self.keep(k).start()

    def forward(self, k):
        @pl.when(jnp.logical_not(self.end))
        def _():
            other = 1 - self.root
            self.exchanged(k).wait_recv()
            self.outward(k, other, self.out).start()

    def drain(self, k):
        @pl.when(self.end)
        def _():
            for h in range(2):
                self.inward(k, h).wait_send()
                self.outward(k, h, self.out).wait_recv()

        @pl.when(jnp.logical_not(self.end))
        def _():
            self.partial(k).wait_send()
            self.exchange(k).wait_send()
            self.keep(k).wait()
            for h in range(2):
                self.outward(k, h, self.out).wait_send()

    def greet(self):
        barrier = pltpu.get_barrier_semaphore()

        @pl.when(self.end)
        def _():
            pl.semaphore_signal(barrier, inc=1, device_id=self.inner, device_id_type=MESH)
            pl.semaphore_wait(barrier, 1)

        @pl.when(jnp.logical_not(self.end))
        def _():
            pl.semaphore_signal(barrier, inc=1, device_id=self.outer, device_id_type=MESH)
            pl.semaphore_signal(barrier, inc=1, device_id=self.across, device_id_type=MESH)
            pl.semaphore_wait(barrier, 2)


def line_sems(count):
    dma = pltpu.SemaphoreType.DMA
    return [
        dma((count, 2)), dma((count, 2)), dma((count,)), dma((count,)), dma((count,)), dma((count,)),
        dma((count, 2)), dma((count, 2)), dma((count,)),
    ]


def line_kernel(g, a, g_out, a_out, g_mine, g_in, g_mid, a_mine, a_in, a_mid, load, *sems):
    big = Line(g_mine, g_in, g_mid, g_out, sems[:9])
    small = Line(a_mine, a_in, a_mid, a_out, sems[9:])
    count = g_mine.shape[0]
    fetch = [pltpu.make_async_copy(g, g_mine, load.at[0]), pltpu.make_async_copy(a, a_mine, load.at[1])]
    for copy in fetch:
        copy.start()
    big.greet()
    for copy in fetch:
        copy.wait()

    def send(k, carry):
        big.send(k)
        return carry

    lax.fori_loop(0, count, send, 0)
    small.send(0)
    big.add(0)
    big.add(1)
    big.total(0)

    def step(k, carry):
        big.add(k)
        big.total(k - 1)
        big.forward(k - 2)
        return carry

    lax.fori_loop(2, count, step, 0)
    small.add(0)
    big.total(count - 1)
    big.forward(count - 2)
    small.total(0)
    big.forward(count - 1)
    small.forward(0)

    def drain(k, carry):
        big.drain(k)
        return carry

    lax.fori_loop(0, count, drain, 0)
    small.drain(0)


def line_sum(g, a):
    count = g.shape[0]
    shape, small = g.shape[2:], a.shape[2:]
    dma = pltpu.SemaphoreType.DMA
    return pl.pallas_call(
        line_kernel,
        out_shape=(jax.ShapeDtypeStruct(g.shape, BF), jax.ShapeDtypeStruct(a.shape, BF)),
        in_specs=[any_spec()] * 2,
        out_specs=[any_spec()] * 2,
        scratch_shapes=[
            pltpu.VMEM(g.shape, BF), pltpu.VMEM(g.shape, BF), pltpu.VMEM((count,) + shape, BF),
            pltpu.VMEM(a.shape, BF), pltpu.VMEM(a.shape, BF), pltpu.VMEM((1,) + small, BF),
            dma((2,)),
        ] + line_sems(count) + line_sems(1),
        compiler_params=params(6),
        name="line_sum",
    )(g, a)


def swap(values, d_row, d_col):
    n_row, n_col = lax.axis_size("row"), lax.axis_size("col")
    pairs = [
        (i * n_col + j, (i ^ d_row) * n_col + (j ^ d_col))
        for i in range(n_row)
        for j in range(n_col)
    ]
    return lax.ppermute(values, ("row", "col"), pairs)


def all_sum(values):
    for d_row, d_col in ((1, 0), (0, 1), (2, 0)):
        values = values + swap(values, d_row, d_col)
    if lax.axis_size("dp") != 4:
        return lax.psum(values, "dp")
    for step in (1, 2):
        values = values + lax.ppermute(values, "dp", [(i, i ^ step) for i in range(4)])
    return values


def cut_low(values):
    return lax.reduce_precision(values, 8, 7)


def split3(values):
    high = cut_low(values)
    middle = cut_low(values - high)
    low = cut_low(values - high - middle)
    return jnp.stack([high, middle, low]).astype(BF)


def dp_sums(grads, attn):
    if lax.axis_size("dp") != 4:
        return lax.psum(grads.astype(F32), "dp"), lax.psum(attn.astype(F32), "dp")
    return line_sum(grads, attn)


def body(
    tokens,
    cotangent,
    weight_query,
    weight_key,
    weight_value,
    weight_out,
    weight_gate,
    weight_up,
    weight_down,
    gain_input,
    gain_attn,
    gain_pre,
    gain_post,
    gain_query,
    gain_key,
    doc_lengths,
    block_size,
):
    n_row, n_col = lax.axis_size("row"), lax.axis_size("col")
    members = n_row * n_col
    tok_count, cut = tokens.shape
    width = cut * members
    local = tok_count // members
    row, col = lax.axis_index("row"), lax.axis_index("col")
    high, core = row // 2, row % 2
    me = row * n_col + col
    depth = weight_query.shape[0]
    q_half = weight_query.shape[1]
    kv_half = weight_key.shape[1]
    qkv_half = q_half + 2 * kv_half
    head_count = n_col * q_half // HD
    hidden_half = weight_gate.shape[1]
    slab = -(-hidden_half // 512) * 256
    query_scale = 1.0 / math.sqrt(HD)

    gains = jnp.concatenate([split3(g) for g in (gain_input, gain_attn, gain_pre, gain_post)])
    gains = jnp.broadcast_to(jnp.pad(gains, ((0, 4), (0, 0)))[None], (members, 16, cut))
    token_blocks = jnp.concatenate([tokens.reshape(members, local, cut), gains], axis=1)
    attn_block = jnp.concatenate([weight_query, weight_key, weight_value, weight_out.T], axis=1)
    hidden_block = jnp.pad(
        jnp.stack([weight_gate, weight_up, weight_down.T]),
        ((0, 0), (0, 0), (0, 2 * slab - hidden_half)),
    )
    got_tokens, got_cotangent, w_attn, w_hidden = entry(
        token_blocks, cotangent.reshape(members, local, cut), attn_block, hidden_block
    )
    with_gains = got_tokens.transpose(1, 0, 2).reshape(-1, width)
    inputs = with_gains[:local].astype(F32)
    upstream_bf = got_cotangent.transpose(1, 0, 2).reshape(local, width)
    upstream = upstream_bf.astype(F32)
    gain_rows = with_gains[local : local + 12].astype(F32).reshape(4, 3, width).sum(axis=1)
    g_input, g_attn, g_pre, g_post = (gain_rows[i] for i in range(4))
    w_qkv = w_attn[:, :, :qkv_half]
    w_out = jnp.concatenate([w_attn[j, :, qkv_half:] for j in range(n_col)], axis=1)

    lengths = doc_lengths[0]
    span = block_size[0]
    slots = [
        ((row + 2 * (s // 4)) % 4 // 2 * 2 + (core + (s // 2) % 2) % 2) * n_col + (col + s) % 2
        for s in range(members)
    ]
    my_tokens = me * local + jnp.arange(local, dtype=jnp.int32)
    key_tokens = jnp.concatenate([s * local + jnp.arange(local, dtype=jnp.int32) for s in slots])
    my_document, my_places = positions(lengths, my_tokens)
    key_document, key_places = positions(lengths, key_tokens)
    allowed = (my_document[:, None] == key_document[None, :]) & (
        key_places[None, :] // span <= my_places[:, None] // span
    )
    cos_table, sin_table = angles(my_places)
    cos_heads, sin_heads = cos_table[:, None, :], sin_table[:, None, :]

    normed, inverse_in = norm(inputs, g_input)
    normed_bf = normed.astype(BF)
    projected = [nn(normed_bf, w_qkv[j]) for j in range(n_col)]
    query_pre = jnp.concatenate([p[:, :q_half] for p in projected], axis=1).reshape(
        local, head_count, HD
    )
    key_pre = jnp.concatenate([p[:, q_half : q_half + kv_half] for p in projected], axis=1)
    value_pre = jnp.concatenate([p[:, q_half + kv_half :] for p in projected], axis=1)
    query_bf = (head_norm(query_pre, gain_query, cos_heads, sin_heads) * query_scale).astype(BF)
    key_bf = head_norm(key_pre, gain_key, cos_table, sin_table).astype(BF)
    kv_all = kv_gather(jnp.concatenate([key_bf, value_pre.astype(BF)], axis=1))
    kv_all = kv_all.reshape(tok_count, 2 * HD)
    keys_bf, values_bf = kv_all[:, :HD], kv_all[:, HD:]

    def attention_scores():
        raw = jnp.einsum("thd,sd->hts", query_bf, keys_bf, preferred_element_type=F32)
        return jnp.where(allowed[None, :, :], raw, -1e30)

    scores = attention_scores()
    row_peak = jnp.max(scores, axis=-1, keepdims=True)
    exp_scores = jnp.exp(scores - row_peak)
    totals = jnp.sum(exp_scores, axis=-1, keepdims=True)
    log_total = row_peak + jnp.log(totals)
    probs_bf = (exp_scores / totals).astype(BF)
    head_out = jnp.einsum("hts,sd->thd", probs_bf, values_bf, preferred_element_type=F32)
    head_bf = head_out.astype(BF).reshape(local, head_count * HD)
    attn_out = nt(head_bf, w_out)
    attn_normed, inverse_attn = norm(attn_out, g_attn)
    residual = inputs + attn_normed
    pre_normed, inverse_pre = norm(residual, g_pre)

    layer_rows, grad_g_post, grad_pre, hidden_grads = mlp(
        pre_normed.astype(BF), residual, upstream_bf, g_post[None], w_hidden[0], w_hidden[1], w_hidden[2]
    )

    grad_resid, grad_g_pre = norm_back(residual, g_pre, inverse_pre, grad_pre)
    grad_resid = grad_resid + upstream
    grad_attn, grad_g_attn = norm_back(attn_out, g_attn, inverse_attn, grad_resid)
    grad_attn_bf = grad_attn.astype(BF)
    grad_w_out = tn(grad_attn_bf, head_bf)
    grad_head_bf = nn(grad_attn_bf, w_out).astype(BF).reshape(local, head_count, HD)

    scores = attention_scores()
    probs = jnp.exp(scores - log_total)
    probs_bf = probs.astype(BF)
    grad_probs = jnp.einsum("thd,sd->hts", grad_head_bf, values_bf, preferred_element_type=F32)
    grad_values = jnp.einsum("hts,thd->sd", probs_bf, grad_head_bf, preferred_element_type=F32)
    row_inner = jnp.sum(probs * grad_probs, axis=-1, keepdims=True)
    grad_scores = (probs * (grad_probs - row_inner)).astype(BF)
    grad_query = (
        jnp.einsum("hts,sd->thd", grad_scores, keys_bf, preferred_element_type=F32) * query_scale
    )
    grad_keys = jnp.einsum("hts,thd->sd", grad_scores, query_bf, preferred_element_type=F32)
    grad_kv = kv_sum(
        jnp.concatenate([grad_keys, grad_values], axis=1).astype(BF).reshape(members, local, 2 * HD)
    )
    grad_key, grad_value = grad_kv[:, :HD], grad_kv[:, HD:]

    unused, pull = jax.vjp(
        lambda rows_in, scales_in: head_norm(rows_in, scales_in, cos_heads, sin_heads),
        query_pre,
        gain_query,
    )
    grad_query_pre, grad_g_query = pull(grad_query)
    unused, pull = jax.vjp(
        lambda rows_in, scales_in: head_norm(rows_in, scales_in, cos_table, sin_table),
        key_pre,
        gain_key,
    )
    grad_key_pre, grad_g_key = pull(grad_key)
    grad_query_bf = grad_query_pre.astype(BF).reshape(local, head_count * HD)
    grad_key_bf = grad_key_pre.astype(BF)
    grad_value_bf = grad_value.astype(BF)
    grad_halves = [
        jnp.concatenate(
            [
                grad_query_bf[:, j * q_half : (j + 1) * q_half],
                grad_key_bf[:, j * kv_half : (j + 1) * kv_half],
                grad_value_bf[:, j * kv_half : (j + 1) * kv_half],
            ],
            axis=1,
        )
        for j in range(n_col)
    ]
    grad_normed = sum(nt(grad_halves[j], w_qkv[j]) for j in range(n_col))
    grad_in, grad_g_input = norm_back(inputs, g_input, inverse_in, grad_normed)

    out_half = grad_w_out.shape[1] // n_col
    attn_grads = jnp.stack(
        [
            jnp.concatenate(
                [tn(normed_bf, grad_halves[j]), grad_w_out[:, j * out_half : (j + 1) * out_half]], axis=1
            ).astype(BF)
            for j in range(n_col)
        ]
    ).reshape(n_col, n_row, depth, -1)
    attn_mine = attn_sum(attn_grads)
    feats = attn_mine.shape[1]
    attn_pair = jnp.stack([attn_mine[:, : feats // 2], attn_mine[:, feats // 2 :]])[None]
    tiles = hidden_grads.shape[1]
    hidden_sum, attn_pair = dp_sums(
        hidden_grads.reshape((3 * tiles, 2, depth, TILE)), attn_pair
    )
    attn_mine = jnp.concatenate([attn_pair[0, 0], attn_pair[0, 1]], axis=1).astype(F32)
    hidden_sum = hidden_sum.reshape(3, tiles, 2, depth, TILE)
    hidden_sum = jnp.where(high == 0, hidden_sum, hidden_sum[:, :, ::-1])
    hidden_sum = hidden_sum.transpose(0, 3, 2, 1, 4).reshape(3, depth, 2 * slab)
    hidden_sum = hidden_sum[:, :, :hidden_half].astype(F32)

    def from_tokens(values):
        cubes = values.astype(BF).reshape(local, members, cut).transpose(1, 0, 2)
        return lax.all_to_all(cubes, ("row", "col"), split_axis=0, concat_axis=0, tiled=True).reshape(
            tok_count, cut
        )

    grad_tokens = from_tokens(grad_in + grad_resid).astype(F32)
    layer_out = from_tokens(layer_rows)

    def my_gain(values):
        return lax.dynamic_slice_in_dim(values, me * cut, cut, 0)

    sums = all_sum(
        jnp.concatenate([grad_g_input, grad_g_attn, grad_g_pre, grad_g_post[0], grad_g_query, grad_g_key])
    )
    return (
        layer_out,
        grad_tokens,
        attn_mine[:, :q_half],
        attn_mine[:, q_half : q_half + kv_half],
        attn_mine[:, q_half + kv_half : qkv_half],
        attn_mine[:, qkv_half:].T,
        hidden_sum[0],
        hidden_sum[1],
        hidden_sum[2].T,
        my_gain(sums[:width]),
        my_gain(sums[width : 2 * width]),
        my_gain(sums[2 * width : 3 * width]),
        my_gain(sums[3 * width : 4 * width]),
        sums[4 * width : 4 * width + HD],
        sums[4 * width + HD :],
    )


def solution(mesh):
    in_specs = (
        P("dp", ("row", "col")),
        P("dp", ("row", "col")),
        P("row", "col"),
        P("row", "col"),
        P("row", "col"),
        P("col", "row"),
        P("row", "col"),
        P("row", "col"),
        P("col", "row"),
        P(("row", "col")),
        P(("row", "col")),
        P(("row", "col")),
        P(("row", "col")),
        P(),
        P(),
        P("dp", None),
        P(),
    )
    out_specs = (
        P("dp", ("row", "col")),
        P("dp", ("row", "col")),
        P("row", "col"),
        P("row", "col"),
        P("row", "col"),
        P("col", "row"),
        P("row", "col"),
        P("row", "col"),
        P("col", "row"),
        P(("row", "col")),
        P(("row", "col")),
        P(("row", "col")),
        P(("row", "col")),
        P(),
        P(),
    )
    return jax.shard_map(body, mesh=mesh, in_specs=in_specs, out_specs=out_specs, check_vma=False)
```

```python
import math

import jax
import jax.numpy as jnp
from jax import lax
from jax.experimental import pallas as pl
from jax.experimental.pallas import tpu as pltpu
from jax.sharding import PartitionSpec as P

HD = 256
EPS = 1e-06
ROPE_BASE = 1000000.0
GELU_C = 0.7978845608028654
BF = jnp.bfloat16
F32 = jnp.float32
PLANE = ("row", "col")


def dot(left, right, dims):
    return lax.dot_general(left, right, (dims, ((), ())), preferred_element_type=F32)


def nn(left, right):
    return dot(left, right, ((1,), (0,)))


def nt(left, right):
    return dot(left, right, ((1,), (1,)))


def tn(left, right):
    return dot(left, right, ((0,), (0,)))


def gelu_tanh(values):
    return 0.5 * values * (1.0 + jnp.tanh(GELU_C * (values + 0.044715 * values * values * values)))


def rotate(values, cos_table, sin_table):
    half_width = values.shape[-1] // 2
    first_half = values[..., :half_width]
    second_half = values[..., half_width:]
    return jnp.concatenate(
        [
            first_half * cos_table - second_half * sin_table,
            second_half * cos_table + first_half * sin_table,
        ],
        axis=-1,
    )


def head_norm(values, scales, cos_table, sin_table):
    mean_square = jnp.mean(values * values, axis=-1, keepdims=True)
    return rotate(values * lax.rsqrt(mean_square + EPS) * (1.0 + scales), cos_table, sin_table)


def positions(lengths, token_ids):
    doc_ends = jnp.cumsum(lengths, dtype=jnp.int32)
    doc_starts = doc_ends - lengths
    document = jnp.sum(
        (token_ids[:, None] >= doc_ends[None, :]).astype(jnp.int32), axis=1, dtype=jnp.int32
    )
    doc_ids = jnp.arange(lengths.shape[0], dtype=jnp.int32)
    doc_first = jnp.sum(
        jnp.where(doc_ids[None, :] == document[:, None], doc_starts[None, :], 0),
        axis=1,
        dtype=jnp.int32,
    )
    return (document, token_ids - doc_first)


def angles(places):
    half_width = HD // 2
    frequency = jnp.exp(
        jnp.arange(half_width, dtype=jnp.float32) * (-2.0 * math.log(ROPE_BASE) / HD)
    )
    phases = places.astype(jnp.float32)[:, None] * frequency[None, :]
    return (jnp.cos(phases), jnp.sin(phases))


def norm(values, scales):
    inverse = lax.rsqrt(jnp.mean(values * values, axis=1, keepdims=True) + EPS)
    return (values * inverse * (1.0 + scales), inverse)


def norm_back(values, scales, inverse, upstream):
    scaled = upstream * (1.0 + scales)
    inner = jnp.mean(scaled * values, axis=1, keepdims=True)
    grad_values = scaled * inverse - values * inverse * inverse * inverse * inner
    return (grad_values, jnp.sum(upstream * values * inverse, axis=0))


MESH = pl.DeviceIdType.MESH
TILE = 256
VMEM_LIMIT = 64 * 1024 * 1024 - 512 * 1024


def whereabouts():
    place, row, col = lax.axis_index("dp"), lax.axis_index("row"), lax.axis_index("col")
    return place, row, col, row // 2, row % 2


def peers():
    place, row, col, high, core = whereabouts()
    far = row + 2 - 4 * high
    return (
        (place, row, 1 - col),
        (place, far, col),
        (place, far, 1 - col),
        (place, row + 1 - 2 * core, col),
    )


def remote(src, dst, send, recv, device):
    return pltpu.make_async_remote_copy(
        src_ref=src, dst_ref=dst, send_sem=send, recv_sem=recv, device_id=device, device_id_type=MESH
    )


def greet(devices):
    barrier = pltpu.get_barrier_semaphore()
    for device in devices:
        pl.semaphore_signal(barrier, inc=1, device_id=device, device_id_type=MESH)
    pl.semaphore_wait(barrier, len(devices))


def any_spec():
    return pl.BlockSpec(memory_space=pl.ANY)


def vmem_spec():
    return pl.BlockSpec(memory_space=pltpu.VMEM)


def params(number):
    return pltpu.CompilerParams(
        collective_id=number, has_side_effects=True, vmem_limit_bytes=VMEM_LIMIT
    )


def entry_kernel(tk, ct, wa, wm, tk_out, ct_out, wa_out, wm_out, tk_s, tk_r, ct_s, ct_r, wa_s, wa_r, wm_s, wm_r, loc):
    place, row, col, high, core = whereabouts()
    depth = wa.shape[0]
    slab = wm_out.shape[2]
    me = 2 * row + col
    px, py, pd, pc = peers()
    others = []
    for step in range(1, 8):
        r2, c2 = (row + step // 2) % 4, (col + step) % 2
        others.append((2 * r2 + c2, (place, r2, c2)))
    greet([device for _, device in others])
    copies = []

    def start(copy):
        copy.start()
        copies.append(copy)
        return copy

    for i, (index, device) in enumerate(others):
        start(remote(tk.at[index], tk_out.at[me], tk_s.at[i], tk_r.at[i], device))
    local = [
        pltpu.make_async_copy(tk.at[me], tk_out.at[me], loc.at[0]),
        pltpu.make_async_copy(ct.at[me], ct_out.at[me], loc.at[1]),
        pltpu.make_async_copy(wa, wa_out.at[col, pl.ds(row * depth, depth)], loc.at[2]),
        pltpu.make_async_copy(
            wm.at[:, :, pl.ds(high * slab, slab)], wm_out.at[:, pl.ds(row * depth, depth)], loc.at[3]
        ),
    ]
    for copy in local:
        copy.start()
    slot = wa_out.at[col, pl.ds(row * depth, depth)]
    first = [start(remote(wa, slot, wa_s.at[i], wa_r.at[i], p)) for i, p in enumerate((px, py, pd, pc))]
    mine = pl.ds(high * slab, slab)
    away = pl.ds((1 - high) * slab, slab)
    rows = pl.ds(row * depth, depth)
    far_row = row + 2 - 4 * high
    far_rows = pl.ds(far_row * depth, depth)
    over = []
    for m in range(3):
        over.append(start(remote(wm.at[m, :, away], wm_out.at[m, rows], wm_s.at[m, 0], wm_r.at[m, 0], py)))
        start(remote(wm.at[m, :, mine], wm_out.at[m, rows], wm_s.at[m, 1], wm_r.at[m, 1], pc))
    for i, (index, device) in enumerate(others):
        start(remote(ct.at[index], ct_out.at[me], ct_s.at[i], ct_r.at[i], device))
    relay = []
    for i, (r2, c2) in enumerate(((row, 1 - col), (far_row, col), (far_row, 1 - col))):
        first[i].wait_recv()
        part = wa_out.at[c2, pl.ds(r2 * depth, depth)]
        relay.append(remote(part, part, wa_s.at[4 + i], wa_r.at[4 + i], pc))
        relay[-1].start()
    for m in range(3):
        over[m].wait_recv()
        part = wm_out.at[m, far_rows]
        relay.append(remote(part, part, wm_s.at[m, 2], wm_r.at[m, 2], pc))
        relay[-1].start()
    waited = first[:3] + over
    for copy in copies:
        copy.wait_send()
        if not any(copy is other for other in waited):
            copy.wait_recv()
    for copy in relay:
        copy.wait()
    for copy in local:
        copy.wait()


def entry(tk, ct, wa, wm):
    depth, feats = wa.shape
    slab = wm.shape[2] // 2
    dma = pltpu.SemaphoreType.DMA
    return pl.pallas_call(
        entry_kernel,
        out_shape=(
            jax.ShapeDtypeStruct(tk.shape, BF),
            jax.ShapeDtypeStruct(ct.shape, BF),
            jax.ShapeDtypeStruct((2, 4 * depth, feats), BF),
            jax.ShapeDtypeStruct((3, 4 * depth, slab), BF),
        ),
        in_specs=[any_spec()] * 4,
        out_specs=[any_spec()] * 4,
        scratch_shapes=[
            dma((7,)), dma((7,)), dma((7,)), dma((7,)), dma((7,)), dma((7,)),
            dma((3, 3)), dma((3, 3)), dma((4,)),
        ],
        compiler_params=params(1),
        name="entry",
    )(tk, ct, wa, wm)


KV_SLOTS = (0, 1, 4, 5)


def kv_kernel(kv, out, send, recv, loc):
    px, py, pd, pc = peers()
    greet((px, py, pd, pc))
    own = pltpu.make_async_copy(kv, out.at[0], loc)
    own.start()
    first = [
        remote(kv, out.at[slot], send.at[i], recv.at[i], device)
        for i, (slot, device) in enumerate(((1, px), (4, py), (5, pd), (2, pc)))
    ]
    for copy in first:
        copy.start()
    relay = []
    for i, slot in enumerate((1, 4, 5)):
        first[i].wait_recv()
        copy = remote(out.at[slot], out.at[slot + 2], send.at[4 + i], recv.at[4 + i], pc)
        copy.start()
        relay.append(copy)
    for copy in first:
        copy.wait_send()
    first[3].wait_recv()
    for copy in relay:
        copy.wait()
    own.wait()


def kv_gather(kv):
    dma = pltpu.SemaphoreType.DMA
    return pl.pallas_call(
        kv_kernel,
        out_shape=jax.ShapeDtypeStruct((8,) + kv.shape, BF),
        in_specs=[any_spec()],
        out_specs=any_spec(),
        scratch_shapes=[dma((7,)), dma((7,)), dma(())],
        compiler_params=params(2),
        name="kv_gather",
    )(kv)


def mlp_kernel(
    pre, res, ct, gpost, wg_h, wu_h, wd_h,
    lo, dgpost, dpre, grads,
    wg, wu, wd, pre_all, pre_t, gm_all, gm_t, aa, bb, hh, acc, own, parts, prc, prc2, dwb, crecv,
    w_sem, ag_s, ag_r, rs_s, rs_r, gs_s, gs_r, bs_s, bs_r, c_s, c_r, l_s,
):
    place, row, col, high, core = whereabouts()
    px, py, pd, pc = peers()
    quad = (px, py, pd)
    loc, width = pre.shape
    slab = wg.shape[1]
    tiles = slab // TILE
    depth = crecv.shape[3]
    loads = [
        pltpu.make_async_copy(src, dst, w_sem.at[i])
        for i, (src, dst) in enumerate(((wg_h, wg), (wu_h, wu), (wd_h, wd)))
    ]
    for copy in loads:
        copy.start()
    greet((px, py, pd, pc))

    def spread(src, buffer, send, recv):
        copies = [remote(src, buffer.at[i + 1], send.at[i], recv.at[i], p) for i, p in enumerate(quad)]
        for copy in copies:
            copy.start()
        return copies

    def lanes(n):
        return pl.ds(pl.multiple_of(n * TILE, TILE), TILE)

    gathers = spread(pre, pre_all, ag_s, ag_r)
    pre_all[0] = pre[...]
    for copy in loads:
        copy.wait()

    scatters = []
    for j in range(4):
        if j:
            gathers[j - 1].wait_recv()
        acc[...] = jnp.zeros_like(acc)
        rows = pl.ds(j * loc, loc)

        def forward(n, carry, j=j, rows=rows):
            x = pre_all[j]
            gate = nn(x, wg[:, lanes(n)])
            up = nn(x, wu[:, lanes(n)])
            square = gate * gate
            bend = jnp.tanh(GELU_C * gate * (1.0 + 0.044715 * square))
            half = 0.5 * (1.0 + bend)
            gelu = gate * half
            slope = half + 0.5 * gate * (1.0 - bend * bend) * (GELU_C * (1.0 + 0.134145 * square))
            hidden = (gelu * up).astype(BF)
            aa[rows, lanes(n)] = gelu.astype(BF)
            bb[rows, lanes(n)] = (up * slope).astype(BF)
            hh[rows, lanes(n)] = hidden
            acc[...] += nt(hidden, wd[:, lanes(n)])
            return carry

        lax.fori_loop(0, tiles, forward, 0)
        if j:
            parts[j - 1] = acc[...].astype(BF)
            copy = remote(parts.at[j - 1], prc.at[j - 1], rs_s.at[j - 1], rs_r.at[j - 1], quad[j - 1])
            copy.start()
            scatters.append(copy)
        else:
            own[...] = acc[...]
    for j in range(4):
        pre_t[:, j * loc : (j + 1) * loc] = pre_all[j].T
    for copy in scatters:
        copy.wait()
    out = own[...] + prc[0].astype(F32) + prc[1].astype(F32) + prc[2].astype(F32)
    scale = 1.0 + gpost[...]
    inverse = lax.rsqrt(jnp.mean(out * out, axis=1, keepdims=True) + EPS)
    lo[...] = (res[...] + out * inverse * scale).astype(BF)
    upstream = ct[...].astype(F32)
    scaled = upstream * scale
    inner = jnp.mean(scaled * out, axis=1, keepdims=True)
    gm_all[0] = (scaled * inverse - out * (inverse * inverse * inverse * inner)).astype(BF)
    dgpost[...] = jnp.sum(upstream * out * inverse, axis=0, keepdims=True)

    gathers2 = spread(gm_all.at[0], gm_all, gs_s, gs_r)
    scatters2 = []
    for j in range(4):
        if j:
            gathers2[j - 1].wait_recv()
        acc[...] = jnp.zeros_like(acc)
        rows = pl.ds(j * loc, loc)

        def backward(n, carry, j=j, rows=rows):
            grad_hidden = nn(gm_all[j], wd[:, lanes(n)])
            grad_gate = (grad_hidden * bb[rows, lanes(n)].astype(F32)).astype(BF)
            grad_up = (grad_hidden * aa[rows, lanes(n)].astype(F32)).astype(BF)
            bb[rows, lanes(n)] = grad_gate
            aa[rows, lanes(n)] = grad_up
            acc[...] += nt(grad_gate, wg[:, lanes(n)]) + nt(grad_up, wu[:, lanes(n)])
            return carry

        lax.fori_loop(0, tiles, backward, 0)
        gm_t[:, j * loc : (j + 1) * loc] = gm_all[j].T
        if j:
            parts[j - 1] = acc[...].astype(BF)
            copy = remote(parts.at[j - 1], prc2.at[j - 1], bs_s.at[j - 1], bs_r.at[j - 1], quad[j - 1])
            copy.start()
            scatters2.append(copy)
        else:
            own[...] = acc[...]

    def to_core(n, m, y2):
        return remote(
            dwb.at[n % 2, m, 2 * y2 + 1 - core], crecv.at[m, n, y2], c_s.at[n % 2, m, y2], c_r.at[m, n, y2], pc
        )

    def to_out(n, m, y2):
        slot = (high + y2) % 2
        return pltpu.make_async_copy(crecv.at[m, n, y2], grads.at[m, n, slot], l_s.at[m, n, y2])

    def produce(n):
        for m, (left, right) in enumerate(((pre_t, bb), (pre_t, aa), (gm_t, hh))):
            product = nn(left[...], right[:, lanes(n)]).astype(BF)
            dwb[n % 2, m] = product.reshape(4, depth, TILE)
            for y2 in range(2):
                to_core(n, m, y2).start()

    def settle(n):
        for m in range(3):
            for y2 in range(2):
                to_core(n, m, y2).wait()
                crecv[m, n, y2] = (
                    crecv[m, n, y2].astype(F32) + dwb[n % 2, m, 2 * y2 + core].astype(F32)
                ).astype(BF)
            for y2 in range(2):
                to_out(n, m, y2).start()

    produce(0)

    def step(n, carry):
        produce(n)
        settle(n - 1)
        return carry

    lax.fori_loop(1, tiles, step, 0)
    settle(tiles - 1)
    for copy in scatters2:
        copy.wait()
    dpre[...] = own[...] + prc2[0].astype(F32) + prc2[1].astype(F32) + prc2[2].astype(F32)

    def finish(n, carry):
        for m in range(3):
            for y2 in range(2):
                to_out(n, m, y2).wait()
        return carry

    lax.fori_loop(0, tiles, finish, 0)
    for copy in gathers + gathers2:
        copy.wait_send()


def mlp(pre, res, ct, gpost, w_gate, w_up, w_down):
    loc, width = pre.shape
    slab = w_gate.shape[1]
    tiles = slab // TILE
    depth = width // 4
    dma = pltpu.SemaphoreType.DMA
    return pl.pallas_call(
        mlp_kernel,
        out_shape=(
            jax.ShapeDtypeStruct((loc, width), BF),
            jax.ShapeDtypeStruct((1, width), F32),
            jax.ShapeDtypeStruct((loc, width), F32),
            jax.ShapeDtypeStruct((3, tiles, 2, depth, TILE), BF),
        ),
        in_specs=[vmem_spec()] * 4 + [any_spec()] * 3,
        out_specs=[vmem_spec()] * 3 + [any_spec()],
        scratch_shapes=[
            pltpu.VMEM((width, slab), BF),
            pltpu.VMEM((width, slab), BF),
            pltpu.VMEM((width, slab), BF),
            pltpu.VMEM((4, loc, width), BF),
            pltpu.VMEM((width, 4 * loc), BF),
            pltpu.VMEM((4, loc, width), BF),
            pltpu.VMEM((width, 4 * loc), BF),
            pltpu.VMEM((4 * loc, slab), BF),
            pltpu.VMEM((4 * loc, slab), BF),
            pltpu.VMEM((4 * loc, slab), BF),
            pltpu.VMEM((loc, width), F32),
            pltpu.VMEM((loc, width), F32),
            pltpu.VMEM((3, loc, width), BF),
            pltpu.VMEM((3, loc, width), BF),
            pltpu.VMEM((3, loc, width), BF),
            pltpu.VMEM((2, 3, 4, depth, TILE), BF),
            pltpu.VMEM((3, tiles, 2, depth, TILE), BF),
            dma((3,)),
            dma((3,)), dma((3,)), dma((3,)), dma((3,)), dma((3,)), dma((3,)), dma((3,)), dma((3,)),
            dma((2, 3, 2)), dma((3, tiles, 2)), dma((3, tiles, 2)),
        ],
        compiler_params=params(3),
        name="feed_forward",
    )(pre, res, ct, gpost, w_gate, w_up, w_down)


class Line:
    def __init__(self, mine, inbox, middle, out, sems):
        self.mine, self.inbox, self.middle, self.out = mine, inbox, middle, out
        self.in_s, self.in_r, self.mid_s, self.mid_r, self.x_s, self.x_r, self.o_s, self.o_r, self.l_s = sems
        place, row, col = lax.axis_index("dp"), lax.axis_index("row"), lax.axis_index("col")
        self.end = (place % 3) == 0
        inner = jnp.where(place == 0, 1, 2)
        self.inner = (inner, row, col)
        self.outer = ((place - 1) * 3 % 6, row, col)
        self.across = (3 - place, row, col)
        self.root = jnp.where(place == 1, 0, 1)
        self.place = place

    def inward(self, k, h):
        return remote(self.mine.at[k, h], self.inbox.at[k, h], self.in_s.at[k, h], self.in_r.at[k, h], self.inner)

    def partial(self, k):
        return remote(
            self.mine.at[k, 1 - self.root], self.middle.at[k], self.mid_s.at[k], self.mid_r.at[k], self.across
        )

    def exchange(self, k):
        return remote(
            self.mine.at[k, self.root], self.out.at[k, self.root], self.x_s.at[k], self.x_r.at[k], self.across
        )

    def exchanged(self, k):
        return remote(
            self.mine.at[k, 1 - self.root], self.out.at[k, 1 - self.root], self.x_s.at[k], self.x_r.at[k], self.across
        )

    def outward(self, k, h, source):
        return remote(source.at[k, h], self.out.at[k, h], self.o_s.at[k, h], self.o_r.at[k, h], self.outer)

    def keep(self, k):
        return pltpu.make_async_copy(self.mine.at[k, self.root], self.out.at[k, self.root], self.l_s.at[k])

    def send(self, k):
        @pl.when(self.end)
        def _():
            for h in range(2):
                self.inward(k, h).start()

    def add(self, k):
        @pl.when(jnp.logical_not(self.end))
        def _():
            other = 1 - self.root
            self.inward(k, other).wait_recv()
            self.mine[k, other] = (
                self.mine[k, other].astype(F32) + self.inbox[k, other].astype(F32)
            ).astype(BF)
            self.partial(k).start()

    def total(self, k):
        @pl.when(jnp.logical_not(self.end))
        def _():
            root = self.root
            self.inward(k, root).wait_recv()
            self.partial(k).wait_recv()
            self.mine[k, root] = (
                self.mine[k, root].astype(F32) + self.inbox[k, root].astype(F32) + self.middle[k].astype(F32)
            ).astype(BF)
            self.outward(k, root, self.mine).start()
            self.exchange(k).start()
            self.keep(k).start()

    def forward(self, k):
        @pl.when(jnp.logical_not(self.end))
        def _():
            other = 1 - self.root
            self.exchanged(k).wait_recv()
            self.outward(k, other, self.out).start()

    def drain(self, k):
        @pl.when(self.end)
        def _():
            for h in range(2):
                self.inward(k, h).wait_send()
                self.outward(k, h, self.out).wait_recv()

        @pl.when(jnp.logical_not(self.end))
        def _():
            self.partial(k).wait_send()
            self.exchange(k).wait_send()
            self.keep(k).wait()
            for h in range(2):
                self.outward(k, h, self.out).wait_send()


class Alone:
    def __init__(self, mine, inbox, middle, out, sems):
        self.mine, self.out, self.sems = mine, out, sems[0]

    def send(self, k):
        pass

    def add(self, k):
        pass

    def forward(self, k):
        pass

    def copy(self, k, h):
        return pltpu.make_async_copy(self.mine.at[k, h], self.out.at[k, h], self.sems.at[k, h])

    def total(self, k):
        for h in range(2):
            self.copy(k, h).start()

    def drain(self, k):
        for h in range(2):
            self.copy(k, h).wait()


def line_sems(count):
    dma = pltpu.SemaphoreType.DMA
    return [
        dma((count, 2)), dma((count, 2)), dma((count,)), dma((count,)), dma((count,)), dma((count,)),
        dma((count, 2)), dma((count, 2)), dma((count,)),
    ]


def mask_bias(lengths, span, bias, me, slots):
    local = bias.shape[1]
    inverse = 1.0 / jnp.full((1, 1), span[0], jnp.int32).astype(F32)

    def place(tokens):
        document = jnp.zeros_like(tokens)
        first = jnp.zeros_like(tokens)
        end = jnp.int32(0)
        for i in range(lengths.shape[1]):
            end = end + lengths[0, i]
            past = tokens >= end
            document = jnp.where(past, i + 1, document)
            first = jnp.where(past, end, first)
        return document, jnp.floor(((tokens - first).astype(F32) + 0.5) * inverse)

    query_doc, query_block = place(me * local + lax.broadcasted_iota(jnp.int32, (1, local), 1))
    for s, owner in enumerate(slots):
        key_doc, key_block = place(owner * local + lax.broadcasted_iota(jnp.int32, (local, 1), 0))
        seen = (key_doc == query_doc) & (key_block <= query_block)
        bias[s * local : (s + 1) * local, :] = jnp.where(seen, 0.0, -1e30)


def slot_owners():
    place, row, col, high, core = whereabouts()
    owners = []
    for s in range(8):
        r2 = (high + s // 4) % 2 * 2 + (core + s // 2) % 2
        owners.append(2 * r2 + (col + s) % 2)
    return owners


def sent_to_all(index):
    place, row, col, high, core = whereabouts()
    others = []
    for s in range(1, 8):
        r2, c2 = (high + s // 4) % 2 * 2 + (core + s // 2) % 2, (col + s) % 2
        others.append((2 * r2 + c2, (place, r2, c2)))
    return others


def back_kernel(
    grads, lo, dpre, res, ao, ct, x, gains, gq, gk, heads, q_pre, k_pre, q_bf, kv, lse, cos, sin, wa, dgpost, lengths, span,
    g_out, a_out, lo_out, gt_out, gain_out,
    mine, inbox, middle, a_mine, a_in, a_mid,
    bias, k_t, ga, gh, dk, dv, stage, kv_cr, kv_sum_, kv_qr, dh, g_res, parts, cr, summed, qr, lo_cut, gt_cut, gain_buf, gain_in,
    f_s, y_s, y_r, kc_s, kc_r, kq_s, kq_r, pc_s, pc_r, pq_s, pq_r, lo_s, lo_r, gt_s, gt_r, gn_s, gn_r, loc_s, *line_refs,
):
    place, row, col, high, core = whereabouts()
    me = 2 * row + col
    px, py, pd, pc = peers()
    quad = (px, py, pd)
    others = sent_to_all(me)
    on_line = lax.axis_size("dp") == 4
    make = Line if on_line else Alone
    line = make(mine, inbox, middle, g_out, line_refs[:9])
    small = make(a_mine, a_in, a_mid, a_out, line_refs[9:])
    hidden_pairs = grads.shape[0]
    pairs = mine.shape[0]
    loc, width = x.shape
    depth = mine.shape[2]
    cut = width // 8
    head_count = q_pre.shape[1] // HD
    half = HD // 2

    gain_peers = [pc, px, py]
    friends = [device for _, device in others]
    if on_line:
        gain_peers += [(place + 1 - 2 * (place % 2), row, col), ((place + 2) % 4, row, col)]
        friends += [((place + i) % 4, row, col) for i in range(1, 4)]
    greet(friends)

    def fetch(k):
        return pltpu.make_async_copy(grads.at[k, 0], mine.at[k, 0], f_s.at[k])

    def pull(k):
        return remote(grads.at[k, 1], mine.at[k, 1], y_s.at[k], y_r.at[k], py)

    def begin(k, carry):
        fetch(k).start()
        pull(k).start()
        return carry

    lax.fori_loop(0, hidden_pairs, begin, 0)

    def ready(k):
        fetch(k).wait()
        pull(k).wait_recv()
        line.send(k)

    def line_step(k):
        for j in (2 * k + 1, 2 * k + 2):
            if isinstance(k, int):
                if j < hidden_pairs:
                    ready(j)
        line.add(k)
        if not isinstance(k, int) or k >= 1:
            line.total(k - 1)
        if not isinstance(k, int) or k >= 2:
            line.forward(k - 2)

    for f in range(8):
        lo_cut[f] = lo[:, f * cut : (f + 1) * cut]
    lo_copies = [remote(lo_cut.at[i], lo_out.at[me], lo_s.at[j], lo_r.at[j], d) for j, (i, d) in enumerate(others)]
    for copy in lo_copies:
        copy.start()
    lo_own = pltpu.make_async_copy(lo_cut.at[me], lo_out.at[me], loc_s.at[0])
    lo_own.start()

    def norm_grad(values, scales, upstream):
        inverse = lax.rsqrt(jnp.mean(values * values, axis=1, keepdims=True) + EPS)
        scaled = upstream * (1.0 + scales)
        inner = jnp.mean(scaled * values, axis=1, keepdims=True)
        grad = scaled * inverse - values * (inverse * inverse * inverse * inner)
        return grad, jnp.sum(upstream * values * inverse, axis=0, keepdims=True)

    gain_buf[...] = jnp.zeros_like(gain_buf)
    grad, gain_buf[0, 2:3, :] = norm_grad(res[...], gains[2:3, :], dpre[...])
    g_res[...] = grad + ct[...].astype(F32)
    grad, gain_buf[0, 1:2, :] = norm_grad(ao[...], gains[1:2, :], g_res[...])
    ga[...] = grad.astype(BF)
    gain_buf[0, 3:4, :] = dgpost[...]
    feats = heads.shape[1] // 2
    qkv = wa.shape[2] - feats
    for j in range(2):
        gh[:, j * feats : (j + 1) * feats] = nn(ga[...], wa[j, :, qkv:]).astype(BF)
    ready(0)
    mask_bias(lengths, span, bias, me, slot_owners())
    k_t[...] = kv[:, :HD].T
    line_step(0)

    step_keys = 512
    for h in range(head_count):
        cols = slice(h * HD, (h + 1) * HD)
        query, grad_head = q_bf[:, cols], gh[:, cols]
        delta = jnp.sum(
            (grad_head.astype(F32) * heads[:, cols].astype(F32)).T, axis=0, keepdims=True
        )

        def keys(c, total, h=h, query=query, grad_head=grad_head, delta=delta):
            rows = pl.ds(pl.multiple_of(c * step_keys, step_keys), step_keys)
            scores = nt(kv[rows, :HD], query) + bias[rows, :]
            probs = jnp.exp(scores - lse[h : h + 1, :])
            grad_probs = nt(kv[rows, HD:], grad_head)
            grad_scores = (probs * (grad_probs - delta)).astype(BF)
            add_v = nn(probs.astype(BF), grad_head)
            add_k = nn(grad_scores, query)
            if h:
                dv[rows, :] += add_v
                dk[rows, :] += add_k
            else:
                dv[rows, :] = add_v
                dk[rows, :] = add_k
            return total + nn(k_t[:, rows], grad_scores)

        total = lax.fori_loop(0, kv.shape[0] // step_keys, keys, jnp.zeros((HD, loc), F32))
        grad_query = total.T * (1.0 / math.sqrt(HD))
        first, second = grad_query[:, :half], grad_query[:, half:]
        turned = jnp.concatenate(
            [first * cos[...] + second * sin[...], second * cos[...] - first * sin[...]], axis=1
        )
        grad, gain = norm_grad(q_pre[:, cols], gq[...], turned)
        gain_buf[0, 4:5, :HD] += gain
        dh[h // 2, :, (h % 2) * HD : (h % 2 + 1) * HD] = grad.astype(BF)
        line_step(h + 1)

    for i, slot in enumerate(KV_SLOTS):
        rows = slice((slot + 2) * loc, (slot + 3) * loc)
        stage[i, :, :HD] = dk[rows, :].astype(BF)
        stage[i, :, HD:] = dv[rows, :].astype(BF)
    kv_core = [remote(stage.at[i], kv_cr.at[i], kc_s.at[i], kc_r.at[i], pc) for i in range(4)]
    for copy in kv_core:
        copy.start()
    line_step(5)
    kv_sends = []
    for i, device in ((3, pd), (1, px), (2, py)):
        kv_core[i].wait_recv()
        rows = slice(KV_SLOTS[i] * loc, (KV_SLOTS[i] + 1) * loc)
        kv_sum_[i - 1, :, :HD] = (dk[rows, :] + kv_cr[i, :, :HD].astype(F32)).astype(BF)
        kv_sum_[i - 1, :, HD:] = (dv[rows, :] + kv_cr[i, :, HD:].astype(F32)).astype(BF)
        copy = remote(kv_sum_.at[i - 1], kv_qr.at[i - 1], kq_s.at[i - 1], kq_r.at[i - 1], device)
        copy.start()
        kv_sends.append(copy)
    kv_core[0].wait_recv()
    line_step(6)
    line_step(7)
    for copy in kv_sends:
        copy.wait()
    got = kv_qr[0].astype(F32) + kv_qr[1].astype(F32) + kv_qr[2].astype(F32) + kv_cr[0].astype(F32)
    grad_key = dk[:loc, :] + got[:, :HD]
    grad_value = dv[:loc, :] + got[:, HD:]
    first, second = grad_key[:, :half], grad_key[:, half:]
    turned = jnp.concatenate(
        [first * cos[...] + second * sin[...], second * cos[...] - first * sin[...]], axis=1
    )
    grad, gain_buf[0, 5:6, :HD] = norm_grad(k_pre[...], gk[...], turned)
    feat_q = dh.shape[2] - HD
    for j in range(2):
        dh[j, :, feat_q : feat_q + half] = grad[:, j * half : (j + 1) * half].astype(BF)
        dh[j, :, feat_q + half :] = grad_value[:, j * half : (j + 1) * half].astype(BF)

    inputs = x[...].astype(F32)
    inverse = lax.rsqrt(jnp.mean(inputs * inputs, axis=1, keepdims=True) + EPS)
    normed_t = (inputs * inverse * (1.0 + gains[0:1, :])).astype(BF).T
    ga_t = ga[...].T
    for j in range(2):
        for n in range(qkv // TILE):
            parts[j, :, :, n * TILE : (n + 1) * TILE] = (
                nn(normed_t, dh[j, :, n * TILE : (n + 1) * TILE]).astype(BF).reshape(4, depth, TILE)
            )
        for n in range(feats // TILE):
            parts[j, :, :, qkv + n * TILE : qkv + (n + 1) * TILE] = (
                nn(ga_t, heads[:, j * feats + n * TILE : j * feats + (n + 1) * TILE]).astype(BF).reshape(4, depth, TILE)
            )
    wanted = ((1 - col, 1 - high, pd), (1 - col, high, px), (col, 1 - high, py), (col, high, None))
    part_core = [
        remote(parts.at[c2, 2 * y2 + 1 - core], cr.at[c2, y2], pc_s.at[i], pc_r.at[c2, y2], pc)
        for i, (c2, y2, _) in enumerate(wanted)
    ]
    for copy in part_core:
        copy.start()
    grad_normed = nt(dh[0], wa[0, :, :qkv]) + nt(dh[1], wa[1, :, :qkv])
    grad, gain_buf[0, 0:1, :] = norm_grad(inputs, gains[0:1, :], grad_normed)
    grad = (grad + g_res[...]).astype(BF)
    for f in range(8):
        gt_cut[f] = grad[:, f * cut : (f + 1) * cut]
    gt_copies = [remote(gt_cut.at[i], gt_out.at[me], gt_s.at[j], gt_r.at[j], d) for j, (i, d) in enumerate(others)]
    for copy in gt_copies:
        copy.start()
    gt_own = pltpu.make_async_copy(gt_cut.at[me], gt_out.at[me], loc_s.at[1])
    gt_own.start()
    line_step(8)
    part_sends = []
    for i, (c2, y2, device) in enumerate(wanted):
        part_core[i].wait_recv()
        if device is None:
            break
        summed[i] = (parts[c2, 2 * y2 + core].astype(F32) + cr[c2, y2].astype(F32)).astype(BF)
        copy = remote(summed.at[i], qr.at[i], pq_s.at[i], pq_r.at[i], device)
        copy.start()
        part_sends.append(copy)
    for i in range(5):
        if i < len(gain_peers):
            copy = remote(gain_buf.at[i], gain_in.at[i], gn_s.at[i], gn_r.at[i], gain_peers[i])
            copy.start()
        line_step(9 + i)
        if i < len(gain_peers):
            copy.wait()
            gain_buf[i + 1] = gain_buf[i] + gain_in[i]
    gain_out[...] = gain_buf[len(gain_peers)]
    for copy in part_sends:
        copy.wait()
    total = (
        parts[col, 2 * high + core].astype(F32)
        + cr[col, high].astype(F32)
        + qr[0].astype(F32)
        + qr[1].astype(F32)
        + qr[2].astype(F32)
    ).astype(BF)
    whole = total.shape[1] // TILE // 2
    for i in range(2 * whole):
        mine[hidden_pairs + i // 2, i % 2] = total[:, i * TILE : (i + 1) * TILE]
    for i in range(2):
        a_mine[0, i] = total[i * depth // 2 : (i + 1) * depth // 2, 2 * whole * TILE :]
    for k in range(hidden_pairs, pairs):
        line.send(k)
    small.send(0)

    def step(k, carry):
        line_step(k)
        return carry

    lax.fori_loop(14, pairs, step, 0)
    small.add(0)
    line.total(pairs - 1)
    line.forward(pairs - 2)
    small.total(0)
    line.forward(pairs - 1)
    small.forward(0)

    def drain(k, carry):
        line.drain(k)
        return carry

    lax.fori_loop(0, pairs, drain, 0)
    small.drain(0)

    def pulled(k, carry):
        pull(k).wait_send()
        return carry

    lax.fori_loop(0, hidden_pairs, pulled, 0)
    for copy in lo_copies + gt_copies:
        copy.wait()
    lo_own.wait()
    gt_own.wait()
    for copy in kv_core + part_core:
        copy.wait_send()


def attention_back(*args):
    grads, lo, heads, q_pre, kv, wa = args[0], args[1], args[10], args[11], args[14], args[18]
    hidden_pairs, _, depth, _ = grads.shape
    loc, width = lo.shape
    feats = wa.shape[2]
    pairs = hidden_pairs + feats // TILE // 2
    keys = kv.shape[0]
    cut = width // 8
    dma = pltpu.SemaphoreType.DMA
    piece = (depth, TILE)
    rest = (depth // 2, feats - 2 * (feats // TILE // 2) * TILE)
    smem = pl.BlockSpec(memory_space=pltpu.SMEM)
    return pl.pallas_call(
        back_kernel,
        out_shape=(
            jax.ShapeDtypeStruct((pairs, 2) + piece, BF),
            jax.ShapeDtypeStruct((1, 2) + rest, BF),
            jax.ShapeDtypeStruct((8, loc, cut), BF),
            jax.ShapeDtypeStruct((8, loc, cut), BF),
            jax.ShapeDtypeStruct((8, width), F32),
        ),
        in_specs=[any_spec()] + [vmem_spec()] * (len(args) - 3) + [smem] * 2,
        out_specs=[any_spec()] * 4 + [vmem_spec()],
        scratch_shapes=[
            pltpu.VMEM((pairs, 2) + piece, BF),
            pltpu.VMEM((pairs, 2) + piece, BF),
            pltpu.VMEM((pairs,) + piece, BF),
            pltpu.VMEM((1, 2) + rest, BF),
            pltpu.VMEM((1, 2) + rest, BF),
            pltpu.VMEM((1,) + rest, BF),
            pltpu.VMEM((keys, loc), F32),
            pltpu.VMEM((HD, keys), BF),
            pltpu.VMEM((loc, width), BF),
            pltpu.VMEM(heads.shape, BF),
            pltpu.VMEM((keys, HD), F32),
            pltpu.VMEM((keys, HD), F32),
            pltpu.VMEM((4, loc, 2 * HD), BF),
            pltpu.VMEM((4, loc, 2 * HD), BF),
            pltpu.VMEM((3, loc, 2 * HD), BF),
            pltpu.VMEM((3, loc, 2 * HD), BF),
            pltpu.VMEM((2, loc, feats - heads.shape[1] // 2), BF),
            pltpu.VMEM((loc, width), F32),
            pltpu.VMEM((2, 4, depth, feats), BF),
            pltpu.VMEM((2, 2, depth, feats), BF),
            pltpu.VMEM((3, depth, feats), BF),
            pltpu.VMEM((3, depth, feats), BF),
            pltpu.VMEM((8, loc, cut), BF),
            pltpu.VMEM((8, loc, cut), BF),
            pltpu.VMEM((6, 8, width), F32),
            pltpu.VMEM((5, 8, width), F32),
            dma((hidden_pairs,)), dma((hidden_pairs,)), dma((hidden_pairs,)),
            dma((4,)), dma((4,)), dma((3,)), dma((3,)),
            dma((4,)), dma((2, 2)), dma((3,)), dma((3,)),
            dma((7,)), dma((7,)), dma((7,)), dma((7,)), dma((5,)), dma((5,)), dma((2,)),
        ] + line_sems(pairs) + line_sems(1),
        compiler_params=params(6),
        name="attention_back",
    )(*args)


def finish_kernel(high, pieces, gate, up, down):
    gate[...] = pieces[0, 0, 0].astype(F32)
    up[...] = pieces[1, 0, 0].astype(F32)
    down[...] = pieces[2, 0, 0].astype(F32).T


def finish(pieces, high, hidden):
    _, tiles, _, depth, _ = pieces.shape
    return pl.pallas_call(
        finish_kernel,
        grid_spec=pltpu.PrefetchScalarGridSpec(
            num_scalar_prefetch=1,
            grid=(-(-hidden // TILE),),
            in_specs=[
                pl.BlockSpec(
                    (3, 1, 1, depth, TILE), lambda i, high: (0, i % tiles, (i // tiles + high[0]) % 2, 0, 0)
                )
            ],
            out_specs=[
                pl.BlockSpec((depth, TILE), lambda i, high: (0, i)),
                pl.BlockSpec((depth, TILE), lambda i, high: (0, i)),
                pl.BlockSpec((TILE, depth), lambda i, high: (i, 0)),
            ],
        ),
        out_shape=(
            jax.ShapeDtypeStruct((depth, hidden), F32),
            jax.ShapeDtypeStruct((depth, hidden), F32),
            jax.ShapeDtypeStruct((hidden, depth), F32),
        ),
        name="finish",
    )(high, pieces)


def cut_low(values):
    return lax.reduce_precision(values, 8, 7)


def split3(values):
    high = cut_low(values)
    middle = cut_low(values - high)
    low = cut_low(values - high - middle)
    return jnp.stack([high, middle, low]).astype(BF)


def body(
    tokens,
    cotangent,
    weight_query,
    weight_key,
    weight_value,
    weight_out,
    weight_gate,
    weight_up,
    weight_down,
    gain_input,
    gain_attn,
    gain_pre,
    gain_post,
    gain_query,
    gain_key,
    doc_lengths,
    block_size,
):
    n_row, n_col = lax.axis_size("row"), lax.axis_size("col")
    members = n_row * n_col
    tok_count, cut = tokens.shape
    width = cut * members
    local = tok_count // members
    row, col = lax.axis_index("row"), lax.axis_index("col")
    high, core = row // 2, row % 2
    me = row * n_col + col
    depth = weight_query.shape[0]
    q_half = weight_query.shape[1]
    kv_half = weight_key.shape[1]
    qkv_half = q_half + 2 * kv_half
    head_count = n_col * q_half // HD
    hidden_half = weight_gate.shape[1]
    slab = -(-hidden_half // 512) * 256
    query_scale = 1.0 / math.sqrt(HD)

    gains = jnp.concatenate([split3(g) for g in (gain_input, gain_attn, gain_pre, gain_post)])
    gains = jnp.broadcast_to(jnp.pad(gains, ((0, 4), (0, 0)))[None], (members, 16, cut))
    token_blocks = jnp.concatenate([tokens.reshape(members, local, cut), gains], axis=1)
    attn_block = jnp.concatenate([weight_query, weight_key, weight_value, weight_out.T], axis=1)
    hidden_block = jnp.pad(
        jnp.stack([weight_gate, weight_up, weight_down.T]),
        ((0, 0), (0, 0), (0, 2 * slab - hidden_half)),
    )
    got_tokens, got_cotangent, w_attn, w_hidden = entry(
        token_blocks, cotangent.reshape(members, local, cut), attn_block, hidden_block
    )
    with_gains = got_tokens.transpose(1, 0, 2).reshape(-1, width)
    inputs = with_gains[:local].astype(F32)
    upstream_bf = got_cotangent.transpose(1, 0, 2).reshape(local, width)
    upstream = upstream_bf.astype(F32)
    gain_rows = with_gains[local : local + 12].astype(F32).reshape(4, 3, width).sum(axis=1)
    g_input, g_attn, g_pre, g_post = (gain_rows[i] for i in range(4))
    w_qkv = w_attn[:, :, :qkv_half]
    w_out = jnp.concatenate([w_attn[j, :, qkv_half:] for j in range(n_col)], axis=1)

    lengths = doc_lengths[0]
    span = block_size[0]
    slots = [
        ((row + 2 * (s // 4)) % 4 // 2 * 2 + (core + (s // 2) % 2) % 2) * n_col + (col + s) % 2
        for s in range(members)
    ]
    my_tokens = me * local + jnp.arange(local, dtype=jnp.int32)
    key_tokens = jnp.concatenate([s * local + jnp.arange(local, dtype=jnp.int32) for s in slots])
    my_document, my_places = positions(lengths, my_tokens)
    key_document, key_places = positions(lengths, key_tokens)
    allowed = (my_document[:, None] == key_document[None, :]) & (
        key_places[None, :] // span <= my_places[:, None] // span
    )
    cos_table, sin_table = angles(my_places)
    cos_heads, sin_heads = cos_table[:, None, :], sin_table[:, None, :]

    normed, inverse_in = norm(inputs, g_input)
    normed_bf = normed.astype(BF)
    projected = [nn(normed_bf, w_qkv[j]) for j in range(n_col)]
    query_pre = jnp.concatenate([p[:, :q_half] for p in projected], axis=1).reshape(
        local, head_count, HD
    )
    key_pre = jnp.concatenate([p[:, q_half : q_half + kv_half] for p in projected], axis=1)
    value_pre = jnp.concatenate([p[:, q_half + kv_half :] for p in projected], axis=1)
    query_bf = (head_norm(query_pre, gain_query, cos_heads, sin_heads) * query_scale).astype(BF)
    key_bf = head_norm(key_pre, gain_key, cos_table, sin_table).astype(BF)
    kv_all = kv_gather(jnp.concatenate([key_bf, value_pre.astype(BF)], axis=1))
    kv_all = kv_all.reshape(tok_count, 2 * HD)
    keys_bf, values_bf = kv_all[:, :HD], kv_all[:, HD:]

    def attention_scores():
        raw = jnp.einsum("thd,sd->hts", query_bf, keys_bf, preferred_element_type=F32)
        return jnp.where(allowed[None, :, :], raw, -1e30)

    scores = attention_scores()
    row_peak = jnp.max(scores, axis=-1, keepdims=True)
    exp_scores = jnp.exp(scores - row_peak)
    totals = jnp.sum(exp_scores, axis=-1, keepdims=True)
    log_total = row_peak + jnp.log(totals)
    probs_bf = (exp_scores / totals).astype(BF)
    head_out = jnp.einsum("hts,sd->thd", probs_bf, values_bf, preferred_element_type=F32)
    head_bf = head_out.astype(BF).reshape(local, head_count * HD)
    attn_out = nt(head_bf, w_out)
    attn_normed, inverse_attn = norm(attn_out, g_attn)
    residual = inputs + attn_normed
    pre_normed, inverse_pre = norm(residual, g_pre)

    layer_rows, grad_g_post, grad_pre, hidden_grads = mlp(
        pre_normed.astype(BF), residual, upstream_bf, g_post[None], w_hidden[0], w_hidden[1], w_hidden[2]
    )

    tiles = hidden_grads.shape[1]
    summed, attn_rest, layer_cut, token_cut, gain_sums = attention_back(
        hidden_grads.reshape(3 * tiles, 2, depth, TILE),
        layer_rows,
        grad_pre,
        residual,
        attn_out,
        upstream_bf,
        inputs.astype(BF),
        gain_rows,
        gain_query[None],
        gain_key[None],
        head_bf,
        query_pre.reshape(local, head_count * HD),
        key_pre,
        query_bf.reshape(local, head_count * HD),
        kv_all,
        log_total[:, :, 0],
        cos_table,
        sin_table,
        w_attn,
        grad_g_post,
        doc_lengths,
        block_size,
    )
    if lax.axis_size("dp") != 4:
        summed, attn_rest, gain_sums = (
            lax.psum(v.astype(F32), "dp") for v in (summed, attn_rest, gain_sums)
        )
    grad_gate, grad_up, grad_down = finish(
        summed[: 3 * tiles].reshape(3, tiles, 2, depth, TILE), high[None], hidden_half
    )
    attn_mine = jnp.concatenate(
        [summed[3 * tiles + i // 2, i % 2] for i in range(2 * (summed.shape[0] - 3 * tiles))]
        + [attn_rest[0].reshape(depth, -1)],
        axis=1,
    ).astype(F32)

    def my_gain(i):
        return lax.dynamic_slice_in_dim(gain_sums[i], me * cut, cut, 0)

    return (
        layer_cut.reshape(tok_count, cut),
        token_cut.reshape(tok_count, cut).astype(F32),
        attn_mine[:, :q_half],
        attn_mine[:, q_half : q_half + kv_half],
        attn_mine[:, q_half + kv_half : qkv_half],
        attn_mine[:, qkv_half:].T,
        grad_gate,
        grad_up,
        grad_down,
        my_gain(0),
        my_gain(1),
        my_gain(2),
        my_gain(3),
        gain_sums[4, :HD],
        gain_sums[5, :HD],
    )


def solution(mesh):
    in_specs = (
        P("dp", ("row", "col")),
        P("dp", ("row", "col")),
        P("row", "col"),
        P("row", "col"),
        P("row", "col"),
        P("col", "row"),
        P("row", "col"),
        P("row", "col"),
        P("col", "row"),
        P(("row", "col")),
        P(("row", "col")),
        P(("row", "col")),
        P(("row", "col")),
        P(),
        P(),
        P("dp", None),
        P(),
    )
    out_specs = (
        P("dp", ("row", "col")),
        P("dp", ("row", "col")),
        P("row", "col"),
        P("row", "col"),
        P("row", "col"),
        P("col", "row"),
        P("row", "col"),
        P("row", "col"),
        P("col", "row"),
        P(("row", "col")),
        P(("row", "col")),
        P(("row", "col")),
        P(("row", "col")),
        P(),
        P(),
    )
    return jax.shard_map(body, mesh=mesh, in_specs=in_specs, out_specs=out_specs, check_vma=False)
```

```python
import math

import jax
import jax.numpy as jnp
from jax import lax
from jax.experimental import pallas as pl
from jax.experimental.pallas import tpu as pltpu
from jax.sharding import PartitionSpec as P

HD = 256
EPS = 1e-06
ROPE_BASE = 1000000.0
GELU_C = 0.7978845608028654
BF = jnp.bfloat16
F32 = jnp.float32
PLANE = ("row", "col")


def dot(left, right, dims):
    return lax.dot_general(left, right, (dims, ((), ())), preferred_element_type=F32)


def nn(left, right):
    return dot(left, right, ((1,), (0,)))


def nt(left, right):
    return dot(left, right, ((1,), (1,)))


def tn(left, right):
    return dot(left, right, ((0,), (0,)))


MESH = pl.DeviceIdType.MESH
TILE = 256
KV_SLOTS = (0, 1, 4, 5)
LEAD = 4
VMEM_LIMIT = 64 * 1024 * 1024 - 512 * 1024


def whereabouts():
    place, row, col = lax.axis_index("dp"), lax.axis_index("row"), lax.axis_index("col")
    return place, row, col, row // 2, row % 2


def peers():
    place, row, col, high, core = whereabouts()
    far = row + 2 - 4 * high
    return (
        (place, row, 1 - col),
        (place, far, col),
        (place, far, 1 - col),
        (place, row + 1 - 2 * core, col),
    )


def remote(src, dst, send, recv, device):
    return pltpu.make_async_remote_copy(
        src_ref=src, dst_ref=dst, send_sem=send, recv_sem=recv, device_id=device, device_id_type=MESH
    )


def greet(devices):
    barrier = pltpu.get_barrier_semaphore()
    for device in devices:
        pl.semaphore_signal(barrier, inc=1, device_id=device, device_id_type=MESH)
    pl.semaphore_wait(barrier, len(devices))


def any_spec():
    return pl.BlockSpec(memory_space=pl.ANY)


def vmem_spec():
    return pl.BlockSpec(memory_space=pltpu.VMEM)


def params(number):
    return pltpu.CompilerParams(
        collective_id=number, has_side_effects=True, vmem_limit_bytes=VMEM_LIMIT
    )


def token_places(lengths, span, tokens):
    inverse = 1.0 / jnp.full((1, 1), span[0], jnp.int32).astype(F32)
    document = jnp.zeros_like(tokens)
    first = jnp.zeros_like(tokens)
    end = jnp.int32(0)
    for i in range(lengths.shape[1]):
        end = end + lengths[0, i]
        past = tokens >= end
        document = jnp.where(past, i + 1, document)
        first = jnp.where(past, end, first)
    position = (tokens - first).astype(F32)
    return document, jnp.floor((position + 0.5) * inverse), position


def mask_bias(lengths, span, bias, me, slots):
    local = bias.shape[1]
    query_doc, query_block, _ = token_places(
        lengths, span, me * local + lax.broadcasted_iota(jnp.int32, (1, local), 1)
    )
    for s, owner in enumerate(slots):
        key_doc, key_block, _ = token_places(
            lengths, span, owner * local + lax.broadcasted_iota(jnp.int32, (local, 1), 0)
        )
        seen = (key_doc == query_doc) & (key_block <= query_block)
        bias[s * local : (s + 1) * local, :] = jnp.where(seen, 0.0, -1e30).astype(BF)


def slot_owners():
    place, row, col, high, core = whereabouts()
    owners = []
    for s in range(8):
        r2 = (high + s // 4) % 2 * 2 + (core + s // 2) % 2
        owners.append(2 * r2 + (col + s) % 2)
    return owners


def sent_to_all(index):
    place, row, col, high, core = whereabouts()
    others = []
    for s in range(1, 8):
        r2, c2 = (high + s // 4) % 2 * 2 + (core + s // 2) % 2, (col + s) % 2
        others.append((2 * r2 + c2, (place, r2, c2)))
    return others


def head_forward(values, scales, cos, sin):
    half = values.shape[1] // 2
    inverse = lax.rsqrt(jnp.mean(values * values, axis=1, keepdims=True) + EPS)
    scaled = values * inverse * (1.0 + scales)
    first, second = scaled[:, :half], scaled[:, half:]
    return jnp.concatenate([first * cos - second * sin, second * cos + first * sin], axis=1)


def front_kernel(
    tok, ct, gain_block, wq, wk, wv, wo, wg, wu, wd, gq, gk, lengths, span,
    wm_out, wa_out, kv_out, bias_out, x_out, ct_out, gains, q_pre, k_pre, lse, cos, sin, heads, ao, res, pre,
    wm, wa, tok_all, ct_all, gain_all, q_out, kv, v_t, bias, probs,
    wm_l, wa_l, tk_s, tk_r, ct_s, ct_r, gn_s, gn_r, wa_s, wa_r, wb_s, wb_r, wy_s, wy_r, wu_s, wd_s, wz_r, wc_s, wc_r, wo_s, wo_r, kv_s, kv_r, loc_s,
):
    place, row, col, high, core = whereabouts()
    me = 2 * row + col
    px, py, pd, pc = peers()
    others = sent_to_all(me)
    depth, hidden = wg.shape
    slab = wm_out.shape[2]
    cut = tok.shape[0]
    loc = x_out.shape[0]
    head_count = heads.shape[1] // HD
    half = HD // 2
    members = len(others) + 1
    share = lax.axis_size("dp") == 4
    far_row = row + 2 - 4 * high
    friends = [device for _, device in others]
    if share:
        friends += [((place + i) % 4, row, col) for i in range(1, 4)]

    loads = [
        pltpu.make_async_copy(src, wm.at[m, :, pl.ds(0, hidden)], wm_l.at[m]) for m, src in enumerate((wg, wu, wd))
    ]
    rows = pl.ds(row * depth, depth)
    far_rows = pl.ds(far_row * depth, depth)
    spots, at = [], 0
    for src in (wq, wk, wv, wo):
        spots.append(pl.ds(at, src.shape[1]))
        at += src.shape[1]
    qkv = at - wo.shape[1]
    own = [
        pltpu.make_async_copy(src, wa.at[col, rows, spot], wa_l.at[i])
        for i, (src, spot) in enumerate(zip((wq, wk, wv, wo), spots))
    ]
    tok_own = pltpu.make_async_copy(
        tok.at[:, pl.ds(pl.multiple_of(me * loc, 128), loc)], tok_all.at[pl.ds(me * cut, cut)], loc_s.at[0]
    )
    ct_own = pltpu.make_async_copy(
        ct.at[:, pl.ds(pl.multiple_of(me * loc, 128), loc)], ct_all.at[pl.ds(me * cut, cut)], loc_s.at[1]
    )
    gain_own = pltpu.make_async_copy(gain_block, gain_all.at[me], loc_s.at[2])
    for copy in [tok_own, gain_own] + own + [ct_own] + loads:
        copy.start()
    greet(friends)

    def scatter(src, dst, send, recv):
        copies = [
            remote(
                src.at[:, pl.ds(pl.multiple_of(index * loc, 128), loc)],
                dst.at[pl.ds(me * cut, cut)],
                send.at[j],
                recv.at[j],
                device,
            )
            for j, (index, device) in enumerate(others)
        ]
        for copy in copies:
            copy.start()
        return copies

    tok_copies = scatter(tok, tok_all, tk_s, tk_r)
    gain_copies = [
        remote(gain_block, gain_all.at[me], gn_s.at[j], gn_r.at[j], device) for j, (_, device) in enumerate(others)
    ]
    for copy in gain_copies:
        copy.start()
    attn_copies = {}

    def hand_out(which):
        for i in ((0, 1, 2), (3,))[which]:
            for j, device in enumerate((px, py, pd, pc)):
                attn_copies[i, j] = remote(
                    (wq, wk, wv, wo)[i], wa.at[col, rows, spots[i]], wa_s.at[i, j], wa_r.at[i, j], device
                )
                attn_copies[i, j].start()

    hand_out(0)

    for copy in loads:
        copy.wait()
    for m in range(3):
        wm[m, :, hidden:] = jnp.zeros((depth, 2 * slab - hidden), BF)
    mine = pl.ds(pl.multiple_of(high * slab, 128), slab)
    away = pl.ds(pl.multiple_of((1 - high) * slab, 128), slab)
    unit = depth // 6
    groups, rounds = 18, 4

    def group(start, g):
        return g // 6, pl.ds(pl.multiple_of(start + g % 6 * unit, 16), unit)

    def over(g):
        m, at = group(0, g)
        return remote(wm.at[m, at, away], wm_out.at[group(row * depth, g)], wy_s.at[g], wy_r.at[g], py)

    def along(g, step):
        spot = wm_out.at[group(far_row * depth, g)]
        return remote(spot, spot, (wu_s if step > 0 else wd_s).at[g], wz_r.at[g], ((place + step) % 4, row, col))

    def between(g):
        spot = wm_out.at[group(far_row * depth, g)]
        return remote(spot, spot, wc_s.at[g], wc_r.at[g], pc)

    own_hidden = [pltpu.make_async_copy(wm.at[m, :, mine], wm_out.at[m, rows], wm_l.at[m]) for m in range(3)]
    beside = [remote(wm.at[m, :, mine], wm_out.at[m, rows], wo_s.at[m], wo_r.at[m], pc) for m in range(3)]
    extra = 16 + place % 2
    for m in range(3):
        own_hidden[m].start()
        beside[m].start()
    fetched = [rounds * r + place for r in range(rounds)] + [extra] if share else list(range(groups))
    for g in fetched:
        over(g).start()

    def travel(distance, act_up, act_down):
        for r in range(rounds):
            if distance == 0:
                g = rounds * r + place
                pl.when(place < 3)(lambda g=g: act_up(g))
                pl.when(place > 0)(lambda g=g: act_down(g))
            else:
                below, above = rounds * r + place - distance, rounds * r + place + distance
                pl.when(jnp.logical_and(place >= distance, place < 3))(lambda g=below: act_up(g))
                pl.when(jnp.logical_and(place + distance <= 3, place > 0))(lambda g=above: act_down(g))

    def arrive(distance):
        if not share:
            if distance == 0:
                for g in fetched:
                    over(g).wait_recv()
                    between(g).start()
            return
        if distance == 0:
            for g in fetched:
                over(g).wait_recv()
                between(g).start()
            step = 1 - 2 * (place % 2)
            pl.when(step > 0)(lambda: along(extra, 1).start())
            pl.when(step < 0)(lambda: along(extra, -1).start())
        else:
            for r in range(rounds):
                for g, there in (
                    (rounds * r + place - distance, place >= distance),
                    (rounds * r + place + distance, place + distance <= 3),
                ):

                    @pl.when(there)
                    def _(g=g):
                        along(g, 1).wait_recv()
                        between(g).start()

        travel(distance, lambda g: along(g, 1).start(), lambda g: along(g, -1).start())

    def arrived():
        if share:
            other = 33 - extra
            along(other, 1).wait_recv()
            between(other).start()
            pl.when(place % 2 == 0)(lambda: along(extra, 1).wait_send())
            pl.when(place % 2 == 1)(lambda: along(extra, -1).wait_send())
            for distance in range(4):
                travel(distance, lambda g: along(g, 1).wait_send(), lambda g: along(g, -1).wait_send())
        for g in fetched:
            over(g).wait_send()
        for g in range(groups):
            between(g).wait()
        for m in range(3):
            beside[m].wait()
            own_hidden[m].wait()

    doc, _, position = token_places(lengths, span, me * loc + lax.broadcasted_iota(jnp.int32, (loc, 1), 0))
    steps = lax.broadcasted_iota(jnp.int32, (1, half), 1).astype(F32)
    phases = position * jnp.exp(steps * (-2.0 * math.log(ROPE_BASE) / HD))
    cos[...] = jnp.cos(phases)
    sin[...] = jnp.sin(phases)
    mask_bias(lengths, span, bias, me, slot_owners())
    bias_copy = pltpu.make_async_copy(bias, bias_out, loc_s.at[3])
    bias_copy.start()

    tok_own.wait()
    gain_own.wait()
    for copy in tok_copies + gain_copies:
        copy.wait_recv()
    for f in range(members):
        gains[:, f * cut : (f + 1) * cut] = gain_all[f]
    x_out[...] = tok_all[...].T
    inputs = x_out[...].astype(F32)
    inverse = lax.rsqrt(jnp.mean(inputs * inputs, axis=1, keepdims=True) + EPS)
    normed = (inputs * inverse * (1.0 + gains[0:1, :])).astype(BF)

    corners = ((row, 1 - col), (far_row, col), (far_row, 1 - col))
    part_spots = (pl.ds(0, qkv), pl.ds(qkv, wo.shape[1]))
    passed = {}

    def pass_on(which):
        for j, (r2, c2) in enumerate(corners):
            for i in ((0, 1, 2), (3,))[which]:
                attn_copies[i, j].wait_recv()
            slot = wa.at[c2, pl.ds(r2 * depth, depth), part_spots[which]]
            passed[which, j] = remote(slot, slot, wb_s.at[which, j], wb_r.at[which, j], pc)
            passed[which, j].start()

    def settled(which):
        for i in ((0, 1, 2), (3,))[which]:
            own[i].wait()
            attn_copies[i, 3].wait_recv()
        for j in range(3):
            passed[which, j].wait_recv()

    pass_on(0)
    settled(0)
    q_half, kv_half = wq.shape[1], wk.shape[1]
    for j in range(2):
        found = nn(normed, wa[j, :, :qkv])
        q_pre[:, j * q_half : (j + 1) * q_half] = found[:, :q_half]
        k_pre[:, j * kv_half : (j + 1) * kv_half] = found[:, q_half : q_half + kv_half]
        kv[:loc, HD + j * kv_half : HD + (j + 1) * kv_half] = found[:, q_half + kv_half :].astype(BF)
    kv[:loc, :HD] = head_forward(k_pre[...], gk[...], cos[...], sin[...]).astype(BF)
    kv_first = [
        remote(kv.at[pl.ds(0, loc)], kv.at[pl.ds(slot * loc, loc)], kv_s.at[i], kv_r.at[i], device)
        for i, (slot, device) in enumerate(((1, px), (4, py), (5, pd), (2, pc)))
    ]
    for copy in kv_first:
        copy.start()
    hand_out(1)
    ct_copies = scatter(ct, ct_all, ct_s, ct_r)
    for h in range(head_count):
        cols = slice(h * HD, (h + 1) * HD)
        q_out[:, cols] = (head_forward(q_pre[:, cols], gq[...], cos[...], sin[...]) * (1.0 / math.sqrt(HD))).astype(BF)
    lse[...] = jnp.zeros_like(lse)
    arrive(0)

    def slot_scores(slot):
        keys = slice(slot * loc, (slot + 1) * loc)
        v_t[:, keys] = kv[keys, HD:].T
        for h in range(head_count):
            grown = jnp.exp(nt(kv[keys, :HD], q_out[:, h * HD : (h + 1) * HD]) + bias[keys, :].astype(F32))
            probs[h, keys, :] = grown
            lse[h : h + 1, :] += jnp.sum(grown, axis=0, keepdims=True)

    slot_scores(0)
    kv_relay = []
    for i, slot in enumerate((1, 4, 5)):
        kv_first[i].wait_recv()
        keys = pl.ds(slot * loc, loc)
        copy = remote(kv.at[keys], kv.at[pl.ds((slot + 2) * loc, loc)], kv_s.at[4 + i], kv_r.at[4 + i], pc)
        copy.start()
        kv_relay.append(copy)
        slot_scores(slot)
        if i == 0:
            kv_first[3].wait_recv()
            slot_scores(2)
    arrive(1)
    for i, slot in enumerate((3, 6, 7)):
        kv_relay[i].wait_recv()
        slot_scores(slot)
    kv_copy = pltpu.make_async_copy(kv, kv_out, loc_s.at[4])
    kv_copy.start()
    arrive(2)
    pass_on(1)
    for h in range(head_count):
        inverse = 1.0 / lse[h : h + 1, :]
        total = nn(v_t[...], (probs[h] * inverse).astype(BF))
        heads[:, h * HD : (h + 1) * HD] = total.T.astype(BF)
    lse[...] = jnp.log(lse[...])
    settled(1)
    wa_copy = pltpu.make_async_copy(wa, wa_out, loc_s.at[5])
    wa_copy.start()
    feats = wo.shape[1]
    ao[...] = nt(heads[:, :feats], wa[0, :, qkv:]) + nt(heads[:, feats:], wa[1, :, qkv:])

    def norm_rows(values, scales):
        inverse = lax.rsqrt(jnp.mean(values * values, axis=1, keepdims=True) + EPS)
        return values * inverse * (1.0 + scales)

    res[...] = inputs + norm_rows(ao[...], gains[1:2, :])
    pre[...] = norm_rows(res[...], gains[2:3, :]).astype(BF)
    ct_own.wait()
    for copy in ct_copies:
        copy.wait_recv()
    ct_out[...] = ct_all[...].T
    arrive(3)
    arrived()
    for copy in tok_copies + gain_copies + ct_copies + kv_first:
        copy.wait_send()
    for copy in kv_relay + list(passed.values()) + list(attn_copies.values()):
        copy.wait_send()
    bias_copy.wait()
    kv_copy.wait()
    wa_copy.wait()


def attention_front(*args):
    tok, _, gain_block, wq, wk, wv, wo, wg = args[:8]
    cut, tok_count = tok.shape
    members = 8
    width, loc = cut * members, tok_count // members
    depth, hidden = wg.shape
    slab = -(-hidden // (2 * TILE)) * TILE
    feats = wq.shape[1] + wk.shape[1] + wv.shape[1] + wo.shape[1]
    q_width = 2 * wq.shape[1]
    dma = pltpu.SemaphoreType.DMA
    struct = jax.ShapeDtypeStruct
    smem = pl.BlockSpec(memory_space=pltpu.SMEM)
    return pl.pallas_call(
        front_kernel,
        out_shape=(
            struct((3, width, slab), BF),
            struct((2, width, feats), BF),
            struct((tok_count, 2 * HD), BF),
            struct((tok_count, loc), BF),
            struct((loc, width), BF),
            struct((loc, width), BF),
            struct((8, width), F32),
            struct((loc, q_width), F32),
            struct((loc, HD), F32),
            struct((q_width // HD, loc), F32),
            struct((loc, HD // 2), F32),
            struct((loc, HD // 2), F32),
            struct((loc, q_width), BF),
            struct((loc, width), F32),
            struct((loc, width), F32),
            struct((loc, width), BF),
        ),
        in_specs=[any_spec()] * 10 + [vmem_spec()] * 2 + [smem] * 2,
        out_specs=[any_spec()] * 4 + [vmem_spec()] * 12,
        scratch_shapes=[
            pltpu.VMEM((3, depth, 2 * slab), BF),
            pltpu.VMEM((2, width, feats), BF),
            pltpu.VMEM((width, loc), BF),
            pltpu.VMEM((width, loc), BF),
            pltpu.VMEM((members,) + gain_block.shape, F32),
            pltpu.VMEM((loc, q_width), BF),
            pltpu.VMEM((tok_count, 2 * HD), BF),
            pltpu.VMEM((HD, tok_count), BF),
            pltpu.VMEM((tok_count, loc), BF),
            pltpu.VMEM((q_width // HD, tok_count, loc), F32),
            dma((3,)), dma((4,)), dma((7,)), dma((7,)), dma((7,)), dma((7,)), dma((7,)), dma((7,)),
            dma((4, 4)), dma((4, 4)), dma((2, 3)), dma((2, 3)), dma((18,)), dma((18,)), dma((18,)), dma((18,)),
            dma((18,)), dma((18,)), dma((18,)), dma((3,)), dma((3,)), dma((7,)), dma((7,)), dma((6,)),
        ],
        compiler_params=params(1),
        name="attention_front",
    )(*args)


def mlp_kernel(
    pre, res, ct, gains, w_h,
    lo, dgpost, dpre, dparts, pre_t_out, gm_t_out, hh_out, bb_out, aa_out,
    wg, wu, wd, pre_all, pre_t, gm_all, gm_t, aa, bb, hh, acc, own, parts, prc,
    w_sem, ag_s, ag_r, rs_s, rs_r, gs_s, gs_r, st_s,
):
    place, row, col, high, core = whereabouts()
    px, py, pd, pc = peers()
    quad = (px, py, pd)
    loc, width = pre.shape
    slab = wg.shape[1]
    tiles = slab // TILE
    stores = []

    def store(src, dst):
        copy = pltpu.make_async_copy(src, dst, st_s.at[len(stores)])
        copy.start()
        stores.append(copy)

    loads = [
        pltpu.make_async_copy(src, dst, w_sem.at[i])
        for i, (src, dst) in enumerate(((w_h.at[0], wg), (w_h.at[1], wu), (w_h.at[2], wd)))
    ]
    for copy in loads:
        copy.start()
    greet((px, py, pd, pc))

    def spread(src, buffer, send, recv):
        copies = [remote(src, buffer.at[i + 1], send.at[i], recv.at[i], p) for i, p in enumerate(quad)]
        for copy in copies:
            copy.start()
        return copies

    def lanes(n):
        return pl.ds(pl.multiple_of(n * TILE, TILE), TILE)

    gathers = spread(pre, pre_all, ag_s, ag_r)
    pre_all[0] = pre[...]
    for copy in loads:
        copy.wait()

    scatters = []
    for j in range(4):
        if j:
            gathers[j - 1].wait_recv()
        acc[...] = jnp.zeros_like(acc)
        rows = pl.ds(j * loc, loc)

        def forward(n, carry, j=j, rows=rows):
            x = pre_all[j]
            gate = nn(x, wg[:, lanes(n)])
            up = nn(x, wu[:, lanes(n)])
            square = gate * gate
            bend = jnp.tanh(GELU_C * gate * (1.0 + 0.044715 * square))
            half = 0.5 * (1.0 + bend)
            gelu = gate * half
            slope = half + 0.5 * gate * (1.0 - bend * bend) * (GELU_C * (1.0 + 0.134145 * square))
            hidden = (gelu * up).astype(BF)
            aa[rows, lanes(n)] = gelu.astype(BF)
            bb[rows, lanes(n)] = (up * slope).astype(BF)
            hh[rows, lanes(n)] = hidden
            acc[...] += nt(hidden, wd[:, lanes(n)])
            return carry

        lax.fori_loop(0, tiles, forward, 0)
        store(hh.at[rows], hh_out.at[rows])
        if j:
            parts[j - 1] = acc[...].astype(BF)
            copy = remote(parts.at[j - 1], prc.at[j - 1], rs_s.at[j - 1], rs_r.at[j - 1], quad[j - 1])
            copy.start()
            scatters.append(copy)
        else:
            own[...] = acc[...]
    for j in range(4):
        pre_t[:, j * loc : (j + 1) * loc] = pre_all[j].T
    store(pre_t, pre_t_out)
    for copy in scatters:
        copy.wait()
    out = own[...] + prc[0].astype(F32) + prc[1].astype(F32) + prc[2].astype(F32)
    scale = 1.0 + gains[3:4, :]
    inverse = lax.rsqrt(jnp.mean(out * out, axis=1, keepdims=True) + EPS)
    lo[...] = (res[...] + out * inverse * scale).astype(BF)
    upstream = ct[...].astype(F32)
    scaled = upstream * scale
    inner = jnp.mean(scaled * out, axis=1, keepdims=True)
    gm_all[0] = (scaled * inverse - out * (inverse * inverse * inverse * inner)).astype(BF)
    dgpost[...] = jnp.sum(upstream * out * inverse, axis=0, keepdims=True)

    gathers2 = spread(gm_all.at[0], gm_all, gs_s, gs_r)
    for j in range(4):
        if j:
            gathers2[j - 1].wait_recv()
        acc[...] = jnp.zeros_like(acc)
        rows = pl.ds(j * loc, loc)

        def backward(n, carry, j=j, rows=rows):
            grad_hidden = nn(gm_all[j], wd[:, lanes(n)])
            grad_gate = (grad_hidden * bb[rows, lanes(n)].astype(F32)).astype(BF)
            grad_up = (grad_hidden * aa[rows, lanes(n)].astype(F32)).astype(BF)
            bb[rows, lanes(n)] = grad_gate
            aa[rows, lanes(n)] = grad_up
            acc[...] += nt(grad_gate, wg[:, lanes(n)]) + nt(grad_up, wu[:, lanes(n)])
            return carry

        lax.fori_loop(0, tiles, backward, 0)
        gm_t[:, j * loc : (j + 1) * loc] = gm_all[j].T
        store(bb.at[rows], bb_out.at[rows])
        store(aa.at[rows], aa_out.at[rows])
        if j:
            dparts[j - 1] = acc[...].astype(BF)
        else:
            dpre[...] = acc[...]
    store(gm_t, gm_t_out)
    for copy in stores:
        copy.wait()
    for copy in gathers + gathers2:
        copy.wait_send()


def mlp(pre, res, ct, gains, weights):
    loc, width = pre.shape
    slab = weights.shape[2]
    dma = pltpu.SemaphoreType.DMA
    struct = jax.ShapeDtypeStruct
    return pl.pallas_call(
        mlp_kernel,
        out_shape=(
            struct((loc, width), BF),
            struct((1, width), F32),
            struct((loc, width), F32),
            struct((3, loc, width), BF),
            struct((width, 4 * loc), BF),
            struct((width, 4 * loc), BF),
            struct((4 * loc, slab), BF),
            struct((4 * loc, slab), BF),
            struct((4 * loc, slab), BF),
        ),
        in_specs=[vmem_spec()] * 4 + [any_spec()],
        out_specs=[vmem_spec()] * 4 + [any_spec()] * 5,
        scratch_shapes=[
            pltpu.VMEM((width, slab), BF),
            pltpu.VMEM((width, slab), BF),
            pltpu.VMEM((width, slab), BF),
            pltpu.VMEM((4, loc, width), BF),
            pltpu.VMEM((width, 4 * loc), BF),
            pltpu.VMEM((4, loc, width), BF),
            pltpu.VMEM((width, 4 * loc), BF),
            pltpu.VMEM((4 * loc, slab), BF),
            pltpu.VMEM((4 * loc, slab), BF),
            pltpu.VMEM((4 * loc, slab), BF),
            pltpu.VMEM((loc, width), F32),
            pltpu.VMEM((loc, width), F32),
            pltpu.VMEM((3, loc, width), BF),
            pltpu.VMEM((3, loc, width), BF),
            dma((3,)),
            dma((3,)), dma((3,)), dma((3,)), dma((3,)), dma((3,)), dma((3,)), dma((14,)),
        ],
        compiler_params=params(3),
        name="feed_forward",
    )(pre, res, ct, gains, weights)


class Line:
    def __init__(self, mine, inbox, middle, turned, out, sems, turns):
        self.mine, self.inbox, self.middle, self.turned, self.out = mine, inbox, middle, turned, out
        self.in_s, self.in_r, self.mid_s, self.mid_r, self.x_s, self.x_r, self.o_s, self.o_r, self.l_s, self.y_s, self.y_r = sems
        place, row, col, high, core = whereabouts()
        self.turns = turns
        self.end = (place % 3) == 0
        self.inner = (jnp.where(place == 0, 1, 2), row, col)
        self.outer = ((place - 1) * 3 % 6, row, col)
        self.across = (3 - place, row, col)
        self.beside = (place, row + 2 - 4 * high, col)
        self.place = place

    def root(self, k):
        return (k + self.place + 1) % 2

    def inward(self, k, h):
        return remote(self.mine.at[k, h], self.inbox.at[k, h], self.in_s.at[k, h], self.in_r.at[k, h], self.inner)

    def partial(self, k):
        return remote(
            self.mine.at[k, 1 - self.root(k)], self.middle.at[k], self.mid_s.at[k], self.mid_r.at[k], self.across
        )

    def turn(self, k):
        return remote(self.mine.at[k, 1], self.turned.at[k], self.y_s.at[k], self.y_r.at[k], self.beside)

    def exchange(self, k, h, source):
        return remote(source, self.out.at[k, h], self.x_s.at[k], self.x_r.at[k], self.across)

    def outward(self, k, h, source):
        return remote(source, self.out.at[k, h], self.o_s.at[k, h], self.o_r.at[k, h], self.outer)

    def keep(self, k, h, source):
        return pltpu.make_async_copy(source, self.out.at[k, h], self.l_s.at[k])

    def inside(self, act):
        pl.when(jnp.logical_not(self.end))(act)

    def turns_here(self, k):
        return jnp.logical_and(k < self.turns, self.root(k) == 1)

    def send(self, k):
        @pl.when(self.end)
        def _():
            for h in range(2):
                self.inward(k, h).start()

    def sent(self, k):
        @pl.when(self.end)
        def _():
            for h in range(2):
                self.inward(k, h).wait_send()

    def add(self, k):
        def act():
            other = 1 - self.root(k)
            self.inward(k, other).wait_recv()
            self.mine[k, other] = (
                self.mine[k, other].astype(F32) + self.inbox[k, other].astype(F32)
            ).astype(BF)
            self.partial(k).start()

        self.inside(act)

    def share(self, k, h, source):
        self.outward(k, h, source).start()
        self.exchange(k, h, source).start()
        self.keep(k, h, source).start()

    def total(self, k):
        def act():
            root = self.root(k)
            self.inward(k, root).wait_recv()
            self.partial(k).wait_recv()
            self.mine[k, root] = (
                self.mine[k, root].astype(F32) + self.inbox[k, root].astype(F32) + self.middle[k].astype(F32)
            ).astype(BF)

            if isinstance(k, int) and k >= self.turns:
                self.share(k, root, self.mine.at[k, root])
                return

            @pl.when(self.turns_here(k))
            def _():
                self.turn(k).start()

            @pl.when(jnp.logical_not(self.turns_here(k)))
            def _():
                self.share(k, root, self.mine.at[k, root])

        self.inside(act)

    def spread(self, k):
        @pl.when(jnp.logical_and(jnp.logical_not(self.end), self.turns_here(k)))
        def _():
            self.turn(k).wait_recv()
            self.share(k, 1, self.turned.at[k])

    def forward(self, k):
        def act():
            other = 1 - self.root(k)
            source = self.out.at[k, other]
            self.exchange(k, other, self.mine.at[k, other]).wait_recv()
            self.outward(k, other, source).start()

        self.inside(act)

    def drain(self, k):
        @pl.when(self.end)
        def _():
            for h in range(2):
                self.outward(k, h, self.mine.at[k, h]).wait_recv()

        def act():
            root = self.root(k)
            self.partial(k).wait_send()
            self.exchange(k, root, self.mine.at[k, root]).wait_send()
            self.keep(k, root, self.mine.at[k, root]).wait()
            for h in range(2):
                self.outward(k, h, self.mine.at[k, h]).wait_send()

            if not isinstance(k, int):
                pl.when(self.turns_here(k))(lambda: self.turn(k).wait_send())

        self.inside(act)


class Alone:
    def __init__(self, mine, inbox, middle, turned, out, sems, turns):
        self.mine, self.out, self.turns = mine, out, turns
        self.l_s, self.y_s, self.y_r = sems[0], sems[9], sems[10]
        place, row, col, high, core = whereabouts()
        self.beside = (place, row + 2 - 4 * high, col)

    def send(self, k):
        pass

    def sent(self, k):
        pass

    def add(self, k):
        pass

    def spread(self, k):
        pass

    def forward(self, k):
        pass

    def copy(self, k, h):
        return pltpu.make_async_copy(self.mine.at[k, h], self.out.at[k, h], self.l_s.at[k, h])

    def turn(self, k):
        return remote(self.mine.at[k, 1], self.out.at[k, 1], self.y_s.at[k], self.y_r.at[k], self.beside)

    def total(self, k):
        self.copy(k, 0).start()
        if isinstance(k, int):
            (self.turn(k) if k < self.turns else self.copy(k, 1)).start()
        else:
            pl.when(k < self.turns)(lambda: self.turn(k).start())
            pl.when(k >= self.turns)(lambda: self.copy(k, 1).start())

    def drain(self, k):
        self.copy(k, 0).wait()
        if isinstance(k, int):
            (self.turn(k) if k < self.turns else self.copy(k, 1)).wait()
        else:
            pl.when(k < self.turns)(lambda: self.turn(k).wait())
            pl.when(k >= self.turns)(lambda: self.copy(k, 1).wait())


def line_sems(count):
    dma = pltpu.SemaphoreType.DMA
    return [
        dma((count, 2)), dma((count, 2)), dma((count,)), dma((count,)), dma((count,)), dma((count,)),
        dma((count, 2)), dma((count, 2)), dma((count,)), dma((count,)), dma((count,)),
    ]


EARLY, AHEAD = 5, 3


def back_kernel(
    dparts, pre_t_h, gm_t_h, hh_h, bb_h, aa_h, own_h, lo_h, ao_h, ct_h, x_h, heads_h, q_pre_h, k_pre_h, kv_h,
    bias_h, wa_h, gains, gq, gk, lse, cos, sin, dgpost,
    g_out, a_out, lo_out, gt_out, gain_out,
    mine, inbox, middle, turned, a_mine, a_in, a_mid, parts, cr, summed, qr, rsr, lefts, ring, halves,
    own, ga, ao, ct, x, heads, q_pre, k_pre, kv, bias,
    k_t, gh, dk, dv, kv_cr, kv_qr, dh, cut_t, gain_buf, gain_in,
    in_s, t_s, big_s, wa_l, rs_s, rs_r, c_s, c_r, kc_s, kc_r, kq_s, kq_r, pc_s, pc_r, pq_s, pq_r,
    lo_s, lo_r, gt_s, gt_r, gn_s, gn_r, loc_s, *line_refs,
):
    place, row, col, high, core = whereabouts()
    me = 2 * row + col
    px, py, pd, pc = peers()
    quad = (px, py, pd)
    others = sent_to_all(me)
    on_line = lax.axis_size("dp") == 4
    make = Line if on_line else Alone
    hidden_pairs = turned.shape[0]
    line = make(mine, inbox, middle, turned, g_out, line_refs[:11], hidden_pairs)
    small = make(a_mine, a_in, a_mid, turned, a_out, line_refs[11:], 0)
    tiles = hidden_pairs // 3
    pairs = mine.shape[0]
    loc, width = x.shape
    depth = mine.shape[2]
    cut = width // 8
    all_tok = pre_t_h.shape[1]
    head_count = q_pre.shape[1] // HD
    half = HD // 2
    out_half = heads.shape[1] // 2
    feats = parts.shape[2]
    qkv = feats - out_half

    big = [
        pltpu.make_async_copy(src, lefts.at[i], big_s.at[i]) for i, src in enumerate((pre_t_h, gm_t_h))
    ]
    sources = (bb_h, aa_h, hh_h)

    def lanes(index):
        return pl.ds(pl.multiple_of(index * TILE, TILE), TILE)

    def load(n, m):
        return pltpu.make_async_copy(sources[m].at[:, lanes(n)], ring.at[m], t_s.at[m])

    for m in range(3):
        load(0, m).start()
        if m < 2:
            big[m].start()
    whole_wa = pltpu.make_async_copy(wa_h, parts, wa_l)
    smalls = [
        pltpu.make_async_copy(src, dst, in_s.at[i])
        for i, (src, dst) in enumerate(
            (
                (lo_h, ga), (own_h, own), (ao_h, ao), (ct_h, ct), (heads_h, heads),
                (kv_h, kv), (bias_h, bias), (q_pre_h, q_pre), (k_pre_h, k_pre), (x_h, x),
            )
        )
    ]
    for copy in smalls + [whole_wa]:
        copy.start()
    friends = [device for _, device in others]
    if on_line:
        friends += [((place + i) % 4, row, col) for i in range(1, 4)]
    greet(friends)
    scatters = [remote(dparts.at[i], rsr.at[i], rs_s.at[i], rs_r.at[i], device) for i, device in enumerate(quad)]
    for copy in scatters:
        copy.start()

    def to_core(k, m):
        return (
            remote(halves.at[m, 2 * high + 1 - core], mine.at[k, 0], c_s.at[m, 0], c_r.at[k, 0], pc),
            remote(halves.at[m, 3 - 2 * high - core], mine.at[k, 1], c_s.at[m, 1], c_r.at[k, 1], pc),
        )

    def produce(n):
        for m in range(3):
            load(n, m).wait()

        def one(m, carry):
            product = nn(lefts[m // 2], ring[m]).astype(BF)
            for b in range(4):
                halves[m, b] = product[b * depth : (b + 1) * depth]
            for copy in to_core(3 * n + m, m):
                copy.start()
            return carry

        lax.fori_loop(0, 3, one, 0)
        if n + 1 < tiles:
            for m in range(3):
                load(n + 1, m).start()

    def settle(n):
        def one(m, carry):
            k = 3 * n + m
            for copy in to_core(k, m):
                copy.wait()
            mine[k, 0] = (mine[k, 0].astype(F32) + halves[m, 2 * high + core].astype(F32)).astype(BF)
            mine[k, 1] = (mine[k, 1].astype(F32) + halves[m, 2 - 2 * high + core].astype(F32)).astype(BF)
            return carry

        lax.fori_loop(0, 3, one, 0)

    def line_step(k):
        line.sent(k)
        if isinstance(k, int):
            if k + AHEAD <= hidden_pairs:
                line.send(k + AHEAD)
        else:
            pl.when(k + AHEAD < pairs)(lambda: line.send(k + AHEAD))
        line.add(k)
        if not isinstance(k, int) or k >= 1:
            line.total(k - 1)
        if not isinstance(k, int) or k >= 2:
            line.spread(k - 2)
        if not isinstance(k, int) or k >= 3:
            line.forward(k - 3)

    for copy in big:
        copy.wait()
    produce(0)
    for n in range(1, EARLY):
        settle(n - 1)
        for i in range(3 * n - 3, min(3 * n, AHEAD)):
            line.send(i)
        produce(n)
        if n >= EARLY - 2:
            line_step(n + 2 - EARLY)

    here = pl.ds(pl.multiple_of(me * loc, 128), loc)

    def give(src, dst, send, recv, local):
        copies = [
            remote(src.at[pl.ds(i * cut, cut)], dst.at[:, here], send.at[j], recv.at[j], d)
            for j, (i, d) in enumerate(others)
        ]
        for copy in copies:
            copy.start()
        stays = pltpu.make_async_copy(src.at[pl.ds(me * cut, cut)], dst.at[:, here], local)
        stays.start()
        return copies, stays

    def norm_grad(values, scales, upstream):
        inverse = lax.rsqrt(jnp.mean(values * values, axis=1, keepdims=True) + EPS)
        scaled = upstream * (1.0 + scales)
        inner = jnp.mean(scaled * values, axis=1, keepdims=True)
        grad = scaled * inverse - values * (inverse * inverse * inverse * inner)
        return grad, jnp.sum(upstream * values * inverse, axis=0, keepdims=True)

    smalls[0].wait()
    cut_t[...] = ga[...].T
    lo_copies, lo_own = give(cut_t, lo_out, lo_s, lo_r, loc_s.at[0])
    gain_buf[...] = jnp.zeros_like(gain_buf)
    for copy in smalls[1:] + [whole_wa]:
        copy.wait()
    k_t[...] = kv[:, :HD].T
    settle(EARLY - 1)
    produce(EARLY)
    line_step(2)
    for copy in scatters:
        copy.wait()
    grad_pre = own[...] + rsr[0].astype(F32) + rsr[1].astype(F32) + rsr[2].astype(F32)
    inverse = lax.rsqrt(jnp.mean(ao[...] * ao[...], axis=1, keepdims=True) + EPS)
    residual = x[...].astype(F32) + ao[...] * inverse * (1.0 + gains[1:2, :])
    grad, gain_buf[0, 2:3, :] = norm_grad(residual, gains[2:3, :], grad_pre)
    own[...] = grad + ct[...].astype(F32)
    grad, gain_buf[0, 1:2, :] = norm_grad(ao[...], gains[1:2, :], own[...])
    ga[...] = grad.astype(BF)
    gain_buf[0, 3:4, :] = dgpost[...]
    for j in range(2):
        gh[:, j * out_half : (j + 1) * out_half] = nn(ga[...], parts[j, :, qkv:]).astype(BF)
    line_step(3)

    wanted = ((1 - col, 1 - high, pd), (1 - col, high, px), (col, 1 - high, py), (col, high, None))

    def block(ref, index, columns):
        return ref.at[pl.ds(pl.multiple_of(index * depth, 16), depth), columns]

    class PlaneSum:
        def __init__(self, which, start, size):
            self.columns = pl.ds(start, size)
            self.core = [
                remote(
                    block(parts.at[c2], 2 * y2 + 1 - core, self.columns),
                    block(cr, 2 * c2 + y2, self.columns),
                    pc_s.at[which, i],
                    pc_r.at[which, 2 * c2 + y2],
                    pc,
                )
                for i, (c2, y2, _) in enumerate(wanted)
            ]
            self.sends = [
                remote(block(summed, i, self.columns), qr.at[i, :, self.columns], pq_s.at[which, i], pq_r.at[which, i], d)
                for i, (_, _, d) in enumerate(wanted[:3])
            ]

        def begin(self):
            for copy in self.core:
                copy.start()

        def added(self, i):
            c2, y2, _ = wanted[i]
            self.core[i].wait_recv()
            return block(parts.at[c2], 2 * y2 + core, self.columns)[...].astype(F32) + block(
                cr, 2 * c2 + y2, self.columns
            )[...].astype(F32)

        def spread(self):
            for i in range(3):
                block(summed, i, self.columns)[...] = self.added(i).astype(BF)
                self.sends[i].start()

        def result(self):
            total = self.added(3)
            for i in range(3):
                self.sends[i].wait()
                total = total + qr[i, :, self.columns].astype(F32)
            for copy in self.core:
                copy.wait_send()
            return total.astype(BF)

    ga_t = ga[...].T
    for j in range(2):
        for n in range(out_half // TILE):
            parts[j, :, qkv + n * TILE : qkv + (n + 1) * TILE] = nn(
                ga_t, heads[:, j * out_half + n * TILE : j * out_half + (n + 1) * TILE]
            ).astype(BF)
    out_sum = PlaneSum(0, qkv, out_half)
    out_sum.begin()
    line_step(4)

    step_keys = 512
    for h in range(head_count):
        cols = slice(h * HD, (h + 1) * HD)
        query = head_forward(q_pre[:, cols], gq[...], cos[...], sin[...]) * (1.0 / math.sqrt(HD))
        query, grad_head = query.astype(BF), gh[:, cols]
        delta = jnp.sum((grad_head.astype(F32) * heads[:, cols].astype(F32)).T, axis=0, keepdims=True)

        def keys(c, total, h=h, query=query, grad_head=grad_head, delta=delta):
            rows = pl.ds(pl.multiple_of(c * step_keys, step_keys), step_keys)
            scores = nt(kv[rows, :HD], query) + bias[rows, :].astype(F32)
            probs = jnp.exp(scores - lse[h : h + 1, :])
            grad_probs = nt(kv[rows, HD:], grad_head)
            grad_scores = (probs * (grad_probs - delta)).astype(BF)
            add_v = nn(probs.astype(BF), grad_head)
            add_k = nn(grad_scores, query)
            if h:
                dv[rows, :] += add_v
                dk[rows, :] += add_k
            else:
                dv[rows, :] = add_v
                dk[rows, :] = add_k
            return total + nn(k_t[:, rows], grad_scores)

        total = lax.fori_loop(0, kv.shape[0] // step_keys, keys, jnp.zeros((HD, loc), F32))
        grad_query = total.T * (1.0 / math.sqrt(HD))
        first, second = grad_query[:, :half], grad_query[:, half:]
        turned = jnp.concatenate(
            [first * cos[...] + second * sin[...], second * cos[...] - first * sin[...]], axis=1
        )
        grad, gain = norm_grad(q_pre[:, cols], gq[...], turned)
        gain_buf[0, 4:5, :HD] += gain
        dh[h // 2, :, (h % 2) * HD : (h % 2 + 1) * HD] = grad.astype(BF)
        if h == 0:
            out_sum.spread()
        if h % 2:
            line_step(3 + 2 * (h // 2 + 1))
            line_step(4 + 2 * (h // 2 + 1))

    stage = [rsr.at[i // 2, :, pl.ds(i % 2 * 2 * HD, 2 * HD)] for i in range(4)]
    for i, slot in enumerate(KV_SLOTS):
        rows = slice((slot + 2) * loc, (slot + 3) * loc)
        stage[i][:, :HD] = dk[rows, :].astype(BF)
        stage[i][:, HD:] = dv[rows, :].astype(BF)
    kv_core = [remote(stage[i], kv_cr.at[i], kc_s.at[i], kc_r.at[i], pc) for i in range(4)]
    for copy in kv_core:
        copy.start()
    kv_sums = (ct.at[:, pl.ds(0, 2 * HD)], ct.at[:, pl.ds(2 * HD, 2 * HD)], rsr.at[2, :, pl.ds(0, 2 * HD)])
    kv_sends = []
    for i, device in ((3, pd), (1, px), (2, py)):
        kv_core[i].wait_recv()
        rows = slice(KV_SLOTS[i] * loc, (KV_SLOTS[i] + 1) * loc)
        kv_sums[i - 1][:, :HD] = (dk[rows, :] + kv_cr[i, :, :HD].astype(F32)).astype(BF)
        kv_sums[i - 1][:, HD:] = (dv[rows, :] + kv_cr[i, :, HD:].astype(F32)).astype(BF)
        copy = remote(kv_sums[i - 1], kv_qr.at[i - 1], kq_s.at[i - 1], kq_r.at[i - 1], device)
        copy.start()
        kv_sends.append(copy)
    kv_core[0].wait_recv()
    settle(EARLY)
    produce(EARLY + 1)
    line_step(9)
    line_step(10)
    total = out_sum.result()
    for i in range(2):
        mine[hidden_pairs, i] = total[:, i * TILE : (i + 1) * TILE]
    for copy in kv_sends:
        copy.wait()
    got = kv_qr[0].astype(F32) + kv_qr[1].astype(F32) + kv_qr[2].astype(F32) + kv_cr[0].astype(F32)
    grad_key = dk[:loc, :] + got[:, :HD]
    grad_value = dv[:loc, :] + got[:, HD:]
    first, second = grad_key[:, :half], grad_key[:, half:]
    turned = jnp.concatenate(
        [first * cos[...] + second * sin[...], second * cos[...] - first * sin[...]], axis=1
    )
    grad, gain_buf[0, 5:6, :HD] = norm_grad(k_pre[...], gk[...], turned)
    feat_q = dh.shape[2] - HD
    for j in range(2):
        dh[j, :, feat_q : feat_q + half] = grad[:, j * half : (j + 1) * half].astype(BF)
        dh[j, :, feat_q + half :] = grad_value[:, j * half : (j + 1) * half].astype(BF)

    inputs = x[...].astype(F32)
    inverse = lax.rsqrt(jnp.mean(inputs * inputs, axis=1, keepdims=True) + EPS)
    normed_t = (inputs * inverse * (1.0 + gains[0:1, :])).astype(BF).T
    grad_normed = nt(dh[0], parts[0, :, :qkv]) + nt(dh[1], parts[1, :, :qkv])
    for j in range(2):
        for n in range(qkv // TILE):
            parts[j, :, n * TILE : (n + 1) * TILE] = nn(normed_t, dh[j, :, n * TILE : (n + 1) * TILE]).astype(BF)
    in_sum = PlaneSum(1, 0, qkv)
    in_sum.begin()
    grad, gain_buf[0, 0:1, :] = norm_grad(inputs, gains[0:1, :], grad_normed)
    in_sum.spread()
    for copy in lo_copies:
        copy.wait_send()
    lo_own.wait()
    cut_t[...] = (grad + own[...]).astype(BF).T
    gt_copies, gt_own = give(cut_t, gt_out, gt_s, gt_r, loc_s.at[1])
    settle(EARLY + 1)
    line_step(11)
    gain_copies = [
        remote(gain_buf.at[0], gain_in.at[j], gn_s.at[j], gn_r.at[j], d) for j, (_, d) in enumerate(others)
    ]
    for copy in gain_copies:
        copy.start()
    for i in range(12, 16):
        line_step(i)
    total = in_sum.result()
    for i in range(2):
        mine[hidden_pairs + 1, i] = total[:, i * TILE : (i + 1) * TILE]
        a_mine[0, i] = total[i * depth // 2 : (i + 1) * depth // 2, 2 * TILE :]
    for copy in gain_copies:
        copy.wait()
    gain_buf[1] = gain_buf[0] + sum(gain_in[j] for j in range(7))
    gain_copies = [
        remote(gain_buf.at[1], gain_in.at[7 + i], gn_s.at[7 + i], gn_r.at[7 + i], ((place + i + 1) % 4, row, col))
        for i in range(3 if on_line else 0)
    ]
    for copy in gain_copies:
        copy.start()

    def step(k, carry):
        line_step(k)
        pl.when(k == pairs - 1 - AHEAD)(lambda: small.send(0))
        return carry

    lax.fori_loop(16, pairs, step, 0)
    small.sent(0)
    small.add(0)
    line.total(pairs - 1)
    line.forward(pairs - 3)
    small.total(0)
    line.forward(pairs - 2)
    line.forward(pairs - 1)
    small.forward(0)

    def drain(k, carry):
        line.drain(k)
        return carry

    lax.fori_loop(0, pairs, drain, 0)
    small.drain(0)
    for copy in gain_copies:
        copy.wait()
    gain_out[...] = gain_buf[1]
    for i in range(len(gain_copies)):
        gain_out[...] += gain_in[7 + i]
    for copy in lo_copies:
        copy.wait_recv()
    for copy in gt_copies:
        copy.wait()
    gt_own.wait()
    for copy in kv_core:
        copy.wait_send()


def attention_back(*args):
    dparts, pre_t, hh, lo, heads, q_pre, kv, bias, wa = (args[i] for i in (0, 1, 3, 7, 11, 12, 14, 15, 16))
    loc, width = lo.shape
    depth, feats = width // 4, wa.shape[2]
    hidden_pairs = 3 * hh.shape[1] // TILE
    pairs = hidden_pairs + 2
    keys = kv.shape[0]
    cut = width // 8
    dma = pltpu.SemaphoreType.DMA
    piece = (depth, TILE)
    rest = (depth // 2, TILE)
    struct = jax.ShapeDtypeStruct
    vmem = pltpu.VMEM
    return pl.pallas_call(
        back_kernel,
        out_shape=(
            struct((pairs, 2) + piece, BF),
            struct((1, 2) + rest, BF),
            struct((cut, keys), BF),
            struct((cut, keys), BF),
            struct((8, width), F32),
        ),
        in_specs=[any_spec()] * 17 + [vmem_spec()] * 7,
        out_specs=[any_spec()] * 4 + [vmem_spec()],
        scratch_shapes=[
            vmem((pairs, 2) + piece, BF),
            vmem((pairs, 2) + piece, BF),
            vmem((pairs,) + piece, BF),
            vmem((hidden_pairs,) + piece, BF),
            vmem((1, 2) + rest, BF),
            vmem((1, 2) + rest, BF),
            vmem((1,) + rest, BF),
            vmem((2, width, feats), BF),
            vmem((width, feats), BF),
            vmem((3 * depth, feats), BF),
            vmem((3, depth, feats), BF),
            vmem(dparts.shape, BF),
            vmem((2,) + pre_t.shape, BF),
            vmem((3, pre_t.shape[1], TILE), BF),
            vmem((3, 4) + piece, BF),
        ]
        + [vmem(args[i].shape, args[i].dtype) for i in (6, 7, 8, 9, 10, 11, 12, 13, 14, 15)]
        + [
            vmem((HD, keys), BF),
            vmem(heads.shape, BF),
            vmem((keys, HD), F32),
            vmem((keys, HD), F32),
            vmem((4, loc, 2 * HD), BF),
            vmem((3, loc, 2 * HD), BF),
            vmem((2, loc, feats - heads.shape[1] // 2), BF),
            vmem((width, loc), BF),
            vmem((2, 8, width), F32),
            vmem((10, 8, width), F32),
            dma((12,)), dma((3,)), dma((2,)), dma(()), dma((3,)), dma((3,)), dma((3, 2)), dma((hidden_pairs, 2)),
            dma((4,)), dma((4,)), dma((3,)), dma((3,)),
            dma((2, 4)), dma((2, 4)), dma((2, 3)), dma((2, 3)),
            dma((7,)), dma((7,)), dma((7,)), dma((7,)), dma((10,)), dma((10,)), dma((2,)),
        ]
        + line_sems(pairs)
        + line_sems(1),
        compiler_params=params(6),
        name="attention_back",
    )(*args)


def finish_kernel(high, gate_in, up_in, down_in, gate, up, down):
    gate[...] = gate_in[0, 0].astype(F32)
    up[...] = up_in[0, 0].astype(F32)
    down[...] = down_in[0, 0].astype(F32)


def finish(pieces, high, hidden, tiles):
    depth = pieces.shape[2]

    def source(m):
        return pl.BlockSpec(
            (1, 1, depth, TILE), lambda i, high: (3 * (i % tiles) + m, (i // tiles + high[0]) % 2, 0, 0)
        )

    return pl.pallas_call(
        finish_kernel,
        grid_spec=pltpu.PrefetchScalarGridSpec(
            num_scalar_prefetch=1,
            grid=(-(-hidden // TILE),),
            in_specs=[source(m) for m in range(3)],
            out_specs=[pl.BlockSpec((depth, TILE), lambda i, high: (0, i))] * 3,
        ),
        out_shape=[jax.ShapeDtypeStruct((depth, hidden), F32)] * 3,
        name="finish",
    )(high, pieces, pieces, pieces)


def body(
    tokens,
    cotangent,
    weight_query,
    weight_key,
    weight_value,
    weight_out,
    weight_gate,
    weight_up,
    weight_down,
    gain_input,
    gain_attn,
    gain_pre,
    gain_post,
    gain_query,
    gain_key,
    doc_lengths,
    block_size,
):
    cut = tokens.shape[1]
    row, col = lax.axis_index("row"), lax.axis_index("col")
    me = row * lax.axis_size("col") + col
    depth, hidden_half = weight_gate.shape
    q_half, kv_half = weight_query.shape[1], weight_key.shape[1]
    qkv_half = q_half + 2 * kv_half
    gain_block = jnp.pad(jnp.stack([gain_input, gain_attn, gain_pre, gain_post]), ((0, 4), (0, 0)))
    (
        w_hidden, w_attn, kv_all, bias, inputs, upstream, gains, query_pre, key_pre, log_total,
        cos_table, sin_table, head_bf, attn_out, residual, pre_normed,
    ) = attention_front(
        tokens.T, cotangent.T, gain_block, weight_query, weight_key, weight_value, weight_out.T,
        weight_gate, weight_up, weight_down.T, gain_query[None], gain_key[None], doc_lengths, block_size,
    )
    layer_rows, grad_g_post, grad_own, grad_parts, pre_t, grad_mlp_t, hidden, grad_gate, grad_up = mlp(
        pre_normed, residual, upstream, gains, w_hidden
    )
    tiles = hidden.shape[1] // TILE
    summed, attn_rest, layer_cut, token_cut, gain_sums = attention_back(
        grad_parts, pre_t, grad_mlp_t, hidden, grad_gate, grad_up, grad_own, layer_rows, attn_out, upstream,
        inputs, head_bf, query_pre, key_pre, kv_all, bias, w_attn, gains, gain_query[None], gain_key[None],
        log_total, cos_table, sin_table, grad_g_post,
    )
    if lax.axis_size("dp") != 4:
        summed, attn_rest, gain_sums = (lax.psum(v.astype(F32), "dp") for v in (summed, attn_rest, gain_sums))
    grad_gate, grad_up, grad_down = finish(summed, (row // 2)[None], hidden_half, tiles)
    attn_mine = jnp.concatenate(
        [summed[-1, 0], summed[-1, 1], attn_rest[0].reshape(depth, -1), summed[-2, 0], summed[-2, 1]], axis=1
    ).astype(F32)
    my_gains = lax.dynamic_slice_in_dim(gain_sums[:4], me * cut, cut, 1)
    return (
        layer_cut.T,
        token_cut.T.astype(F32),
        attn_mine[:, :q_half],
        attn_mine[:, q_half : q_half + kv_half],
        attn_mine[:, q_half + kv_half : qkv_half],
        attn_mine[:, qkv_half:].T,
        grad_gate,
        grad_up,
        grad_down.T,
        my_gains[0],
        my_gains[1],
        my_gains[2],
        my_gains[3],
        gain_sums[4, :HD],
        gain_sums[5, :HD],
    )


def solution(mesh):
    in_specs = (
        P("dp", ("row", "col")),
        P("dp", ("row", "col")),
        P("row", "col"),
        P("row", "col"),
        P("row", "col"),
        P("col", "row"),
        P("row", "col"),
        P("row", "col"),
        P("col", "row"),
        P(("row", "col")),
        P(("row", "col")),
        P(("row", "col")),
        P(("row", "col")),
        P(),
        P(),
        P("dp", None),
        P(),
    )
    out_specs = (
        P("dp", ("row", "col")),
        P("dp", ("row", "col")),
        P("row", "col"),
        P("row", "col"),
        P("row", "col"),
        P("col", "row"),
        P("row", "col"),
        P("row", "col"),
        P("col", "row"),
        P(("row", "col")),
        P(("row", "col")),
        P(("row", "col")),
        P(("row", "col")),
        P(),
        P(),
    )
    return jax.shard_map(body, mesh=mesh, in_specs=in_specs, out_specs=out_specs, check_vma=False)
```

```python
import functools
import math

import jax
import jax.numpy as jnp
from jax import lax
from jax.experimental import pallas as pl
from jax.experimental.pallas import tpu as pltpu
from jax.sharding import PartitionSpec as P

HD = 256
EPS = 1e-06
ROPE_BASE = 1000000.0
GELU_C = 0.7978845608028654
BF = jnp.bfloat16
F32 = jnp.float32
PLANE = ("row", "col")


def dot(left, right, dims):
    return lax.dot_general(left, right, (dims, ((), ())), preferred_element_type=F32)


def nn(left, right):
    return dot(left, right, ((1,), (0,)))


def nt(left, right):
    return dot(left, right, ((1,), (1,)))


def tn(left, right):
    return dot(left, right, ((0,), (0,)))


MESH = pl.DeviceIdType.MESH
TILE = 256
KV_SLOTS = (0, 1, 4, 5)
LEAD = 4
VMEM_LIMIT = 64 * 1024 * 1024 - 512 * 1024


def whereabouts():
    place, row, col = lax.axis_index("dp"), lax.axis_index("row"), lax.axis_index("col")
    return place, row, col, row // 2, row % 2


def peers():
    place, row, col, high, core = whereabouts()
    far = row + 2 - 4 * high
    return (
        (place, row, 1 - col),
        (place, far, col),
        (place, far, 1 - col),
        (place, row + 1 - 2 * core, col),
    )


def remote(src, dst, send, recv, device):
    return pltpu.make_async_remote_copy(
        src_ref=src, dst_ref=dst, send_sem=send, recv_sem=recv, device_id=device, device_id_type=MESH
    )


def greet(devices):
    barrier = pltpu.get_barrier_semaphore()
    for device in devices:
        pl.semaphore_signal(barrier, inc=1, device_id=device, device_id_type=MESH)
    pl.semaphore_wait(barrier, len(devices))


def any_spec():
    return pl.BlockSpec(memory_space=pl.ANY)


def vmem_spec():
    return pl.BlockSpec(memory_space=pltpu.VMEM)


def params(number):
    return pltpu.CompilerParams(
        collective_id=number, has_side_effects=True, vmem_limit_bytes=VMEM_LIMIT
    )


def token_places(lengths, span, tokens):
    inverse = 1.0 / jnp.full((1, 1), span[0], jnp.int32).astype(F32)
    document = jnp.zeros_like(tokens)
    first = jnp.zeros_like(tokens)
    end = jnp.int32(0)
    for i in range(lengths.shape[1]):
        end = end + lengths[0, i]
        past = tokens >= end
        document = jnp.where(past, i + 1, document)
        first = jnp.where(past, end, first)
    position = (tokens - first).astype(F32)
    return document, jnp.floor((position + 0.5) * inverse), position


def mask_bias(lengths, span, bias, me, slots):
    local = bias.shape[1]
    query_doc, query_block, _ = token_places(
        lengths, span, me * local + lax.broadcasted_iota(jnp.int32, (1, local), 1)
    )
    for s, owner in enumerate(slots):
        key_doc, key_block, _ = token_places(
            lengths, span, owner * local + lax.broadcasted_iota(jnp.int32, (local, 1), 0)
        )
        seen = (key_doc == query_doc) & (key_block <= query_block)
        bias[s * local : (s + 1) * local, :] = jnp.where(seen, 0.0, -1e30).astype(BF)


def slot_owners():
    place, row, col, high, core = whereabouts()
    owners = []
    for s in range(8):
        r2 = (high + s // 4) % 2 * 2 + (core + s // 2) % 2
        owners.append(2 * r2 + (col + s) % 2)
    return owners


def sent_to_all(index):
    place, row, col, high, core = whereabouts()
    others = []
    for s in range(1, 8):
        r2, c2 = (high + s // 4) % 2 * 2 + (core + s // 2) % 2, (col + s) % 2
        others.append((2 * r2 + c2, (place, r2, c2)))
    return others


def head_forward(values, scales, cos, sin):
    half = values.shape[1] // 2
    inverse = lax.rsqrt(jnp.mean(values * values, axis=1, keepdims=True) + EPS)
    scaled = values * inverse * (1.0 + scales)
    first, second = scaled[:, :half], scaled[:, half:]
    return jnp.concatenate([first * cos - second * sin, second * cos + first * sin], axis=1)


def front_kernel(
    tok, ct, gain_block, wq, wk, wv, wo, wg, wu, wd, gq, gk, lengths, span,
    wm_out, wa_out, kv_out, bias_out, x_out, ct_out, gains, q_pre, k_pre, lse, cos, sin, heads, ao, res, pre,
    wm, wa, tok_all, ct_all, gain_all, q_out, kv, v_t, bias, probs,
    wm_l, wa_l, tk_s, tk_r, ct_s, ct_r, gn_s, gn_r, wa_s, wa_r, wb_s, wb_r, wy_s, wy_r, wu_s, wd_s, wz_r, wc_s, wc_r, wo_s, wo_r, kv_s, kv_r, loc_s,
):
    place, row, col, high, core = whereabouts()
    me = 2 * row + col
    px, py, pd, pc = peers()
    others = sent_to_all(me)
    depth, hidden = wg.shape
    slab = wm_out.shape[2]
    cut = tok.shape[0]
    loc = x_out.shape[0]
    head_count = heads.shape[1] // HD
    half = HD // 2
    members = len(others) + 1
    share = lax.axis_size("dp") == 4
    far_row = row + 2 - 4 * high
    friends = [device for _, device in others]
    if share:
        friends += [((place + i) % 4, row, col) for i in range(1, 4)]

    loads = [
        pltpu.make_async_copy(src, wm.at[m, :, pl.ds(0, hidden)], wm_l.at[m]) for m, src in enumerate((wg, wu, wd))
    ]
    rows = pl.ds(row * depth, depth)
    far_rows = pl.ds(far_row * depth, depth)
    spots, at = [], 0
    for src in (wq, wk, wv, wo):
        spots.append(pl.ds(at, src.shape[1]))
        at += src.shape[1]
    qkv = at - wo.shape[1]
    own = [
        pltpu.make_async_copy(src, wa.at[col, rows, spot], wa_l.at[i])
        for i, (src, spot) in enumerate(zip((wq, wk, wv, wo), spots))
    ]
    tok_own = pltpu.make_async_copy(
        tok.at[:, pl.ds(pl.multiple_of(me * loc, 128), loc)], tok_all.at[pl.ds(me * cut, cut)], loc_s.at[0]
    )
    ct_own = pltpu.make_async_copy(
        ct.at[:, pl.ds(pl.multiple_of(me * loc, 128), loc)], ct_all.at[pl.ds(me * cut, cut)], loc_s.at[1]
    )
    gain_own = pltpu.make_async_copy(gain_block, gain_all.at[me], loc_s.at[2])
    for copy in [tok_own, gain_own] + own + [ct_own] + loads:
        copy.start()
    greet(friends)

    def scatter(src, dst, send, recv):
        copies = [
            remote(
                src.at[:, pl.ds(pl.multiple_of(index * loc, 128), loc)],
                dst.at[pl.ds(me * cut, cut)],
                send.at[j],
                recv.at[j],
                device,
            )
            for j, (index, device) in enumerate(others)
        ]
        for copy in copies:
            copy.start()
        return copies

    tok_copies = scatter(tok, tok_all, tk_s, tk_r)
    gain_copies = [
        remote(gain_block, gain_all.at[me], gn_s.at[j], gn_r.at[j], device) for j, (_, device) in enumerate(others)
    ]
    for copy in gain_copies:
        copy.start()
    attn_copies = {}

    def hand_out(which):
        for i in ((0, 1, 2), (3,))[which]:
            for j, device in enumerate((px, py, pd, pc)):
                attn_copies[i, j] = remote(
                    (wq, wk, wv, wo)[i], wa.at[col, rows, spots[i]], wa_s.at[i, j], wa_r.at[i, j], device
                )
                attn_copies[i, j].start()

    hand_out(0)

    for copy in loads:
        copy.wait()
    for m in range(3):
        wm[m, :, hidden:] = jnp.zeros((depth, 2 * slab - hidden), BF)
    mine = pl.ds(pl.multiple_of(high * slab, 128), slab)
    away = pl.ds(pl.multiple_of((1 - high) * slab, 128), slab)
    unit = depth // 6
    groups, rounds = 18, 4

    def group(start, g):
        return g // 6, pl.ds(pl.multiple_of(start + g % 6 * unit, 16), unit)

    def over(g):
        m, at = group(0, g)
        return remote(wm.at[m, at, away], wm_out.at[group(row * depth, g)], wy_s.at[g], wy_r.at[g], py)

    def along(g, step):
        spot = wm_out.at[group(far_row * depth, g)]
        return remote(spot, spot, (wu_s if step > 0 else wd_s).at[g], wz_r.at[g], ((place + step) % 4, row, col))

    def between(g):
        spot = wm_out.at[group(far_row * depth, g)]
        return remote(spot, spot, wc_s.at[g], wc_r.at[g], pc)

    own_hidden = [pltpu.make_async_copy(wm.at[m, :, mine], wm_out.at[m, rows], wm_l.at[m]) for m in range(3)]
    beside = [remote(wm.at[m, :, mine], wm_out.at[m, rows], wo_s.at[m], wo_r.at[m], pc) for m in range(3)]
    extra = 16 + place % 2
    for m in range(3):
        own_hidden[m].start()
        beside[m].start()
    fetched = [rounds * r + place for r in range(rounds)] + [extra] if share else list(range(groups))
    for g in fetched:
        over(g).start()

    def travel(distance, r, act_up, act_down):
        if distance == 0:
            g = rounds * r + place
            pl.when(place < 3)(lambda: act_up(g))
            pl.when(place > 0)(lambda: act_down(g))
        else:
            below, above = rounds * r + place - distance, rounds * r + place + distance
            pl.when(jnp.logical_and(place >= distance, place < 3))(lambda: act_up(below))
            pl.when(jnp.logical_and(place + distance <= 3, place > 0))(lambda: act_down(above))

    def arrive(distance, r):
        if distance == 0:
            g = rounds * r + place
            over(g).wait_recv()
            between(g).start()
        else:
            for g, there in (
                (rounds * r + place - distance, place >= distance),
                (rounds * r + place + distance, place + distance <= 3),
            ):

                @pl.when(there)
                def _(g=g):
                    along(g, 1).wait_recv()
                    between(g).start()

        travel(distance, r, lambda g: along(g, 1).start(), lambda g: along(g, -1).start())

    def arrive_extra():
        over(extra).wait_recv()
        between(extra).start()
        pl.when(place % 2 == 0)(lambda: along(extra, 1).start())
        pl.when(place % 2 == 1)(lambda: along(extra, -1).start())

    def arrive_whole():
        for g in fetched:
            over(g).wait_recv()
            between(g).start()

    if share:
        events = [
            functools.partial(arrive, distance, r)
            for distance, r in (
                (0, 0), (0, 1), (0, 2), (1, 0), (0, 3), (1, 1), (2, 0), (1, 2), (2, 1), (3, 0), (1, 3), (2, 2), (3, 1),
                (2, 3), (3, 2), (3, 3),
            )
        ]
        events.insert(7, arrive_extra)
    else:
        events = [arrive_whole]

    def poll(count):
        for _ in range(min(count, len(events))):
            events.pop(0)()

    def arrived():
        if share:
            other = 33 - extra
            along(other, 1).wait_recv()
            between(other).start()
            pl.when(place % 2 == 0)(lambda: along(extra, 1).wait_send())
            pl.when(place % 2 == 1)(lambda: along(extra, -1).wait_send())
            for distance in range(4):
                for r in range(rounds):
                    travel(distance, r, lambda g: along(g, 1).wait_send(), lambda g: along(g, -1).wait_send())
        for g in fetched:
            over(g).wait_send()
        for g in range(groups):
            between(g).wait()
        for m in range(3):
            beside[m].wait()
            own_hidden[m].wait()

    doc, _, position = token_places(lengths, span, me * loc + lax.broadcasted_iota(jnp.int32, (loc, 1), 0))
    steps = lax.broadcasted_iota(jnp.int32, (1, half), 1).astype(F32)
    phases = position * jnp.exp(steps * (-2.0 * math.log(ROPE_BASE) / HD))
    cos[...] = jnp.cos(phases)
    sin[...] = jnp.sin(phases)
    mask_bias(lengths, span, bias, me, slot_owners())
    bias_copy = pltpu.make_async_copy(bias, bias_out, loc_s.at[3])
    bias_copy.start()

    tok_own.wait()
    gain_own.wait()
    for copy in tok_copies + gain_copies:
        copy.wait_recv()
    for f in range(members):
        gains[:, f * cut : (f + 1) * cut] = gain_all[f]
    x_out[...] = tok_all[...].T
    inputs = x_out[...].astype(F32)
    inverse = lax.rsqrt(jnp.mean(inputs * inputs, axis=1, keepdims=True) + EPS)
    normed = (inputs * inverse * (1.0 + gains[0:1, :])).astype(BF)

    corners = ((row, 1 - col), (far_row, col), (far_row, 1 - col))
    part_spots = (pl.ds(0, qkv), pl.ds(qkv, wo.shape[1]))
    passed = {}

    def pass_on(which):
        for j, (r2, c2) in enumerate(corners):
            for i in ((0, 1, 2), (3,))[which]:
                attn_copies[i, j].wait_recv()
            slot = wa.at[c2, pl.ds(r2 * depth, depth), part_spots[which]]
            passed[which, j] = remote(slot, slot, wb_s.at[which, j], wb_r.at[which, j], pc)
            passed[which, j].start()

    def settled(which):
        for i in ((0, 1, 2), (3,))[which]:
            own[i].wait()
            attn_copies[i, 3].wait_recv()
        for j in range(3):
            passed[which, j].wait_recv()

    pass_on(0)
    poll(1)
    settled(0)
    poll(1)
    q_half, kv_half = wq.shape[1], wk.shape[1]
    for j in range(2):
        found = nn(normed, wa[j, :, :qkv])
        q_pre[:, j * q_half : (j + 1) * q_half] = found[:, :q_half]
        k_pre[:, j * kv_half : (j + 1) * kv_half] = found[:, q_half : q_half + kv_half]
        kv[:loc, HD + j * kv_half : HD + (j + 1) * kv_half] = found[:, q_half + kv_half :].astype(BF)
    kv[:loc, :HD] = head_forward(k_pre[...], gk[...], cos[...], sin[...]).astype(BF)
    kv_first = [
        remote(kv.at[pl.ds(0, loc)], kv.at[pl.ds(slot * loc, loc)], kv_s.at[i], kv_r.at[i], device)
        for i, (slot, device) in enumerate(((1, px), (4, py), (5, pd), (2, pc)))
    ]
    for copy in kv_first:
        copy.start()
    hand_out(1)
    ct_copies = scatter(ct, ct_all, ct_s, ct_r)
    for h in range(head_count):
        cols = slice(h * HD, (h + 1) * HD)
        q_out[:, cols] = (head_forward(q_pre[:, cols], gq[...], cos[...], sin[...]) * (1.0 / math.sqrt(HD))).astype(BF)
    lse[...] = jnp.zeros_like(lse)
    poll(1)

    def slot_scores(slot):
        keys = slice(slot * loc, (slot + 1) * loc)
        v_t[:, keys] = kv[keys, HD:].T
        for h in range(head_count):
            grown = jnp.exp(nt(kv[keys, :HD], q_out[:, h * HD : (h + 1) * HD]) + bias[keys, :].astype(F32))
            probs[h, keys, :] = grown
            lse[h : h + 1, :] += jnp.sum(grown, axis=0, keepdims=True)

    slot_scores(0)
    poll(2)
    kv_relay = []
    for i, slot in enumerate((1, 4, 5)):
        kv_first[i].wait_recv()
        keys = pl.ds(slot * loc, loc)
        copy = remote(kv.at[keys], kv.at[pl.ds((slot + 2) * loc, loc)], kv_s.at[4 + i], kv_r.at[4 + i], pc)
        copy.start()
        kv_relay.append(copy)
        slot_scores(slot)
        poll(1)
        if i == 0:
            kv_first[3].wait_recv()
            slot_scores(2)
            poll(1)
    for i, slot in enumerate((3, 6, 7)):
        kv_relay[i].wait_recv()
        slot_scores(slot)
        poll(1)
    kv_copy = pltpu.make_async_copy(kv, kv_out, loc_s.at[4])
    kv_copy.start()
    for h in range(head_count):
        inverse = 1.0 / lse[h : h + 1, :]
        total = nn(v_t[...], (probs[h] * inverse).astype(BF))
        heads[:, h * HD : (h + 1) * HD] = total.T.astype(BF)
        poll(1)
    lse[...] = jnp.log(lse[...])
    pass_on(1)
    poll(1)
    settled(1)
    wa_copy = pltpu.make_async_copy(wa, wa_out, loc_s.at[5])
    wa_copy.start()
    feats = wo.shape[1]
    ao[...] = nt(heads[:, :feats], wa[0, :, qkv:]) + nt(heads[:, feats:], wa[1, :, qkv:])

    def norm_rows(values, scales):
        inverse = lax.rsqrt(jnp.mean(values * values, axis=1, keepdims=True) + EPS)
        return values * inverse * (1.0 + scales)

    res[...] = inputs + norm_rows(ao[...], gains[1:2, :])
    pre[...] = norm_rows(res[...], gains[2:3, :]).astype(BF)
    ct_own.wait()
    for copy in ct_copies:
        copy.wait_recv()
    ct_out[...] = ct_all[...].T
    poll(len(events))
    arrived()
    for copy in tok_copies + gain_copies + ct_copies + kv_first:
        copy.wait_send()
    for copy in kv_relay + list(passed.values()) + list(attn_copies.values()):
        copy.wait_send()
    bias_copy.wait()
    kv_copy.wait()
    wa_copy.wait()


def attention_front(*args):
    tok, _, gain_block, wq, wk, wv, wo, wg = args[:8]
    cut, tok_count = tok.shape
    members = 8
    width, loc = cut * members, tok_count // members
    depth, hidden = wg.shape
    slab = -(-hidden // (2 * TILE)) * TILE
    feats = wq.shape[1] + wk.shape[1] + wv.shape[1] + wo.shape[1]
    q_width = 2 * wq.shape[1]
    dma = pltpu.SemaphoreType.DMA
    struct = jax.ShapeDtypeStruct
    smem = pl.BlockSpec(memory_space=pltpu.SMEM)
    return pl.pallas_call(
        front_kernel,
        out_shape=(
            struct((3, width, slab), BF),
            struct((2, width, feats), BF),
            struct((tok_count, 2 * HD), BF),
            struct((tok_count, loc), BF),
            struct((loc, width), BF),
            struct((loc, width), BF),
            struct((8, width), F32),
            struct((loc, q_width), F32),
            struct((loc, HD), F32),
            struct((q_width // HD, loc), F32),
            struct((loc, HD // 2), F32),
            struct((loc, HD // 2), F32),
            struct((loc, q_width), BF),
            struct((loc, width), F32),
            struct((loc, width), F32),
            struct((loc, width), BF),
        ),
        in_specs=[any_spec()] * 10 + [vmem_spec()] * 2 + [smem] * 2,
        out_specs=[any_spec()] * 4 + [vmem_spec()] * 12,
        scratch_shapes=[
            pltpu.VMEM((3, depth, 2 * slab), BF),
            pltpu.VMEM((2, width, feats), BF),
            pltpu.VMEM((width, loc), BF),
            pltpu.VMEM((width, loc), BF),
            pltpu.VMEM((members,) + gain_block.shape, F32),
            pltpu.VMEM((loc, q_width), BF),
            pltpu.VMEM((tok_count, 2 * HD), BF),
            pltpu.VMEM((HD, tok_count), BF),
            pltpu.VMEM((tok_count, loc), BF),
            pltpu.VMEM((q_width // HD, tok_count, loc), F32),
            dma((3,)), dma((4,)), dma((7,)), dma((7,)), dma((7,)), dma((7,)), dma((7,)), dma((7,)),
            dma((4, 4)), dma((4, 4)), dma((2, 3)), dma((2, 3)), dma((18,)), dma((18,)), dma((18,)), dma((18,)),
            dma((18,)), dma((18,)), dma((18,)), dma((3,)), dma((3,)), dma((7,)), dma((7,)), dma((6,)),
        ],
        compiler_params=params(1),
        name="attention_front",
    )(*args)


def mlp_kernel(
    pre, res, ct, gains, w_h,
    lo, dgpost, dpre, dparts, pre_t_out, gm_t_out, hh_out, bb_out, aa_out,
    wg, wu, wd, pre_all, pre_t, gm_all, gm_t, aa, bb, hh, acc, own, parts, prc,
    w_sem, ag_s, ag_r, rs_s, rs_r, gs_s, gs_r, st_s,
):
    place, row, col, high, core = whereabouts()
    px, py, pd, pc = peers()
    quad = (px, py, pd)
    loc, width = pre.shape
    slab = wg.shape[1]
    tiles = slab // TILE

    def store(kind, j, src, dst):
        rows = chunk_rows(j)
        return pltpu.make_async_copy(src.at[rows], dst.at[rows], st_s.at[kind, j])

    loads = [
        pltpu.make_async_copy(src, dst, w_sem.at[i])
        for i, (src, dst) in enumerate(((w_h.at[0], wg), (w_h.at[1], wu), (w_h.at[2], wd)))
    ]
    for copy in loads:
        copy.start()
    greet((px, py, pd, pc))

    def spread(src, buffer, send, recv):
        copies = [remote(src, buffer.at[i + 1], send.at[i], recv.at[i], p) for i, p in enumerate(quad)]
        for copy in copies:
            copy.start()
        return copies

    gathers = spread(pre, pre_all, ag_s, ag_r)
    pre_all[0] = pre[...]
    for copy in loads:
        copy.wait()

    def chunk_rows(j):
        return pl.ds(pl.multiple_of(j * loc, 256), loc)

    def chunk_device(j):
        return (place, (row + j // 2 * 2) % 4, (col + j) % 2)

    def give_part(j):
        return remote(parts.at[j - 1], prc.at[j - 1], rs_s.at[j - 1], rs_r.at[j - 1], chunk_device(j))

    def got_chunk(j, buffer, send, recv):
        pl.when(j > 0)(lambda: remote(pre, buffer.at[j], send.at[j - 1], recv.at[j - 1], chunk_device(j)).wait_recv())

    def forward(j, carry):
        got_chunk(j, pre_all, ag_s, ag_r)
        acc[...] = jnp.zeros_like(acc)
        rows = chunk_rows(j)
        for n in range(tiles):
            at = slice(n * TILE, (n + 1) * TILE)
            x = pre_all[j]
            gate = nn(x, wg[:, at])
            up = nn(x, wu[:, at])
            square = gate * gate
            bend = jnp.tanh(GELU_C * gate * (1.0 + 0.044715 * square))
            half = 0.5 * (1.0 + bend)
            gelu = gate * half
            slope = half + 0.5 * gate * (1.0 - bend * bend) * (GELU_C * (1.0 + 0.134145 * square))
            hidden = (gelu * up).astype(BF)
            aa[rows, at] = gelu.astype(BF)
            bb[rows, at] = (up * slope).astype(BF)
            hh[rows, at] = hidden
            acc[...] += nt(hidden, wd[:, at])
        store(0, j, hh, hh_out).start()

        @pl.when(j == 0)
        def _():
            own[...] = acc[...]

        @pl.when(j > 0)
        def _():
            parts[j - 1] = acc[...].astype(BF)
            give_part(j).start()

        return carry

    lax.fori_loop(0, 4, forward, 0)
    for j in range(4):
        pre_t[:, j * loc : (j + 1) * loc] = pre_all[j].T
    pre_copy = pltpu.make_async_copy(pre_t, pre_t_out, st_s.at[3, 0])
    pre_copy.start()
    for j in range(1, 4):
        give_part(j).wait()
    out = own[...] + prc[0].astype(F32) + prc[1].astype(F32) + prc[2].astype(F32)
    scale = 1.0 + gains[3:4, :]
    inverse = lax.rsqrt(jnp.mean(out * out, axis=1, keepdims=True) + EPS)
    lo[...] = (res[...] + out * inverse * scale).astype(BF)
    upstream = ct[...].astype(F32)
    scaled = upstream * scale
    inner = jnp.mean(scaled * out, axis=1, keepdims=True)
    gm_all[0] = (scaled * inverse - out * (inverse * inverse * inverse * inner)).astype(BF)
    dgpost[...] = jnp.sum(upstream * out * inverse, axis=0, keepdims=True)

    gathers2 = spread(gm_all.at[0], gm_all, gs_s, gs_r)
    def backward(j, carry):
        got_chunk(j, gm_all, gs_s, gs_r)
        acc[...] = jnp.zeros_like(acc)
        rows = chunk_rows(j)
        for n in range(tiles):
            at = slice(n * TILE, (n + 1) * TILE)
            grad_hidden = nn(gm_all[j], wd[:, at])
            grad_gate = (grad_hidden * bb[rows, at].astype(F32)).astype(BF)
            grad_up = (grad_hidden * aa[rows, at].astype(F32)).astype(BF)
            bb[rows, at] = grad_gate
            aa[rows, at] = grad_up
            acc[...] += nt(grad_gate, wg[:, at]) + nt(grad_up, wu[:, at])
        gm_t[:, rows] = gm_all[j].T
        store(1, j, bb, bb_out).start()
        store(2, j, aa, aa_out).start()

        @pl.when(j == 0)
        def _():
            dpre[...] = acc[...]

        @pl.when(j > 0)
        def _():
            dparts[j - 1] = acc[...].astype(BF)

        return carry

    lax.fori_loop(0, 4, backward, 0)
    gm_copy = pltpu.make_async_copy(gm_t, gm_t_out, st_s.at[3, 1])
    gm_copy.start()
    for j in range(4):
        store(0, j, hh, hh_out).wait()
        store(1, j, bb, bb_out).wait()
        store(2, j, aa, aa_out).wait()
    pre_copy.wait()
    gm_copy.wait()
    for copy in gathers + gathers2:
        copy.wait_send()


def mlp(pre, res, ct, gains, weights):
    loc, width = pre.shape
    slab = weights.shape[2]
    dma = pltpu.SemaphoreType.DMA
    struct = jax.ShapeDtypeStruct
    return pl.pallas_call(
        mlp_kernel,
        out_shape=(
            struct((loc, width), BF),
            struct((1, width), F32),
            struct((loc, width), F32),
            struct((3, loc, width), BF),
            struct((width, 4 * loc), BF),
            struct((width, 4 * loc), BF),
            struct((4 * loc, slab), BF),
            struct((4 * loc, slab), BF),
            struct((4 * loc, slab), BF),
        ),
        in_specs=[vmem_spec()] * 4 + [any_spec()],
        out_specs=[vmem_spec()] * 4 + [any_spec()] * 5,
        scratch_shapes=[
            pltpu.VMEM((width, slab), BF),
            pltpu.VMEM((width, slab), BF),
            pltpu.VMEM((width, slab), BF),
            pltpu.VMEM((4, loc, width), BF),
            pltpu.VMEM((width, 4 * loc), BF),
            pltpu.VMEM((4, loc, width), BF),
            pltpu.VMEM((width, 4 * loc), BF),
            pltpu.VMEM((4 * loc, slab), BF),
            pltpu.VMEM((4 * loc, slab), BF),
            pltpu.VMEM((4 * loc, slab), BF),
            pltpu.VMEM((loc, width), F32),
            pltpu.VMEM((loc, width), F32),
            pltpu.VMEM((3, loc, width), BF),
            pltpu.VMEM((3, loc, width), BF),
            dma((3,)),
            dma((3,)), dma((3,)), dma((3,)), dma((3,)), dma((3,)), dma((3,)), dma((4, 4)),
        ],
        compiler_params=params(3),
        name="feed_forward",
    )(pre, res, ct, gains, weights)


class Line:
    def __init__(self, mine, inbox, middle, turned, out, sems, turns):
        self.mine, self.inbox, self.middle, self.turned, self.out = mine, inbox, middle, turned, out
        self.in_s, self.in_r, self.mid_s, self.mid_r, self.x_s, self.x_r, self.o_s, self.o_r, self.l_s, self.y_s, self.y_r = sems
        place, row, col, high, core = whereabouts()
        self.turns = turns
        self.end = (place % 3) == 0
        self.inner = (jnp.where(place == 0, 1, 2), row, col)
        self.outer = ((place - 1) * 3 % 6, row, col)
        self.across = (3 - place, row, col)
        self.beside = (place, row + 2 - 4 * high, col)
        self.place = place

    def root(self, k):
        return (k + self.place + 1) % 2

    def inward(self, k, h):
        return remote(self.mine.at[k, h], self.inbox.at[k, h], self.in_s.at[k, h], self.in_r.at[k, h], self.inner)

    def partial(self, k):
        return remote(
            self.mine.at[k, 1 - self.root(k)], self.middle.at[k], self.mid_s.at[k], self.mid_r.at[k], self.across
        )

    def turn(self, k):
        return remote(self.mine.at[k, 1], self.turned.at[k // 2], self.y_s.at[k], self.y_r.at[k], self.beside)

    def spot(self, k, h):
        return self.out(k, h) if isinstance(k, int) else self.mine.at[k, h]

    def exchange(self, k, h, source):
        return remote(source, self.spot(k, h), self.x_s.at[k], self.x_r.at[k], self.across)

    def outward(self, k, h, source):
        return remote(source, self.spot(k, h), self.o_s.at[k, h], self.o_r.at[k, h], self.outer)

    def keep(self, k, h, source):
        return pltpu.make_async_copy(source, self.spot(k, h), self.l_s.at[k])

    def inside(self, act):
        pl.when(jnp.logical_not(self.end))(act)

    def turns_here(self, k):
        return jnp.logical_and(k < self.turns, self.root(k) == 1)

    def send(self, k):
        @pl.when(self.end)
        def _():
            for h in range(2):
                self.inward(k, h).start()

    def sent(self, k):
        @pl.when(self.end)
        def _():
            for h in range(2):
                self.inward(k, h).wait_send()

    def add(self, k):
        def act():
            other = 1 - self.root(k)
            self.inward(k, other).wait_recv()
            self.mine[k, other] = (
                self.mine[k, other].astype(F32) + self.inbox[k, other].astype(F32)
            ).astype(BF)
            self.partial(k).start()

        self.inside(act)

    def share(self, k, h, source):
        self.outward(k, h, source).start()
        self.exchange(k, h, source).start()
        self.keep(k, h, source).start()

    def total(self, k):
        def act():
            root = self.root(k)
            self.inward(k, root).wait_recv()
            self.partial(k).wait_recv()
            self.mine[k, root] = (
                self.mine[k, root].astype(F32) + self.inbox[k, root].astype(F32) + self.middle[k].astype(F32)
            ).astype(BF)

            if isinstance(k, int) and k >= self.turns:
                self.share(k, root, self.mine.at[k, root])
                return

            @pl.when(self.turns_here(k))
            def _():
                self.turn(k).start()

            @pl.when(jnp.logical_not(self.turns_here(k)))
            def _():
                self.share(k, root, self.mine.at[k, root])

        self.inside(act)

    def spread(self, k):
        @pl.when(jnp.logical_and(jnp.logical_not(self.end), self.turns_here(k)))
        def _():
            self.turn(k).wait_recv()
            self.share(k, 1, self.turned.at[k // 2])

    def forward(self, k, late):
        def act():
            other = 1 - self.root(k)
            source = self.out(k, other)
            self.exchange(k, other, self.mine.at[k, other]).wait_recv()
            self.outward(k, other, source).start()

        if k >= self.turns:
            if not late:
                self.inside(act)
        else:
            pl.when(jnp.logical_and(jnp.logical_not(self.end), self.root(k) == (0 if late else 1)))(act)

    def drain(self, k):
        @pl.when(self.end)
        def _():
            for h in range(2):
                self.outward(k, h, self.mine.at[k, h]).wait_recv()

        def act():
            root = self.root(k)
            self.partial(k).wait_send()
            self.exchange(k, root, self.mine.at[k, root]).wait_send()
            self.keep(k, root, self.mine.at[k, root]).wait()
            for h in range(2):
                self.outward(k, h, self.mine.at[k, h]).wait_send()

            if not isinstance(k, int):
                pl.when(self.turns_here(k))(lambda: self.turn(k).wait_send())

        self.inside(act)


class Alone:
    def __init__(self, mine, inbox, middle, turned, out, sems, turns):
        self.mine, self.out, self.turns = mine, out, turns
        self.l_s, self.y_s, self.y_r = sems[0], sems[9], sems[10]
        place, row, col, high, core = whereabouts()
        self.beside = (place, row + 2 - 4 * high, col)

    def send(self, k):
        pass

    def sent(self, k):
        pass

    def add(self, k):
        pass

    def spread(self, k):
        pass

    def forward(self, k, late):
        pass

    def copy(self, k, h):
        spot = self.out(k, h) if isinstance(k, int) else self.mine.at[k, h]
        return pltpu.make_async_copy(self.mine.at[k, h], spot, self.l_s.at[k, h])

    def turn(self, k):
        spot = self.out(k, 0) if isinstance(k, int) else self.mine.at[k, 1]
        return remote(self.mine.at[k, 1], spot, self.y_s.at[k], self.y_r.at[k], self.beside)

    def total(self, k):
        self.copy(k, 0).start()
        if isinstance(k, int):
            (self.turn(k) if k < self.turns else self.copy(k, 1)).start()
        else:
            pl.when(k < self.turns)(lambda: self.turn(k).start())
            pl.when(k >= self.turns)(lambda: self.copy(k, 1).start())

    def drain(self, k):
        self.copy(k, 0).wait()
        if isinstance(k, int):
            (self.turn(k) if k < self.turns else self.copy(k, 1)).wait()
        else:
            pl.when(k < self.turns)(lambda: self.turn(k).wait())
            pl.when(k >= self.turns)(lambda: self.copy(k, 1).wait())


def line_sems(count):
    dma = pltpu.SemaphoreType.DMA
    return [
        dma((count, 2)), dma((count, 2)), dma((count,)), dma((count,)), dma((count,)), dma((count,)),
        dma((count, 2)), dma((count, 2)), dma((count,)), dma((count,)), dma((count,)),
    ]


EARLY, AHEAD, SPREAD, LATE = 5, 3, 4, 6


def back_kernel(
    dparts, pre_t_h, gm_t_h, hh_h, bb_h, aa_h, own_h, lo_h, ao_h, ct_h, x_h, heads_h, q_pre_h, k_pre_h, kv_h,
    bias_h, wa_h, gains, gq, gk, lse, cos, sin, dgpost,
    gate_out, up_out, down_out, a_out, lo_out, gt_out, gain_out,
    mine, inbox, middle, turned, a_mine, a_in, a_mid, parts, cr, summed, qr, rsr, lefts, ring, halves,
    own, ga, ao, ct, x, heads, q_pre, k_pre, kv, bias,
    k_t, gh, dk, dv, kv_cr, kv_qr, dh, cut_t, gain_buf, gain_in,
    in_s, t_s, big_s, wa_l, rs_s, rs_r, c_s, c_r, kc_s, kc_r, kq_s, kq_r, pc_s, pc_r, pq_s, pq_r,
    lo_s, lo_r, gt_s, gt_r, gn_s, gn_r, loc_s, *line_refs,
):
    place, row, col, high, core = whereabouts()
    me = 2 * row + col
    px, py, pd, pc = peers()
    quad = (px, py, pd)
    others = sent_to_all(me)
    on_line = lax.axis_size("dp") == 4
    make = Line if on_line else Alone
    hidden_pairs = mine.shape[0] - 2
    slab = gate_out.shape[1] // 2

    def place_of(k, h):
        if k >= hidden_pairs:
            return a_out.at[:, pl.ds((0 if k > hidden_pairs else qkv) + h * TILE, TILE)]
        start = (high + h) % 2 * slab + k // 3 * TILE
        return (gate_out, up_out, down_out)[k % 3].at[:, pl.ds(pl.multiple_of(start, TILE), TILE)]

    def place_of_small(k, h):
        return a_out.at[pl.ds(h * (depth // 2), depth // 2), pl.ds(qkv - TILE, TILE)]

    line = make(mine, inbox, middle, turned, place_of, line_refs[:11], hidden_pairs)
    small = make(a_mine, a_in, a_mid, turned, place_of_small, line_refs[11:], 0)
    tiles = hidden_pairs // 3
    pairs = mine.shape[0]
    loc, width = x.shape
    depth = mine.shape[2]
    cut = width // 8
    all_tok = pre_t_h.shape[1]
    head_count = q_pre.shape[1] // HD
    half = HD // 2
    out_half = heads.shape[1] // 2
    feats = parts.shape[2]
    qkv = feats - out_half

    big = [
        pltpu.make_async_copy(src, lefts.at[i], big_s.at[i]) for i, src in enumerate((pre_t_h, gm_t_h))
    ]
    sources = (bb_h, aa_h, hh_h)

    def lanes(index):
        return pl.ds(pl.multiple_of(index * TILE, TILE), TILE)

    def load(n, m):
        return pltpu.make_async_copy(sources[m].at[:, lanes(n)], ring.at[m], t_s.at[m])

    for m in range(3):
        load(0, m).start()
        if m < 2:
            big[m].start()
    whole_wa = pltpu.make_async_copy(wa_h, parts, wa_l)
    smalls = [
        pltpu.make_async_copy(src, dst, in_s.at[i])
        for i, (src, dst) in enumerate(
            (
                (lo_h, ga), (own_h, own), (ao_h, ao), (ct_h, ct), (heads_h, heads),
                (kv_h, kv), (bias_h, bias), (q_pre_h, q_pre), (k_pre_h, k_pre), (x_h, x),
            )
        )
    ]
    for copy in smalls + [whole_wa]:
        copy.start()
    friends = [device for _, device in others]
    if on_line:
        friends += [((place + i) % 4, row, col) for i in range(1, 4)]
    greet(friends)
    scatters = [remote(dparts.at[i], rsr.at[i], rs_s.at[i], rs_r.at[i], device) for i, device in enumerate(quad)]
    for copy in scatters:
        copy.start()

    def to_core(k, m):
        return (
            remote(halves.at[m, 2 * high + 1 - core], mine.at[k, 0], c_s.at[m, 0], c_r.at[k, 0], pc),
            remote(halves.at[m, 3 - 2 * high - core], mine.at[k, 1], c_s.at[m, 1], c_r.at[k, 1], pc),
        )

    def produce(n):
        for m in range(3):
            load(n, m).wait()

        def one(m, carry):
            product = nn(lefts[m // 2], ring[m]).astype(BF)
            for b in range(4):
                halves[m, b] = product[b * depth : (b + 1) * depth]
            for copy in to_core(3 * n + m, m):
                copy.start()
            return carry

        lax.fori_loop(0, 3, one, 0)
        if n + 1 < tiles:
            for m in range(3):
                load(n + 1, m).start()

    def settle(n):
        def one(m, carry):
            k = 3 * n + m
            for copy in to_core(k, m):
                copy.wait()
            mine[k, 0] = (mine[k, 0].astype(F32) + halves[m, 2 * high + core].astype(F32)).astype(BF)
            mine[k, 1] = (mine[k, 1].astype(F32) + halves[m, 2 - 2 * high + core].astype(F32)).astype(BF)
            return carry

        lax.fori_loop(0, 3, one, 0)

    order = list(range(14)) + [hidden_pairs] + list(range(14, 18)) + [hidden_pairs + 1] + list(range(18, hidden_pairs))

    def line_rest(p):
        if 0 <= p - 1 < pairs:
            line.total(order[p - 1])
        if 0 <= p - SPREAD < pairs and order[p - SPREAD] < hidden_pairs:
            line.spread(order[p - SPREAD])
        if 0 <= p - 3 < pairs:
            line.forward(order[p - 3], False)
        if 0 <= p - LATE < pairs:
            line.forward(order[p - LATE], True)

    def line_step(p):
        line.sent(order[p])
        if p + AHEAD < pairs:
            line.send(order[p + AHEAD])
        elif p + AHEAD == pairs:
            small.send(0)
        line.add(order[p])
        line_rest(p)

    for copy in big:
        copy.wait()
    produce(0)
    for n in range(1, EARLY):
        settle(n - 1)
        for i in range(3 * n - 3, min(3 * n, AHEAD)):
            line.send(i)
        produce(n)
        if n >= EARLY - 2:
            line_step(n + 2 - EARLY)

    here = pl.ds(pl.multiple_of(me * loc, 128), loc)

    def give(src, dst, send, recv, local):
        copies = [
            remote(src.at[pl.ds(i * cut, cut)], dst.at[:, here], send.at[j], recv.at[j], d)
            for j, (i, d) in enumerate(others)
        ]
        for copy in copies:
            copy.start()
        stays = pltpu.make_async_copy(src.at[pl.ds(me * cut, cut)], dst.at[:, here], local)
        stays.start()
        return copies, stays

    def norm_grad(values, scales, upstream):
        inverse = lax.rsqrt(jnp.mean(values * values, axis=1, keepdims=True) + EPS)
        scaled = upstream * (1.0 + scales)
        inner = jnp.mean(scaled * values, axis=1, keepdims=True)
        grad = scaled * inverse - values * (inverse * inverse * inverse * inner)
        return grad, jnp.sum(upstream * values * inverse, axis=0, keepdims=True)

    smalls[0].wait()
    cut_t[...] = ga[...].T
    lo_copies, lo_own = give(cut_t, lo_out, lo_s, lo_r, loc_s.at[0])
    gain_buf[...] = jnp.zeros_like(gain_buf)
    for copy in smalls[1:] + [whole_wa]:
        copy.wait()
    k_t[...] = kv[:, :HD].T
    settle(EARLY - 1)
    produce(EARLY)
    line_step(2)
    for copy in scatters:
        copy.wait()
    grad_pre = own[...] + rsr[0].astype(F32) + rsr[1].astype(F32) + rsr[2].astype(F32)
    inverse = lax.rsqrt(jnp.mean(ao[...] * ao[...], axis=1, keepdims=True) + EPS)
    residual = x[...].astype(F32) + ao[...] * inverse * (1.0 + gains[1:2, :])
    grad, gain_buf[0, 2:3, :] = norm_grad(residual, gains[2:3, :], grad_pre)
    own[...] = grad + ct[...].astype(F32)
    grad, gain_buf[0, 1:2, :] = norm_grad(ao[...], gains[1:2, :], own[...])
    ga[...] = grad.astype(BF)
    gain_buf[0, 3:4, :] = dgpost[...]
    for j in range(2):
        gh[:, j * out_half : (j + 1) * out_half] = nn(ga[...], parts[j, :, qkv:]).astype(BF)
    line_step(3)

    wanted = ((1 - col, 1 - high, pd), (1 - col, high, px), (col, 1 - high, py), (col, high, None))

    def block(ref, index, columns):
        return ref.at[pl.ds(pl.multiple_of(index * depth, 16), depth), columns]

    class PlaneSum:
        def __init__(self, which, start, size):
            self.columns = pl.ds(start, size)
            self.core = [
                remote(
                    block(parts.at[c2], 2 * y2 + 1 - core, self.columns),
                    block(cr, 2 * c2 + y2, self.columns),
                    pc_s.at[which, i],
                    pc_r.at[which, 2 * c2 + y2],
                    pc,
                )
                for i, (c2, y2, _) in enumerate(wanted)
            ]
            self.sends = [
                remote(block(summed, i, self.columns), qr.at[i, :, self.columns], pq_s.at[which, i], pq_r.at[which, i], d)
                for i, (_, _, d) in enumerate(wanted[:3])
            ]

        def begin(self):
            for copy in self.core:
                copy.start()

        def added(self, i):
            c2, y2, _ = wanted[i]
            self.core[i].wait_recv()
            return block(parts.at[c2], 2 * y2 + core, self.columns)[...].astype(F32) + block(
                cr, 2 * c2 + y2, self.columns
            )[...].astype(F32)

        def spread(self):
            for i in range(3):
                block(summed, i, self.columns)[...] = self.added(i).astype(BF)
                self.sends[i].start()

        def result(self):
            total = self.added(3)
            for i in range(3):
                self.sends[i].wait()
                total = total + qr[i, :, self.columns].astype(F32)
            for copy in self.core:
                copy.wait_send()
            return total.astype(BF)

    ga_t = ga[...].T
    for j in range(2):
        for n in range(out_half // TILE):
            parts[j, :, qkv + n * TILE : qkv + (n + 1) * TILE] = nn(
                ga_t, heads[:, j * out_half + n * TILE : j * out_half + (n + 1) * TILE]
            ).astype(BF)
    out_sum = PlaneSum(0, qkv, out_half)
    out_sum.begin()
    line_step(4)

    step_keys = 512
    for h in range(head_count):
        cols = slice(h * HD, (h + 1) * HD)
        query = head_forward(q_pre[:, cols], gq[...], cos[...], sin[...]) * (1.0 / math.sqrt(HD))
        query, grad_head = query.astype(BF), gh[:, cols]
        delta = jnp.sum((grad_head.astype(F32) * heads[:, cols].astype(F32)).T, axis=0, keepdims=True)

        def keys(c, total, h=h, query=query, grad_head=grad_head, delta=delta):
            rows = pl.ds(pl.multiple_of(c * step_keys, step_keys), step_keys)
            scores = nt(kv[rows, :HD], query) + bias[rows, :].astype(F32)
            probs = jnp.exp(scores - lse[h : h + 1, :])
            grad_probs = nt(kv[rows, HD:], grad_head)
            grad_scores = (probs * (grad_probs - delta)).astype(BF)
            add_v = nn(probs.astype(BF), grad_head)
            add_k = nn(grad_scores, query)
            if h:
                dv[rows, :] += add_v
                dk[rows, :] += add_k
            else:
                dv[rows, :] = add_v
                dk[rows, :] = add_k
            return total + nn(k_t[:, rows], grad_scores)

        total = lax.fori_loop(0, kv.shape[0] // step_keys, keys, jnp.zeros((HD, loc), F32))
        grad_query = total.T * (1.0 / math.sqrt(HD))
        first, second = grad_query[:, :half], grad_query[:, half:]
        turned = jnp.concatenate(
            [first * cos[...] + second * sin[...], second * cos[...] - first * sin[...]], axis=1
        )
        grad, gain = norm_grad(q_pre[:, cols], gq[...], turned)
        gain_buf[0, 4:5, :HD] += gain
        dh[h // 2, :, (h % 2) * HD : (h % 2 + 1) * HD] = grad.astype(BF)
        if h == 0:
            out_sum.spread()
        if h % 2:
            line_step(3 + 2 * (h // 2 + 1))
            line_step(4 + 2 * (h // 2 + 1))

    stage = [rsr.at[i // 2, :, pl.ds(i % 2 * 2 * HD, 2 * HD)] for i in range(4)]
    for i, slot in enumerate(KV_SLOTS):
        rows = slice((slot + 2) * loc, (slot + 3) * loc)
        stage[i][:, :HD] = dk[rows, :].astype(BF)
        stage[i][:, HD:] = dv[rows, :].astype(BF)
    kv_core = [remote(stage[i], kv_cr.at[i], kc_s.at[i], kc_r.at[i], pc) for i in range(4)]
    for copy in kv_core:
        copy.start()
    inputs = x[...].astype(F32)
    inverse = lax.rsqrt(jnp.mean(inputs * inputs, axis=1, keepdims=True) + EPS)
    normed_t = (inputs * inverse * (1.0 + gains[0:1, :])).astype(BF).T
    feat_q = dh.shape[2] - HD
    ao[...] = nt(dh[0, :, :feat_q], parts[0, :, :feat_q]) + nt(dh[1, :, :feat_q], parts[1, :, :feat_q])
    kv_sums = (ct.at[:, pl.ds(0, 2 * HD)], ct.at[:, pl.ds(2 * HD, 2 * HD)], rsr.at[2, :, pl.ds(0, 2 * HD)])
    kv_sends = []
    for i, device in ((3, pd), (1, px), (2, py)):
        kv_core[i].wait_recv()
        rows = slice(KV_SLOTS[i] * loc, (KV_SLOTS[i] + 1) * loc)
        kv_sums[i - 1][:, :HD] = (dk[rows, :] + kv_cr[i, :, :HD].astype(F32)).astype(BF)
        kv_sums[i - 1][:, HD:] = (dv[rows, :] + kv_cr[i, :, HD:].astype(F32)).astype(BF)
        copy = remote(kv_sums[i - 1], kv_qr.at[i - 1], kq_s.at[i - 1], kq_r.at[i - 1], device)
        copy.start()
        kv_sends.append(copy)
    kv_core[0].wait_recv()
    for j in range(2):
        for n in range(feat_q // TILE):
            parts[j, :, n * TILE : (n + 1) * TILE] = nn(normed_t, dh[j, :, n * TILE : (n + 1) * TILE]).astype(BF)
    query_sum = PlaneSum(1, 0, feat_q)
    query_sum.begin()
    settle(EARLY)
    produce(EARLY + 1)
    query_sum.spread()
    line_step(9)
    line_step(10)
    total = out_sum.result()
    for i in range(2):
        mine[hidden_pairs, i] = total[:, i * TILE : (i + 1) * TILE]
    for copy in kv_sends:
        copy.wait()
    got = kv_qr[0].astype(F32) + kv_qr[1].astype(F32) + kv_qr[2].astype(F32) + kv_cr[0].astype(F32)
    grad_key = dk[:loc, :] + got[:, :HD]
    grad_value = dv[:loc, :] + got[:, HD:]
    first, second = grad_key[:, :half], grad_key[:, half:]
    turned_key = jnp.concatenate(
        [first * cos[...] + second * sin[...], second * cos[...] - first * sin[...]], axis=1
    )
    grad, gain_buf[0, 5:6, :HD] = norm_grad(k_pre[...], gk[...], turned_key)
    for j in range(2):
        dh[j, :, feat_q : feat_q + half] = grad[:, j * half : (j + 1) * half].astype(BF)
        dh[j, :, feat_q + half :] = grad_value[:, j * half : (j + 1) * half].astype(BF)
    ao[...] += nt(dh[0, :, feat_q:], parts[0, :, feat_q:qkv]) + nt(dh[1, :, feat_q:], parts[1, :, feat_q:qkv])
    for j in range(2):
        parts[j, :, feat_q:qkv] = nn(normed_t, dh[j, :, feat_q:]).astype(BF)
    key_sum = PlaneSum(2, feat_q, HD)
    key_sum.begin()
    grad, gain_buf[0, 0:1, :] = norm_grad(x[...].astype(F32), gains[0:1, :], ao[...])
    key_sum.spread()
    for copy in lo_copies:
        copy.wait_send()
    lo_own.wait()
    cut_t[...] = (grad + own[...]).astype(BF).T
    gt_copies, gt_own = give(cut_t, gt_out, gt_s, gt_r, loc_s.at[1])
    gain_copies = [
        remote(gain_buf.at[0], gain_in.at[j], gn_s.at[j], gn_r.at[j], d) for j, (_, d) in enumerate(others)
    ]
    for copy in gain_copies:
        copy.start()
    settle(EARLY + 1)
    line_step(11)
    line_step(12)
    line_step(13)
    total = query_sum.result()
    for i in range(2):
        mine[hidden_pairs + 1, i] = total[:, i * TILE : (i + 1) * TILE]
    line_step(14)
    line_step(15)
    total = key_sum.result()
    for i in range(2):
        a_mine[0, i] = total[i * depth // 2 : (i + 1) * depth // 2]
    for copy in gain_copies:
        copy.wait()
    gain_buf[1] = gain_buf[0] + sum(gain_in[j] for j in range(7))
    gain_copies = [
        remote(gain_buf.at[1], gain_in.at[7 + i], gn_s.at[7 + i], gn_r.at[7 + i], ((place + i + 1) % 4, row, col))
        for i in range(3 if on_line else 0)
    ]
    for copy in gain_copies:
        copy.start()

    for p in range(16, pairs):
        line_step(p)
    small.sent(0)
    small.add(0)
    line_rest(pairs)
    small.total(0)
    for p in range(pairs + 1, pairs + 4):
        line_rest(p)
    small.forward(0, False)
    for p in range(pairs + 4, pairs + LATE):
        line_rest(p)

    def drain(k, carry):
        line.drain(k)
        return carry

    lax.fori_loop(0, pairs, drain, 0)
    small.drain(0)
    for copy in gain_copies:
        copy.wait()
    gain_out[...] = gain_buf[1]
    for i in range(len(gain_copies)):
        gain_out[...] += gain_in[7 + i]
    for copy in lo_copies:
        copy.wait_recv()
    for copy in gt_copies:
        copy.wait()
    gt_own.wait()
    for copy in kv_core:
        copy.wait_send()


def attention_back(*args):
    dparts, pre_t, hh, lo, heads, q_pre, kv, bias, wa = (args[i] for i in (0, 1, 3, 7, 11, 12, 14, 15, 16))
    loc, width = lo.shape
    depth, feats = width // 4, wa.shape[2]
    hidden_pairs = 3 * hh.shape[1] // TILE
    pairs = hidden_pairs + 2
    keys = kv.shape[0]
    cut = width // 8
    dma = pltpu.SemaphoreType.DMA
    piece = (depth, TILE)
    rest = (depth // 2, TILE)
    struct = jax.ShapeDtypeStruct
    vmem = pltpu.VMEM
    return pl.pallas_call(
        back_kernel,
        out_shape=(
            struct((depth, 2 * hh.shape[1]), BF),
            struct((depth, 2 * hh.shape[1]), BF),
            struct((depth, 2 * hh.shape[1]), BF),
            struct((depth, feats), BF),
            struct((cut, keys), BF),
            struct((cut, keys), BF),
            struct((8, width), F32),
        ),
        in_specs=[any_spec()] * 17 + [vmem_spec()] * 7,
        out_specs=[any_spec()] * 6 + [vmem_spec()],
        scratch_shapes=[
            vmem((pairs, 2) + piece, BF),
            vmem((pairs, 2) + piece, BF),
            vmem((pairs,) + piece, BF),
            vmem(((hidden_pairs + 1) // 2,) + piece, BF),
            vmem((1, 2) + rest, BF),
            vmem((1, 2) + rest, BF),
            vmem((1,) + rest, BF),
            vmem((2, width, feats), BF),
            vmem((width, feats), BF),
            vmem((3 * depth, feats), BF),
            vmem((3, depth, feats), BF),
            vmem(dparts.shape, BF),
            vmem((2,) + pre_t.shape, BF),
            vmem((3, pre_t.shape[1], TILE), BF),
            vmem((3, 4) + piece, BF),
        ]
        + [vmem(args[i].shape, args[i].dtype) for i in (6, 7, 8, 9, 10, 11, 12, 13, 14, 15)]
        + [
            vmem((HD, keys), BF),
            vmem(heads.shape, BF),
            vmem((keys, HD), F32),
            vmem((keys, HD), F32),
            vmem((4, loc, 2 * HD), BF),
            vmem((3, loc, 2 * HD), BF),
            vmem((2, loc, feats - heads.shape[1] // 2), BF),
            vmem((width, loc), BF),
            vmem((2, 8, width), F32),
            vmem((10, 8, width), F32),
            dma((12,)), dma((3,)), dma((2,)), dma(()), dma((3,)), dma((3,)), dma((3, 2)), dma((hidden_pairs, 2)),
            dma((4,)), dma((4,)), dma((3,)), dma((3,)),
            dma((3, 4)), dma((3, 4)), dma((3, 3)), dma((3, 3)),
            dma((7,)), dma((7,)), dma((7,)), dma((7,)), dma((10,)), dma((10,)), dma((2,)),
        ]
        + line_sems(pairs)
        + line_sems(1),
        compiler_params=params(6),
        name="attention_back",
    )(*args)


def body(
    tokens,
    cotangent,
    weight_query,
    weight_key,
    weight_value,
    weight_out,
    weight_gate,
    weight_up,
    weight_down,
    gain_input,
    gain_attn,
    gain_pre,
    gain_post,
    gain_query,
    gain_key,
    doc_lengths,
    block_size,
):
    cut = tokens.shape[1]
    row, col = lax.axis_index("row"), lax.axis_index("col")
    me = row * lax.axis_size("col") + col
    depth, hidden_half = weight_gate.shape
    q_half, kv_half = weight_query.shape[1], weight_key.shape[1]
    qkv_half = q_half + 2 * kv_half
    gain_block = jnp.pad(jnp.stack([gain_input, gain_attn, gain_pre, gain_post]), ((0, 4), (0, 0)))
    (
        w_hidden, w_attn, kv_all, bias, inputs, upstream, gains, query_pre, key_pre, log_total,
        cos_table, sin_table, head_bf, attn_out, residual, pre_normed,
    ) = attention_front(
        tokens.T, cotangent.T, gain_block, weight_query, weight_key, weight_value, weight_out.T,
        weight_gate, weight_up, weight_down.T, gain_query[None], gain_key[None], doc_lengths, block_size,
    )
    layer_rows, grad_g_post, grad_own, grad_parts, pre_t, grad_mlp_t, hidden, grad_gate, grad_up = mlp(
        pre_normed, residual, upstream, gains, w_hidden
    )
    sum_gate, sum_up, sum_down, attn_sum, layer_cut, token_cut, gain_sums = attention_back(
        grad_parts, pre_t, grad_mlp_t, hidden, grad_gate, grad_up, grad_own, layer_rows, attn_out, upstream,
        inputs, head_bf, query_pre, key_pre, kv_all, bias, w_attn, gains, gain_query[None], gain_key[None],
        log_total, cos_table, sin_table, grad_g_post,
    )
    if lax.axis_size("dp") != 4:
        sum_gate, sum_up, sum_down, attn_sum, gain_sums = (
            lax.psum(v.astype(F32), "dp") for v in (sum_gate, sum_up, sum_down, attn_sum, gain_sums)
        )
    attn_sum = attn_sum.astype(F32)
    my_gains = lax.dynamic_slice_in_dim(gain_sums[:4], me * cut, cut, 1)
    return (
        layer_cut.T,
        token_cut.T.astype(F32),
        attn_sum[:, :q_half],
        attn_sum[:, q_half : q_half + kv_half],
        attn_sum[:, q_half + kv_half : qkv_half],
        attn_sum[:, qkv_half:].T,
        sum_gate[:, :hidden_half].astype(F32),
        sum_up[:, :hidden_half].astype(F32),
        sum_down[:, :hidden_half].astype(F32).T,
        my_gains[0],
        my_gains[1],
        my_gains[2],
        my_gains[3],
        gain_sums[4, :HD],
        gain_sums[5, :HD],
    )


def solution(mesh):
    in_specs = (
        P("dp", ("row", "col")),
        P("dp", ("row", "col")),
        P("row", "col"),
        P("row", "col"),
        P("row", "col"),
        P("col", "row"),
        P("row", "col"),
        P("row", "col"),
        P("col", "row"),
        P(("row", "col")),
        P(("row", "col")),
        P(("row", "col")),
        P(("row", "col")),
        P(),
        P(),
        P("dp", None),
        P(),
    )
    out_specs = (
        P("dp", ("row", "col")),
        P("dp", ("row", "col")),
        P("row", "col"),
        P("row", "col"),
        P("row", "col"),
        P("col", "row"),
        P("row", "col"),
        P("row", "col"),
        P("col", "row"),
        P(("row", "col")),
        P(("row", "col")),
        P(("row", "col")),
        P(("row", "col")),
        P(),
        P(),
    )
    return jax.shard_map(body, mesh=mesh, in_specs=in_specs, out_specs=out_specs, check_vma=False)
```

```python
import functools
import math

import jax
import jax.numpy as jnp
from jax import lax
from jax.experimental import pallas as pl
from jax.experimental.pallas import tpu as pltpu
from jax.sharding import PartitionSpec as P

HD = 256
EPS = 1e-06
ROPE_BASE = 1000000.0
GELU_C = 0.7978845608028654
BF = jnp.bfloat16
F32 = jnp.float32
PLANE = ("row", "col")


def dot(left, right, dims):
    return lax.dot_general(left, right, (dims, ((), ())), preferred_element_type=F32)


def nn(left, right):
    return dot(left, right, ((1,), (0,)))


def nt(left, right):
    return dot(left, right, ((1,), (1,)))


def tn(left, right):
    return dot(left, right, ((0,), (0,)))


MESH = pl.DeviceIdType.MESH
TILE = 256
KV_SLOTS = (0, 1, 4, 5)
LEAD = 4
VMEM_LIMIT = 64 * 1024 * 1024 - 512 * 1024


def whereabouts():
    place, row, col = lax.axis_index("dp"), lax.axis_index("row"), lax.axis_index("col")
    return place, row, col, row // 2, row % 2


def peers():
    place, row, col, high, core = whereabouts()
    far = row + 2 - 4 * high
    return (
        (place, row, 1 - col),
        (place, far, col),
        (place, far, 1 - col),
        (place, row + 1 - 2 * core, col),
    )


def remote(src, dst, send, recv, device):
    return pltpu.make_async_remote_copy(
        src_ref=src, dst_ref=dst, send_sem=send, recv_sem=recv, device_id=device, device_id_type=MESH
    )


def greet(devices):
    barrier = pltpu.get_barrier_semaphore()
    for device in devices:
        pl.semaphore_signal(barrier, inc=1, device_id=device, device_id_type=MESH)
    pl.semaphore_wait(barrier, len(devices))


def any_spec():
    return pl.BlockSpec(memory_space=pl.ANY)


def vmem_spec():
    return pl.BlockSpec(memory_space=pltpu.VMEM)


def params(number):
    return pltpu.CompilerParams(
        collective_id=number, has_side_effects=True, vmem_limit_bytes=VMEM_LIMIT
    )


def token_places(lengths, span, tokens):
    inverse = 1.0 / jnp.full((1, 1), span[0], jnp.int32).astype(F32)
    document = jnp.zeros_like(tokens)
    first = jnp.zeros_like(tokens)
    end = jnp.int32(0)
    for i in range(lengths.shape[1]):
        end = end + lengths[0, i]
        past = tokens >= end
        document = jnp.where(past, i + 1, document)
        first = jnp.where(past, end, first)
    position = (tokens - first).astype(F32)
    return document, jnp.floor((position + 0.5) * inverse), position


def mask_bias(lengths, span, bias, me, slots):
    local = bias.shape[1]
    query_doc, query_block, _ = token_places(
        lengths, span, me * local + lax.broadcasted_iota(jnp.int32, (1, local), 1)
    )
    for s, owner in enumerate(slots):
        key_doc, key_block, _ = token_places(
            lengths, span, owner * local + lax.broadcasted_iota(jnp.int32, (local, 1), 0)
        )
        seen = (key_doc == query_doc) & (key_block <= query_block)
        bias[s * local : (s + 1) * local, :] = jnp.where(seen, 0.0, -1e30).astype(BF)


def slot_owners():
    place, row, col, high, core = whereabouts()
    owners = []
    for s in range(8):
        r2 = (high + s // 4) % 2 * 2 + (core + s // 2) % 2
        owners.append(2 * r2 + (col + s) % 2)
    return owners


def sent_to_all(index):
    place, row, col, high, core = whereabouts()
    others = []
    for s in range(1, 8):
        r2, c2 = (high + s // 4) % 2 * 2 + (core + s // 2) % 2, (col + s) % 2
        others.append((2 * r2 + c2, (place, r2, c2)))
    return others


def head_forward(values, scales, cos, sin):
    half = values.shape[1] // 2
    inverse = lax.rsqrt(jnp.mean(values * values, axis=1, keepdims=True) + EPS)
    scaled = values * inverse * (1.0 + scales)
    first, second = scaled[:, :half], scaled[:, half:]
    return jnp.concatenate([first * cos - second * sin, second * cos + first * sin], axis=1)


def front_kernel(
    tok, ct, gain_block, wq, wk, wv, wo, wg, wu, wd, gq, gk, lengths, span,
    wm_out, wa_out, kv_out, bias_out, x_out, ct_out, gains, q_pre, k_pre, lse, cos, sin, heads, ao, res, pre,
    wm, wa, tok_all, ct_all, gain_all, q_out, kv, v_t, bias, probs,
    wm_l, wa_l, tk_s, tk_r, ct_s, ct_r, gn_s, gn_r, wa_s, wa_r, wb_s, wb_r, wy_s, wy_r, wu_s, wd_s, wz_r, wc_s, wc_r, wo_s, wo_r, kv_s, kv_r, loc_s,
):
    place, row, col, high, core = whereabouts()
    me = 2 * row + col
    px, py, pd, pc = peers()
    others = sent_to_all(me)
    depth, hidden = wg.shape
    slab = wm_out.shape[2]
    cut = tok.shape[0]
    loc = x_out.shape[0]
    head_count = heads.shape[1] // HD
    half = HD // 2
    members = len(others) + 1
    share = lax.axis_size("dp") == 4
    far_row = row + 2 - 4 * high
    friends = [device for _, device in others]
    if share:
        friends += [((place + i) % 4, row, col) for i in range(1, 4)]

    loads = [
        pltpu.make_async_copy(src, wm.at[m, :, pl.ds(0, hidden)], wm_l.at[m]) for m, src in enumerate((wg, wu, wd))
    ]
    rows = pl.ds(row * depth, depth)
    far_rows = pl.ds(far_row * depth, depth)
    spots, at = [], 0
    for src in (wq, wk, wv, wo):
        spots.append(pl.ds(at, src.shape[1]))
        at += src.shape[1]
    qkv = at - wo.shape[1]
    own = [
        pltpu.make_async_copy(src, wa.at[col, rows, spot], wa_l.at[i])
        for i, (src, spot) in enumerate(zip((wq, wk, wv, wo), spots))
    ]
    tok_own = pltpu.make_async_copy(
        tok.at[:, pl.ds(pl.multiple_of(me * loc, 128), loc)], tok_all.at[pl.ds(me * cut, cut)], loc_s.at[0]
    )
    ct_own = pltpu.make_async_copy(
        ct.at[:, pl.ds(pl.multiple_of(me * loc, 128), loc)], ct_all.at[pl.ds(me * cut, cut)], loc_s.at[1]
    )
    gain_own = pltpu.make_async_copy(gain_block, gain_all.at[me], loc_s.at[2])
    for copy in [tok_own, gain_own] + own + [ct_own] + loads:
        copy.start()
    greet(friends)

    def scatter(src, dst, send, recv):
        copies = [
            remote(
                src.at[:, pl.ds(pl.multiple_of(index * loc, 128), loc)],
                dst.at[pl.ds(me * cut, cut)],
                send.at[j],
                recv.at[j],
                device,
            )
            for j, (index, device) in enumerate(others)
        ]
        for copy in copies:
            copy.start()
        return copies

    tok_copies = scatter(tok, tok_all, tk_s, tk_r)
    gain_copies = [
        remote(gain_block, gain_all.at[me], gn_s.at[j], gn_r.at[j], device) for j, (_, device) in enumerate(others)
    ]
    for copy in gain_copies:
        copy.start()
    attn_copies = {}

    def hand_out(which):
        for i in ((0, 1, 2), (3,))[which]:
            for j, device in enumerate((px, py, pd, pc)):
                attn_copies[i, j] = remote(
                    (wq, wk, wv, wo)[i], wa.at[col, rows, spots[i]], wa_s.at[i, j], wa_r.at[i, j], device
                )
                attn_copies[i, j].start()

    for copy in loads:
        copy.wait()
    for m in range(3):
        wm[m, :, hidden:] = jnp.zeros((depth, 2 * slab - hidden), BF)
    mine = pl.ds(pl.multiple_of(high * slab, 128), slab)
    away = pl.ds(pl.multiple_of((1 - high) * slab, 128), slab)
    unit = depth // 6
    groups, rounds = 18, 4

    def group(start, g):
        return g // 6, pl.ds(pl.multiple_of(start + g % 6 * unit, 16), unit)

    def over(g):
        m, at = group(0, g)
        return remote(wm.at[m, at, away], wm_out.at[group(row * depth, g)], wy_s.at[g], wy_r.at[g], py)

    def along(g, step):
        spot = wm_out.at[group(far_row * depth, g)]
        return remote(spot, spot, (wu_s if step > 0 else wd_s).at[g], wz_r.at[g], ((place + step) % 4, row, col))

    def between(g):
        spot = wm_out.at[group(far_row * depth, g)]
        return remote(spot, spot, wc_s.at[g], wc_r.at[g], pc)

    own_hidden = [pltpu.make_async_copy(wm.at[m, :, mine], wm_out.at[m, rows], wm_l.at[m]) for m in range(3)]
    beside = [remote(wm.at[m, :, mine], wm_out.at[m, rows], wo_s.at[m], wo_r.at[m], pc) for m in range(3)]
    extra = 16 + place % 2
    for m in range(3):
        own_hidden[m].start()
        beside[m].start()
    fetched = [rounds * r + place for r in range(rounds)] + [extra] if share else list(range(groups))
    for g in fetched[:rounds]:
        over(g).start()
    hand_out(0)
    for g in fetched[rounds:]:
        over(g).start()

    def travel(distance, r, act_up, act_down):
        if distance == 0:
            g = rounds * r + place
            pl.when(place < 3)(lambda: act_up(g))
            pl.when(place > 0)(lambda: act_down(g))
        else:
            below, above = rounds * r + place - distance, rounds * r + place + distance
            pl.when(jnp.logical_and(place >= distance, place < 3))(lambda: act_up(below))
            pl.when(jnp.logical_and(place + distance <= 3, place > 0))(lambda: act_down(above))

    def arrive(distance, r):
        if distance == 0:
            g = rounds * r + place
            over(g).wait_recv()
            between(g).start()
        else:
            for g, there in (
                (rounds * r + place - distance, place >= distance),
                (rounds * r + place + distance, place + distance <= 3),
            ):

                @pl.when(there)
                def _(g=g):
                    along(g, 1).wait_recv()
                    between(g).start()

        travel(distance, r, lambda g: along(g, 1).start(), lambda g: along(g, -1).start())

    def arrive_extra():
        over(extra).wait_recv()
        between(extra).start()
        pl.when(place % 2 == 0)(lambda: along(extra, 1).start())
        pl.when(place % 2 == 1)(lambda: along(extra, -1).start())

    def arrive_whole():
        for g in fetched:
            over(g).wait_recv()
            between(g).start()

    if share:
        events = [
            functools.partial(arrive, distance, r)
            for distance, r in (
                (0, 0), (0, 1), (0, 2), (1, 0), (0, 3), (1, 1), (2, 0), (1, 2), (2, 1), (3, 0), (1, 3), (2, 2), (3, 1),
                (2, 3), (3, 2), (3, 3),
            )
        ]
        events.insert(7, arrive_extra)
    else:
        events = [arrive_whole]

    def poll(count):
        for _ in range(min(count, len(events))):
            events.pop(0)()

    def arrived():
        if share:
            other = 33 - extra
            along(other, 1).wait_recv()
            between(other).start()
            pl.when(place % 2 == 0)(lambda: along(extra, 1).wait_send())
            pl.when(place % 2 == 1)(lambda: along(extra, -1).wait_send())
            for distance in range(4):
                for r in range(rounds):
                    travel(distance, r, lambda g: along(g, 1).wait_send(), lambda g: along(g, -1).wait_send())
        for g in fetched:
            over(g).wait_send()
        for g in range(groups):
            between(g).wait()
        for m in range(3):
            beside[m].wait()
            own_hidden[m].wait()

    doc, _, position = token_places(lengths, span, me * loc + lax.broadcasted_iota(jnp.int32, (loc, 1), 0))
    steps = lax.broadcasted_iota(jnp.int32, (1, half), 1).astype(F32)
    phases = position * jnp.exp(steps * (-2.0 * math.log(ROPE_BASE) / HD))
    cos[...] = jnp.cos(phases)
    sin[...] = jnp.sin(phases)
    mask_bias(lengths, span, bias, me, slot_owners())
    bias_copy = pltpu.make_async_copy(bias, bias_out, loc_s.at[3])
    bias_copy.start()

    tok_own.wait()
    gain_own.wait()
    for copy in tok_copies + gain_copies:
        copy.wait_recv()
    for f in range(members):
        gains[:, f * cut : (f + 1) * cut] = gain_all[f]
    x_out[...] = tok_all[...].T
    inputs = x_out[...].astype(F32)
    inverse = lax.rsqrt(jnp.mean(inputs * inputs, axis=1, keepdims=True) + EPS)
    normed = (inputs * inverse * (1.0 + gains[0:1, :])).astype(BF)

    corners = ((row, 1 - col), (far_row, col), (far_row, 1 - col))
    part_spots = (pl.ds(0, qkv), pl.ds(qkv, wo.shape[1]))
    passed = {}

    def pass_on(which):
        for j, (r2, c2) in enumerate(corners):
            for i in ((0, 1, 2), (3,))[which]:
                attn_copies[i, j].wait_recv()
            slot = wa.at[c2, pl.ds(r2 * depth, depth), part_spots[which]]
            passed[which, j] = remote(slot, slot, wb_s.at[which, j], wb_r.at[which, j], pc)
            passed[which, j].start()

    def settled(which):
        for i in ((0, 1, 2), (3,))[which]:
            own[i].wait()
            attn_copies[i, 3].wait_recv()
        for j in range(3):
            passed[which, j].wait_recv()

    poll(4)
    pass_on(0)
    poll(1)
    settled(0)
    poll(1)
    q_half, kv_half = wq.shape[1], wk.shape[1]
    for j in range(2):
        found = nn(normed, wa[j, :, :qkv])
        q_pre[:, j * q_half : (j + 1) * q_half] = found[:, :q_half]
        k_pre[:, j * kv_half : (j + 1) * kv_half] = found[:, q_half : q_half + kv_half]
        kv[:loc, HD + j * kv_half : HD + (j + 1) * kv_half] = found[:, q_half + kv_half :].astype(BF)
    kv[:loc, :HD] = head_forward(k_pre[...], gk[...], cos[...], sin[...]).astype(BF)
    kv_first = [
        remote(kv.at[pl.ds(0, loc)], kv.at[pl.ds(slot * loc, loc)], kv_s.at[i], kv_r.at[i], device)
        for i, (slot, device) in enumerate(((1, px), (4, py), (5, pd), (2, pc)))
    ]
    for copy in kv_first:
        copy.start()
    hand_out(1)
    ct_copies = scatter(ct, ct_all, ct_s, ct_r)
    for h in range(head_count):
        cols = slice(h * HD, (h + 1) * HD)
        q_out[:, cols] = (head_forward(q_pre[:, cols], gq[...], cos[...], sin[...]) * (1.0 / math.sqrt(HD))).astype(BF)
    lse[...] = jnp.zeros_like(lse)
    poll(1)

    def slot_scores(slot):
        keys = slice(slot * loc, (slot + 1) * loc)
        v_t[:, keys] = kv[keys, HD:].T
        for h in range(head_count):
            grown = jnp.exp(nt(kv[keys, :HD], q_out[:, h * HD : (h + 1) * HD]) + bias[keys, :].astype(F32))
            probs[h, keys, :] = grown
            lse[h : h + 1, :] += jnp.sum(grown, axis=0, keepdims=True)

    slot_scores(0)
    poll(2)
    kv_relay = []
    for i, slot in enumerate((1, 4, 5)):
        kv_first[i].wait_recv()
        keys = pl.ds(slot * loc, loc)
        copy = remote(kv.at[keys], kv.at[pl.ds((slot + 2) * loc, loc)], kv_s.at[4 + i], kv_r.at[4 + i], pc)
        copy.start()
        kv_relay.append(copy)
        slot_scores(slot)
        poll(1)
        if i == 0:
            kv_first[3].wait_recv()
            slot_scores(2)
            poll(1)
    for i, slot in enumerate((3, 6, 7)):
        kv_relay[i].wait_recv()
        slot_scores(slot)
        poll(1)
    kv_copy = pltpu.make_async_copy(kv, kv_out, loc_s.at[4])
    kv_copy.start()
    for h in range(head_count):
        inverse = 1.0 / lse[h : h + 1, :]
        total = nn(v_t[...], (probs[h] * inverse).astype(BF))
        heads[:, h * HD : (h + 1) * HD] = total.T.astype(BF)
        poll(1)
    lse[...] = jnp.log(lse[...])
    pass_on(1)
    poll(1)
    settled(1)
    wa_copy = pltpu.make_async_copy(wa, wa_out, loc_s.at[5])
    wa_copy.start()
    feats = wo.shape[1]
    ao[...] = nt(heads[:, :feats], wa[0, :, qkv:]) + nt(heads[:, feats:], wa[1, :, qkv:])

    def norm_rows(values, scales):
        inverse = lax.rsqrt(jnp.mean(values * values, axis=1, keepdims=True) + EPS)
        return values * inverse * (1.0 + scales)

    res[...] = inputs + norm_rows(ao[...], gains[1:2, :])
    pre[...] = norm_rows(res[...], gains[2:3, :]).astype(BF)
    ct_own.wait()
    for copy in ct_copies:
        copy.wait_recv()
    ct_out[...] = ct_all[...].T
    poll(len(events))
    arrived()
    for copy in tok_copies + gain_copies + ct_copies + kv_first:
        copy.wait_send()
    for copy in kv_relay + list(passed.values()) + list(attn_copies.values()):
        copy.wait_send()
    bias_copy.wait()
    kv_copy.wait()
    wa_copy.wait()


def attention_front(*args):
    tok, _, gain_block, wq, wk, wv, wo, wg = args[:8]
    cut, tok_count = tok.shape
    members = 8
    width, loc = cut * members, tok_count // members
    depth, hidden = wg.shape
    slab = -(-hidden // (2 * TILE)) * TILE
    feats = wq.shape[1] + wk.shape[1] + wv.shape[1] + wo.shape[1]
    q_width = 2 * wq.shape[1]
    dma = pltpu.SemaphoreType.DMA
    struct = jax.ShapeDtypeStruct
    smem = pl.BlockSpec(memory_space=pltpu.SMEM)
    return pl.pallas_call(
        front_kernel,
        out_shape=(
            struct((3, width, slab), BF),
            struct((2, width, feats), BF),
            struct((tok_count, 2 * HD), BF),
            struct((tok_count, loc), BF),
            struct((loc, width), BF),
            struct((loc, width), BF),
            struct((8, width), F32),
            struct((loc, q_width), F32),
            struct((loc, HD), F32),
            struct((q_width // HD, loc), F32),
            struct((loc, HD // 2), F32),
            struct((loc, HD // 2), F32),
            struct((loc, q_width), BF),
            struct((loc, width), F32),
            struct((loc, width), F32),
            struct((loc, width), BF),
        ),
        in_specs=[any_spec()] * 10 + [vmem_spec()] * 2 + [smem] * 2,
        out_specs=[any_spec()] * 4 + [vmem_spec()] * 12,
        scratch_shapes=[
            pltpu.VMEM((3, depth, 2 * slab), BF),
            pltpu.VMEM((2, width, feats), BF),
            pltpu.VMEM((width, loc), BF),
            pltpu.VMEM((width, loc), BF),
            pltpu.VMEM((members,) + gain_block.shape, F32),
            pltpu.VMEM((loc, q_width), BF),
            pltpu.VMEM((tok_count, 2 * HD), BF),
            pltpu.VMEM((HD, tok_count), BF),
            pltpu.VMEM((tok_count, loc), BF),
            pltpu.VMEM((q_width // HD, tok_count, loc), F32),
            dma((3,)), dma((4,)), dma((7,)), dma((7,)), dma((7,)), dma((7,)), dma((7,)), dma((7,)),
            dma((4, 4)), dma((4, 4)), dma((2, 3)), dma((2, 3)), dma((18,)), dma((18,)), dma((18,)), dma((18,)),
            dma((18,)), dma((18,)), dma((18,)), dma((3,)), dma((3,)), dma((7,)), dma((7,)), dma((6,)),
        ],
        compiler_params=params(1),
        name="attention_front",
    )(*args)


def mlp_kernel(
    pre, res, ct, gains, w_h,
    lo, dgpost, dpre, dparts, pre_t_out, gm_t_out, hh_out, bb_out, aa_out,
    wg, wu, wd, pre_all, pre_t, gm_all, gm_t, aa, bb, hh, acc, own, parts, prc,
    w_sem, ag_s, ag_r, rs_s, rs_r, gs_s, gs_r, st_s,
):
    place, row, col, high, core = whereabouts()
    px, py, pd, pc = peers()
    quad = (px, py, pd)
    loc, width = pre.shape
    slab = wg.shape[1]
    tiles = slab // TILE

    def store(kind, j, src, dst):
        rows = chunk_rows(j)
        return pltpu.make_async_copy(src.at[rows], dst.at[rows], st_s.at[kind, j])

    loads = [
        pltpu.make_async_copy(src, dst, w_sem.at[i])
        for i, (src, dst) in enumerate(((w_h.at[0], wg), (w_h.at[1], wu), (w_h.at[2], wd)))
    ]
    for copy in loads:
        copy.start()
    greet((px, py, pd, pc))

    def spread(src, buffer, send, recv):
        copies = [remote(src, buffer.at[i + 1], send.at[i], recv.at[i], p) for i, p in enumerate(quad)]
        for copy in copies:
            copy.start()
        return copies

    gathers = spread(pre, pre_all, ag_s, ag_r)
    pre_all[0] = pre[...]
    for copy in loads:
        copy.wait()

    def chunk_rows(j):
        return pl.ds(pl.multiple_of(j * loc, 256), loc)

    def chunk_device(j):
        return (place, (row + j // 2 * 2) % 4, (col + j) % 2)

    def give_part(j):
        return remote(parts.at[j - 1], prc.at[j - 1], rs_s.at[j - 1], rs_r.at[j - 1], chunk_device(j))

    def got_chunk(j, buffer, send, recv):
        pl.when(j > 0)(lambda: remote(pre, buffer.at[j], send.at[j - 1], recv.at[j - 1], chunk_device(j)).wait_recv())

    def forward(j, carry):
        got_chunk(j, pre_all, ag_s, ag_r)
        acc[...] = jnp.zeros_like(acc)
        rows = chunk_rows(j)
        for n in range(tiles):
            at = slice(n * TILE, (n + 1) * TILE)
            x = pre_all[j]
            gate = nn(x, wg[:, at])
            up = nn(x, wu[:, at])
            square = gate * gate
            bend = jnp.tanh(GELU_C * gate * (1.0 + 0.044715 * square))
            half = 0.5 * (1.0 + bend)
            gelu = gate * half
            slope = half + 0.5 * gate * (1.0 - bend * bend) * (GELU_C * (1.0 + 0.134145 * square))
            hidden = (gelu * up).astype(BF)
            aa[rows, at] = gelu.astype(BF)
            bb[rows, at] = (up * slope).astype(BF)
            hh[rows, at] = hidden
            acc[...] += nt(hidden, wd[:, at])
        store(0, j, hh, hh_out).start()

        @pl.when(j == 0)
        def _():
            own[...] = acc[...]

        @pl.when(j > 0)
        def _():
            parts[j - 1] = acc[...].astype(BF)
            give_part(j).start()

        return carry

    lax.fori_loop(0, 4, forward, 0)
    for j in range(4):
        pre_t[:, j * loc : (j + 1) * loc] = pre_all[j].T
    pre_copy = pltpu.make_async_copy(pre_t, pre_t_out, st_s.at[3, 0])
    pre_copy.start()
    for j in range(1, 4):
        give_part(j).wait()
    out = own[...] + prc[0].astype(F32) + prc[1].astype(F32) + prc[2].astype(F32)
    scale = 1.0 + gains[3:4, :]
    inverse = lax.rsqrt(jnp.mean(out * out, axis=1, keepdims=True) + EPS)
    lo[...] = (res[...] + out * inverse * scale).astype(BF)
    upstream = ct[...].astype(F32)
    scaled = upstream * scale
    inner = jnp.mean(scaled * out, axis=1, keepdims=True)
    gm_all[0] = (scaled * inverse - out * (inverse * inverse * inverse * inner)).astype(BF)
    dgpost[...] = jnp.sum(upstream * out * inverse, axis=0, keepdims=True)

    gathers2 = spread(gm_all.at[0], gm_all, gs_s, gs_r)
    def backward(j, carry):
        got_chunk(j, gm_all, gs_s, gs_r)
        acc[...] = jnp.zeros_like(acc)
        rows = chunk_rows(j)
        for n in range(tiles):
            at = slice(n * TILE, (n + 1) * TILE)
            grad_hidden = nn(gm_all[j], wd[:, at])
            grad_gate = (grad_hidden * bb[rows, at].astype(F32)).astype(BF)
            grad_up = (grad_hidden * aa[rows, at].astype(F32)).astype(BF)
            bb[rows, at] = grad_gate
            aa[rows, at] = grad_up
            acc[...] += nt(grad_gate, wg[:, at]) + nt(grad_up, wu[:, at])
        gm_t[:, rows] = gm_all[j].T
        store(1, j, bb, bb_out).start()
        store(2, j, aa, aa_out).start()

        @pl.when(j == 0)
        def _():
            dpre[...] = acc[...]

        @pl.when(j > 0)
        def _():
            dparts[j - 1] = acc[...].astype(BF)

        return carry

    lax.fori_loop(0, 4, backward, 0)
    gm_copy = pltpu.make_async_copy(gm_t, gm_t_out, st_s.at[3, 1])
    gm_copy.start()
    for j in range(4):
        store(0, j, hh, hh_out).wait()
        store(1, j, bb, bb_out).wait()
        store(2, j, aa, aa_out).wait()
    pre_copy.wait()
    gm_copy.wait()
    for copy in gathers + gathers2:
        copy.wait_send()


def mlp(pre, res, ct, gains, weights):
    loc, width = pre.shape
    slab = weights.shape[2]
    dma = pltpu.SemaphoreType.DMA
    struct = jax.ShapeDtypeStruct
    return pl.pallas_call(
        mlp_kernel,
        out_shape=(
            struct((loc, width), BF),
            struct((1, width), F32),
            struct((loc, width), F32),
            struct((3, loc, width), BF),
            struct((width, 4 * loc), BF),
            struct((width, 4 * loc), BF),
            struct((4 * loc, slab), BF),
            struct((4 * loc, slab), BF),
            struct((4 * loc, slab), BF),
        ),
        in_specs=[vmem_spec()] * 4 + [any_spec()],
        out_specs=[vmem_spec()] * 4 + [any_spec()] * 5,
        scratch_shapes=[
            pltpu.VMEM((width, slab), BF),
            pltpu.VMEM((width, slab), BF),
            pltpu.VMEM((width, slab), BF),
            pltpu.VMEM((4, loc, width), BF),
            pltpu.VMEM((width, 4 * loc), BF),
            pltpu.VMEM((4, loc, width), BF),
            pltpu.VMEM((width, 4 * loc), BF),
            pltpu.VMEM((4 * loc, slab), BF),
            pltpu.VMEM((4 * loc, slab), BF),
            pltpu.VMEM((4 * loc, slab), BF),
            pltpu.VMEM((loc, width), F32),
            pltpu.VMEM((loc, width), F32),
            pltpu.VMEM((3, loc, width), BF),
            pltpu.VMEM((3, loc, width), BF),
            dma((3,)),
            dma((3,)), dma((3,)), dma((3,)), dma((3,)), dma((3,)), dma((3,)), dma((4, 4)),
        ],
        compiler_params=params(3),
        name="feed_forward",
    )(pre, res, ct, gains, weights)


class Line:
    def __init__(self, mine, inbox, middle, turned, out, sems, turns):
        self.mine, self.inbox, self.middle, self.turned, self.out = mine, inbox, middle, turned, out
        self.in_s, self.in_r, self.mid_s, self.mid_r, self.x_s, self.x_r, self.o_s, self.o_r, self.l_s, self.y_s, self.y_r = sems
        place, row, col, high, core = whereabouts()
        self.turns = turns
        self.end = (place % 3) == 0
        self.inner = (jnp.where(place == 0, 1, 2), row, col)
        self.outer = ((place - 1) * 3 % 6, row, col)
        self.across = (3 - place, row, col)
        self.beside = (place, row + 2 - 4 * high, col)
        self.place = place

    def root(self, k):
        return (k + self.place + 1) % 2

    def inward(self, k, h):
        return remote(self.mine.at[k, h], self.inbox.at[k, h], self.in_s.at[k, h], self.in_r.at[k, h], self.inner)

    def partial(self, k):
        return remote(
            self.mine.at[k, 1 - self.root(k)], self.middle.at[k], self.mid_s.at[k], self.mid_r.at[k], self.across
        )

    def turn(self, k):
        return remote(self.mine.at[k, 1], self.turned.at[k // 2], self.y_s.at[k], self.y_r.at[k], self.beside)

    def spot(self, k, h):
        return self.out(k, h) if isinstance(k, int) else self.mine.at[k, h]

    def exchange(self, k, h, source):
        return remote(source, self.spot(k, h), self.x_s.at[k], self.x_r.at[k], self.across)

    def outward(self, k, h, source):
        return remote(source, self.spot(k, h), self.o_s.at[k, h], self.o_r.at[k, h], self.outer)

    def keep(self, k, h, source):
        return pltpu.make_async_copy(source, self.spot(k, h), self.l_s.at[k])

    def inside(self, act):
        pl.when(jnp.logical_not(self.end))(act)

    def turns_here(self, k):
        return jnp.logical_and(k < self.turns, self.root(k) == 1)

    def send(self, k):
        @pl.when(self.end)
        def _():
            for h in range(2):
                self.inward(k, h).start()

    def sent(self, k):
        @pl.when(self.end)
        def _():
            for h in range(2):
                self.inward(k, h).wait_send()

    def add(self, k):
        def act():
            other = 1 - self.root(k)
            self.inward(k, other).wait_recv()
            self.mine[k, other] = (
                self.mine[k, other].astype(F32) + self.inbox[k, other].astype(F32)
            ).astype(BF)
            self.partial(k).start()

        self.inside(act)

    def share(self, k, h, source):
        self.outward(k, h, source).start()
        self.exchange(k, h, source).start()
        self.keep(k, h, source).start()

    def total(self, k):
        def act():
            root = self.root(k)
            self.inward(k, root).wait_recv()
            self.partial(k).wait_recv()
            self.mine[k, root] = (
                self.mine[k, root].astype(F32) + self.inbox[k, root].astype(F32) + self.middle[k].astype(F32)
            ).astype(BF)

            if isinstance(k, int) and k >= self.turns:
                self.share(k, root, self.mine.at[k, root])
                return

            @pl.when(self.turns_here(k))
            def _():
                self.turn(k).start()

            @pl.when(jnp.logical_not(self.turns_here(k)))
            def _():
                self.share(k, root, self.mine.at[k, root])

        self.inside(act)

    def spread(self, k):
        @pl.when(jnp.logical_and(jnp.logical_not(self.end), self.turns_here(k)))
        def _():
            self.turn(k).wait_recv()
            self.share(k, 1, self.turned.at[k // 2])

    def forward(self, k, late):
        def act():
            other = 1 - self.root(k)
            source = self.out(k, other)
            self.exchange(k, other, self.mine.at[k, other]).wait_recv()
            self.outward(k, other, source).start()

        if k >= self.turns:
            if not late:
                self.inside(act)
        else:
            pl.when(jnp.logical_and(jnp.logical_not(self.end), self.root(k) == (0 if late else 1)))(act)

    def drain(self, k):
        @pl.when(self.end)
        def _():
            for h in range(2):
                self.outward(k, h, self.mine.at[k, h]).wait_recv()

        def act():
            root = self.root(k)
            self.partial(k).wait_send()
            self.exchange(k, root, self.mine.at[k, root]).wait_send()
            self.keep(k, root, self.mine.at[k, root]).wait()
            for h in range(2):
                self.outward(k, h, self.mine.at[k, h]).wait_send()

            if not isinstance(k, int):
                pl.when(self.turns_here(k))(lambda: self.turn(k).wait_send())

        self.inside(act)


class Alone:
    def __init__(self, mine, inbox, middle, turned, out, sems, turns):
        self.mine, self.out, self.turns = mine, out, turns
        self.l_s, self.y_s, self.y_r = sems[0], sems[9], sems[10]
        place, row, col, high, core = whereabouts()
        self.beside = (place, row + 2 - 4 * high, col)

    def send(self, k):
        pass

    def sent(self, k):
        pass

    def add(self, k):
        pass

    def spread(self, k):
        pass

    def forward(self, k, late):
        pass

    def copy(self, k, h):
        spot = self.out(k, h) if isinstance(k, int) else self.mine.at[k, h]
        return pltpu.make_async_copy(self.mine.at[k, h], spot, self.l_s.at[k, h])

    def turn(self, k):
        spot = self.out(k, 0) if isinstance(k, int) else self.mine.at[k, 1]
        return remote(self.mine.at[k, 1], spot, self.y_s.at[k], self.y_r.at[k], self.beside)

    def total(self, k):
        self.copy(k, 0).start()
        if isinstance(k, int):
            (self.turn(k) if k < self.turns else self.copy(k, 1)).start()
        else:
            pl.when(k < self.turns)(lambda: self.turn(k).start())
            pl.when(k >= self.turns)(lambda: self.copy(k, 1).start())

    def drain(self, k):
        self.copy(k, 0).wait()
        if isinstance(k, int):
            (self.turn(k) if k < self.turns else self.copy(k, 1)).wait()
        else:
            pl.when(k < self.turns)(lambda: self.turn(k).wait())
            pl.when(k >= self.turns)(lambda: self.copy(k, 1).wait())


def line_sems(count):
    dma = pltpu.SemaphoreType.DMA
    return [
        dma((count, 2)), dma((count, 2)), dma((count,)), dma((count,)), dma((count,)), dma((count,)),
        dma((count, 2)), dma((count, 2)), dma((count,)), dma((count,)), dma((count,)),
    ]


EARLY, AHEAD, SPREAD, LATE = 5, 3, 4, 6


def back_kernel(
    dparts, pre_t_h, gm_t_h, hh_h, bb_h, aa_h, own_h, lo_h, ao_h, ct_h, x_h, heads_h, q_pre_h, k_pre_h, kv_h,
    bias_h, wa_h, gains, gq, gk, lse, cos, sin, dgpost,
    gate_out, up_out, down_out, a_out, lo_out, gt_out, gain_out,
    mine, inbox, middle, turned, a_mine, a_in, a_mid, parts, cr, summed, qr, rsr, lefts, ring, halves,
    own, ga, ao, ct, x, heads, q_pre, k_pre, kv, bias,
    k_t, gh, dk, dv, kv_cr, kv_qr, dh, cut_t, gain_buf, gain_in,
    in_s, t_s, big_s, wa_l, rs_s, rs_r, c_s, c_r, kc_s, kc_r, kq_s, kq_r, pc_s, pc_r, pq_s, pq_r,
    lo_s, lo_r, gt_s, gt_r, gn_s, gn_r, loc_s, *line_refs,
):
    place, row, col, high, core = whereabouts()
    me = 2 * row + col
    px, py, pd, pc = peers()
    quad = (px, py, pd)
    others = sent_to_all(me)
    on_line = lax.axis_size("dp") == 4
    make = Line if on_line else Alone
    hidden_pairs = mine.shape[0] - 2
    slab = gate_out.shape[1] // 2

    def place_of(k, h):
        if k >= hidden_pairs:
            return a_out.at[:, pl.ds((0 if k > hidden_pairs else qkv) + h * TILE, TILE)]
        start = (high + h) % 2 * slab + k // 3 * TILE
        return (gate_out, up_out, down_out)[k % 3].at[:, pl.ds(pl.multiple_of(start, TILE), TILE)]

    def place_of_small(k, h):
        return a_out.at[pl.ds(h * (depth // 2), depth // 2), pl.ds(qkv - TILE, TILE)]

    line = make(mine, inbox, middle, turned, place_of, line_refs[:11], hidden_pairs)
    small = make(a_mine, a_in, a_mid, turned, place_of_small, line_refs[11:], 0)
    tiles = hidden_pairs // 3
    pairs = mine.shape[0]
    loc, width = x.shape
    depth = mine.shape[2]
    cut = width // 8
    all_tok = pre_t_h.shape[1]
    head_count = q_pre.shape[1] // HD
    half = HD // 2
    out_half = heads.shape[1] // 2
    feats = parts.shape[2]
    qkv = feats - out_half

    big = [
        pltpu.make_async_copy(src, lefts.at[i], big_s.at[i]) for i, src in enumerate((pre_t_h, gm_t_h))
    ]
    sources = (bb_h, aa_h, hh_h)

    def lanes(index):
        return pl.ds(pl.multiple_of(index * TILE, TILE), TILE)

    def load(n, m):
        return pltpu.make_async_copy(sources[m].at[:, lanes(n)], ring.at[m], t_s.at[m])

    for m in range(3):
        load(0, m).start()
        if m < 2:
            big[m].start()
    whole_wa = pltpu.make_async_copy(wa_h, parts, wa_l)
    smalls = [
        pltpu.make_async_copy(src, dst, in_s.at[i])
        for i, (src, dst) in enumerate(
            (
                (lo_h, ga), (own_h, own), (ao_h, ao), (ct_h, ct), (heads_h, heads),
                (kv_h, kv), (bias_h, bias), (q_pre_h, q_pre), (k_pre_h, k_pre), (x_h, x),
            )
        )
    ]
    for copy in smalls + [whole_wa]:
        copy.start()
    friends = [device for _, device in others]
    if on_line:
        friends += [((place + i) % 4, row, col) for i in range(1, 4)]
    greet(friends)
    scatters = [remote(dparts.at[i], rsr.at[i], rs_s.at[i], rs_r.at[i], device) for i, device in enumerate(quad)]
    for copy in scatters:
        copy.start()

    def to_core(k, m):
        return (
            remote(halves.at[m, 2 * high + 1 - core], mine.at[k, 0], c_s.at[m, 0], c_r.at[k, 0], pc),
            remote(halves.at[m, 3 - 2 * high - core], mine.at[k, 1], c_s.at[m, 1], c_r.at[k, 1], pc),
        )

    def produce(n):
        for m in range(3):
            load(n, m).wait()

        def one(m, carry):
            product = nn(lefts[m // 2], ring[m]).astype(BF)
            for b in range(4):
                halves[m, b] = product[b * depth : (b + 1) * depth]
            for copy in to_core(3 * n + m, m):
                copy.start()
            return carry

        lax.fori_loop(0, 3, one, 0)
        if n + 1 < tiles:
            for m in range(3):
                load(n + 1, m).start()

    def settle(n):
        def one(m, carry):
            k = 3 * n + m
            for copy in to_core(k, m):
                copy.wait()
            mine[k, 0] = (mine[k, 0].astype(F32) + halves[m, 2 * high + core].astype(F32)).astype(BF)
            mine[k, 1] = (mine[k, 1].astype(F32) + halves[m, 2 - 2 * high + core].astype(F32)).astype(BF)
            return carry

        lax.fori_loop(0, 3, one, 0)

    order = list(range(14)) + [hidden_pairs] + list(range(14, 18)) + [hidden_pairs + 1] + list(range(18, hidden_pairs))

    def line_rest(p):
        if 0 <= p - 1 < pairs:
            line.total(order[p - 1])
        if 0 <= p - SPREAD < pairs and order[p - SPREAD] < hidden_pairs:
            line.spread(order[p - SPREAD])
        if 0 <= p - 3 < pairs:
            line.forward(order[p - 3], False)
        if 0 <= p - LATE < pairs:
            line.forward(order[p - LATE], True)

    def line_step(p):
        line.sent(order[p])
        if p + AHEAD < pairs:
            line.send(order[p + AHEAD])
        elif p + AHEAD == pairs:
            small.send(0)
        line.add(order[p])
        line_rest(p)

    for copy in big:
        copy.wait()
    produce(0)
    for n in range(1, EARLY):
        settle(n - 1)
        for i in range(3 * n - 3, min(3 * n, AHEAD)):
            line.send(i)
        produce(n)
        if n >= EARLY - 2:
            line_step(n + 2 - EARLY)

    here = pl.ds(pl.multiple_of(me * loc, 128), loc)

    def give(src, dst, send, recv, local):
        copies = [
            remote(src.at[pl.ds(i * cut, cut)], dst.at[:, here], send.at[j], recv.at[j], d)
            for j, (i, d) in enumerate(others)
        ]
        for copy in copies:
            copy.start()
        stays = pltpu.make_async_copy(src.at[pl.ds(me * cut, cut)], dst.at[:, here], local)
        stays.start()
        return copies, stays

    def norm_grad(values, scales, upstream):
        inverse = lax.rsqrt(jnp.mean(values * values, axis=1, keepdims=True) + EPS)
        scaled = upstream * (1.0 + scales)
        inner = jnp.mean(scaled * values, axis=1, keepdims=True)
        grad = scaled * inverse - values * (inverse * inverse * inverse * inner)
        return grad, jnp.sum(upstream * values * inverse, axis=0, keepdims=True)

    smalls[0].wait()
    cut_t[...] = ga[...].T
    lo_copies, lo_own = give(cut_t, lo_out, lo_s, lo_r, loc_s.at[0])
    gain_buf[...] = jnp.zeros_like(gain_buf)
    for copy in smalls[1:] + [whole_wa]:
        copy.wait()
    k_t[...] = kv[:, :HD].T
    settle(EARLY - 1)
    produce(EARLY)
    line_step(2)
    for copy in scatters:
        copy.wait()
    grad_pre = own[...] + rsr[0].astype(F32) + rsr[1].astype(F32) + rsr[2].astype(F32)
    inverse = lax.rsqrt(jnp.mean(ao[...] * ao[...], axis=1, keepdims=True) + EPS)
    residual = x[...].astype(F32) + ao[...] * inverse * (1.0 + gains[1:2, :])
    grad, gain_buf[0, 2:3, :] = norm_grad(residual, gains[2:3, :], grad_pre)
    own[...] = grad + ct[...].astype(F32)
    grad, gain_buf[0, 1:2, :] = norm_grad(ao[...], gains[1:2, :], own[...])
    ga[...] = grad.astype(BF)
    gain_buf[0, 3:4, :] = dgpost[...]
    for j in range(2):
        gh[:, j * out_half : (j + 1) * out_half] = nn(ga[...], parts[j, :, qkv:]).astype(BF)
    line_step(3)

    wanted = ((1 - col, 1 - high, pd), (1 - col, high, px), (col, 1 - high, py), (col, high, None))

    def block(ref, index, columns):
        return ref.at[pl.ds(pl.multiple_of(index * depth, 16), depth), columns]

    class PlaneSum:
        def __init__(self, which, start, size):
            self.columns = pl.ds(start, size)
            self.core = [
                remote(
                    block(parts.at[c2], 2 * y2 + 1 - core, self.columns),
                    block(cr, 2 * c2 + y2, self.columns),
                    pc_s.at[which, i],
                    pc_r.at[which, 2 * c2 + y2],
                    pc,
                )
                for i, (c2, y2, _) in enumerate(wanted)
            ]
            self.sends = [
                remote(block(summed, i, self.columns), qr.at[i, :, self.columns], pq_s.at[which, i], pq_r.at[which, i], d)
                for i, (_, _, d) in enumerate(wanted[:3])
            ]

        def begin(self):
            for copy in self.core:
                copy.start()

        def added(self, i):
            c2, y2, _ = wanted[i]
            self.core[i].wait_recv()
            return block(parts.at[c2], 2 * y2 + core, self.columns)[...].astype(F32) + block(
                cr, 2 * c2 + y2, self.columns
            )[...].astype(F32)

        def spread(self):
            for i in range(3):
                block(summed, i, self.columns)[...] = self.added(i).astype(BF)
                self.sends[i].start()

        def result(self):
            total = self.added(3)
            for i in range(3):
                self.sends[i].wait()
                total = total + qr[i, :, self.columns].astype(F32)
            for copy in self.core:
                copy.wait_send()
            return total.astype(BF)

    ga_t = ga[...].T
    for j in range(2):
        for n in range(out_half // TILE):
            parts[j, :, qkv + n * TILE : qkv + (n + 1) * TILE] = nn(
                ga_t, heads[:, j * out_half + n * TILE : j * out_half + (n + 1) * TILE]
            ).astype(BF)
    out_sum = PlaneSum(0, qkv, out_half)
    out_sum.begin()
    line_step(4)

    step_keys = 512
    for h in range(head_count):
        cols = slice(h * HD, (h + 1) * HD)
        query = head_forward(q_pre[:, cols], gq[...], cos[...], sin[...]) * (1.0 / math.sqrt(HD))
        query, grad_head = query.astype(BF), gh[:, cols]
        delta = jnp.sum((grad_head.astype(F32) * heads[:, cols].astype(F32)).T, axis=0, keepdims=True)

        def keys(c, total, h=h, query=query, grad_head=grad_head, delta=delta):
            rows = pl.ds(pl.multiple_of(c * step_keys, step_keys), step_keys)
            scores = nt(kv[rows, :HD], query) + bias[rows, :].astype(F32)
            probs = jnp.exp(scores - lse[h : h + 1, :])
            grad_probs = nt(kv[rows, HD:], grad_head)
            grad_scores = (probs * (grad_probs - delta)).astype(BF)
            add_v = nn(probs.astype(BF), grad_head)
            add_k = nn(grad_scores, query)
            if h:
                dv[rows, :] += add_v
                dk[rows, :] += add_k
            else:
                dv[rows, :] = add_v
                dk[rows, :] = add_k
            return total + nn(k_t[:, rows], grad_scores)

        total = lax.fori_loop(0, kv.shape[0] // step_keys, keys, jnp.zeros((HD, loc), F32))
        grad_query = total.T * (1.0 / math.sqrt(HD))
        first, second = grad_query[:, :half], grad_query[:, half:]
        turned = jnp.concatenate(
            [first * cos[...] + second * sin[...], second * cos[...] - first * sin[...]], axis=1
        )
        grad, gain = norm_grad(q_pre[:, cols], gq[...], turned)
        gain_buf[0, 4:5, :HD] += gain
        dh[h // 2, :, (h % 2) * HD : (h % 2 + 1) * HD] = grad.astype(BF)
        if h == 0:
            out_sum.spread()
        if h % 2:
            line_step(3 + 2 * (h // 2 + 1))
            line_step(4 + 2 * (h // 2 + 1))

    stage = [rsr.at[i // 2, :, pl.ds(i % 2 * 2 * HD, 2 * HD)] for i in range(4)]
    for i, slot in enumerate(KV_SLOTS):
        rows = slice((slot + 2) * loc, (slot + 3) * loc)
        stage[i][:, :HD] = dk[rows, :].astype(BF)
        stage[i][:, HD:] = dv[rows, :].astype(BF)
    kv_core = [remote(stage[i], kv_cr.at[i], kc_s.at[i], kc_r.at[i], pc) for i in range(4)]
    for copy in kv_core:
        copy.start()
    inputs = x[...].astype(F32)
    inverse = lax.rsqrt(jnp.mean(inputs * inputs, axis=1, keepdims=True) + EPS)
    normed_t = (inputs * inverse * (1.0 + gains[0:1, :])).astype(BF).T
    feat_q = dh.shape[2] - HD
    ao[...] = nt(dh[0, :, :feat_q], parts[0, :, :feat_q]) + nt(dh[1, :, :feat_q], parts[1, :, :feat_q])
    kv_sums = (ct.at[:, pl.ds(0, 2 * HD)], ct.at[:, pl.ds(2 * HD, 2 * HD)], rsr.at[2, :, pl.ds(0, 2 * HD)])
    kv_sends = []
    for i, device in ((3, pd), (1, px), (2, py)):
        kv_core[i].wait_recv()
        rows = slice(KV_SLOTS[i] * loc, (KV_SLOTS[i] + 1) * loc)
        kv_sums[i - 1][:, :HD] = (dk[rows, :] + kv_cr[i, :, :HD].astype(F32)).astype(BF)
        kv_sums[i - 1][:, HD:] = (dv[rows, :] + kv_cr[i, :, HD:].astype(F32)).astype(BF)
        copy = remote(kv_sums[i - 1], kv_qr.at[i - 1], kq_s.at[i - 1], kq_r.at[i - 1], device)
        copy.start()
        kv_sends.append(copy)
    kv_core[0].wait_recv()
    for j in range(2):
        for n in range(feat_q // TILE):
            parts[j, :, n * TILE : (n + 1) * TILE] = nn(normed_t, dh[j, :, n * TILE : (n + 1) * TILE]).astype(BF)
    query_sum = PlaneSum(1, 0, feat_q)
    query_sum.begin()
    settle(EARLY)
    produce(EARLY + 1)
    query_sum.spread()
    line_step(9)
    line_step(10)
    total = out_sum.result()
    for i in range(2):
        mine[hidden_pairs, i] = total[:, i * TILE : (i + 1) * TILE]
    for copy in kv_sends:
        copy.wait()
    got = kv_qr[0].astype(F32) + kv_qr[1].astype(F32) + kv_qr[2].astype(F32) + kv_cr[0].astype(F32)
    grad_key = dk[:loc, :] + got[:, :HD]
    grad_value = dv[:loc, :] + got[:, HD:]
    first, second = grad_key[:, :half], grad_key[:, half:]
    turned_key = jnp.concatenate(
        [first * cos[...] + second * sin[...], second * cos[...] - first * sin[...]], axis=1
    )
    grad, gain_buf[0, 5:6, :HD] = norm_grad(k_pre[...], gk[...], turned_key)
    for j in range(2):
        dh[j, :, feat_q : feat_q + half] = grad[:, j * half : (j + 1) * half].astype(BF)
        dh[j, :, feat_q + half :] = grad_value[:, j * half : (j + 1) * half].astype(BF)
    ao[...] += nt(dh[0, :, feat_q:], parts[0, :, feat_q:qkv]) + nt(dh[1, :, feat_q:], parts[1, :, feat_q:qkv])
    for j in range(2):
        parts[j, :, feat_q:qkv] = nn(normed_t, dh[j, :, feat_q:]).astype(BF)
    key_sum = PlaneSum(2, feat_q, HD)
    key_sum.begin()
    grad, gain_buf[0, 0:1, :] = norm_grad(x[...].astype(F32), gains[0:1, :], ao[...])
    key_sum.spread()
    for copy in lo_copies:
        copy.wait_send()
    lo_own.wait()
    cut_t[...] = (grad + own[...]).astype(BF).T
    gt_copies, gt_own = give(cut_t, gt_out, gt_s, gt_r, loc_s.at[1])
    gain_copies = [
        remote(gain_buf.at[0], gain_in.at[j], gn_s.at[j], gn_r.at[j], d) for j, (_, d) in enumerate(others)
    ]
    for copy in gain_copies:
        copy.start()
    settle(EARLY + 1)
    line_step(11)
    line_step(12)
    line_step(13)
    total = query_sum.result()
    for i in range(2):
        mine[hidden_pairs + 1, i] = total[:, i * TILE : (i + 1) * TILE]
    line_step(14)
    line_step(15)
    total = key_sum.result()
    for i in range(2):
        a_mine[0, i] = total[i * depth // 2 : (i + 1) * depth // 2]
    for copy in gain_copies:
        copy.wait()
    gain_buf[1] = gain_buf[0] + sum(gain_in[j] for j in range(7))
    gain_copies = [
        remote(gain_buf.at[1], gain_in.at[7 + i], gn_s.at[7 + i], gn_r.at[7 + i], ((place + i + 1) % 4, row, col))
        for i in range(3 if on_line else 0)
    ]
    for copy in gain_copies:
        copy.start()

    for p in range(16, pairs):
        line_step(p)
    small.sent(0)
    small.add(0)
    line_rest(pairs)
    small.total(0)
    for p in range(pairs + 1, pairs + 4):
        line_rest(p)
    small.forward(0, False)
    for p in range(pairs + 4, pairs + LATE):
        line_rest(p)

    def drain(k, carry):
        line.drain(k)
        return carry

    lax.fori_loop(0, pairs, drain, 0)
    small.drain(0)
    for copy in gain_copies:
        copy.wait()
    gain_out[...] = gain_buf[1]
    for i in range(len(gain_copies)):
        gain_out[...] += gain_in[7 + i]
    for copy in lo_copies:
        copy.wait_recv()
    for copy in gt_copies:
        copy.wait()
    gt_own.wait()
    for copy in kv_core:
        copy.wait_send()


def attention_back(*args):
    dparts, pre_t, hh, lo, heads, q_pre, kv, bias, wa = (args[i] for i in (0, 1, 3, 7, 11, 12, 14, 15, 16))
    loc, width = lo.shape
    depth, feats = width // 4, wa.shape[2]
    hidden_pairs = 3 * hh.shape[1] // TILE
    pairs = hidden_pairs + 2
    keys = kv.shape[0]
    cut = width // 8
    dma = pltpu.SemaphoreType.DMA
    piece = (depth, TILE)
    rest = (depth // 2, TILE)
    struct = jax.ShapeDtypeStruct
    vmem = pltpu.VMEM
    return pl.pallas_call(
        back_kernel,
        out_shape=(
            struct((depth, 2 * hh.shape[1]), BF),
            struct((depth, 2 * hh.shape[1]), BF),
            struct((depth, 2 * hh.shape[1]), BF),
            struct((depth, feats), BF),
            struct((cut, keys), BF),
            struct((cut, keys), BF),
            struct((8, width), F32),
        ),
        in_specs=[any_spec()] * 17 + [vmem_spec()] * 7,
        out_specs=[any_spec()] * 6 + [vmem_spec()],
        scratch_shapes=[
            vmem((pairs, 2) + piece, BF),
            vmem((pairs, 2) + piece, BF),
            vmem((pairs,) + piece, BF),
            vmem(((hidden_pairs + 1) // 2,) + piece, BF),
            vmem((1, 2) + rest, BF),
            vmem((1, 2) + rest, BF),
            vmem((1,) + rest, BF),
            vmem((2, width, feats), BF),
            vmem((width, feats), BF),
            vmem((3 * depth, feats), BF),
            vmem((3, depth, feats), BF),
            vmem(dparts.shape, BF),
            vmem((2,) + pre_t.shape, BF),
            vmem((3, pre_t.shape[1], TILE), BF),
            vmem((3, 4) + piece, BF),
        ]
        + [vmem(args[i].shape, args[i].dtype) for i in (6, 7, 8, 9, 10, 11, 12, 13, 14, 15)]
        + [
            vmem((HD, keys), BF),
            vmem(heads.shape, BF),
            vmem((keys, HD), F32),
            vmem((keys, HD), F32),
            vmem((4, loc, 2 * HD), BF),
            vmem((3, loc, 2 * HD), BF),
            vmem((2, loc, feats - heads.shape[1] // 2), BF),
            vmem((width, loc), BF),
            vmem((2, 8, width), F32),
            vmem((10, 8, width), F32),
            dma((12,)), dma((3,)), dma((2,)), dma(()), dma((3,)), dma((3,)), dma((3, 2)), dma((hidden_pairs, 2)),
            dma((4,)), dma((4,)), dma((3,)), dma((3,)),
            dma((3, 4)), dma((3, 4)), dma((3, 3)), dma((3, 3)),
            dma((7,)), dma((7,)), dma((7,)), dma((7,)), dma((10,)), dma((10,)), dma((2,)),
        ]
        + line_sems(pairs)
        + line_sems(1),
        compiler_params=params(6),
        name="attention_back",
    )(*args)


def finish_kernel(gate_in, up_in, down_in, attn_in, tok_in, gate, up, down, wq, wk, wv, wo, tok):
    for src, dst in ((gate_in, gate), (up_in, up), (down_in, down)):
        dst[...] = src[:, : dst.shape[1]].astype(F32)
    at = 0
    for dst in (wq, wk, wv, wo):
        dst[...] = attn_in[:, at : at + dst.shape[1]].astype(F32)
        at += dst.shape[1]
    tok[...] = tok_in[...].astype(F32)


def finish(gate, up, down, attn, tok, hidden, widths):
    depth, cut = gate.shape[0], tok.shape[0]
    steps = cut // 16
    outs = [(depth, hidden)] * 3 + [(depth, width) for width in widths] + [tok.shape]

    def rows(shape):
        return pl.BlockSpec((shape[0] // steps, shape[1]), lambda i: (i, 0))

    return pl.pallas_call(
        finish_kernel,
        grid=(steps,),
        in_specs=[rows(array.shape) for array in (gate, up, down, attn, tok)],
        out_specs=[rows(shape) for shape in outs],
        out_shape=[jax.ShapeDtypeStruct(shape, F32) for shape in outs],
        compiler_params=pltpu.CompilerParams(vmem_limit_bytes=VMEM_LIMIT),
        name="finish",
    )(gate, up, down, attn, tok)


def body(
    tokens,
    cotangent,
    weight_query,
    weight_key,
    weight_value,
    weight_out,
    weight_gate,
    weight_up,
    weight_down,
    gain_input,
    gain_attn,
    gain_pre,
    gain_post,
    gain_query,
    gain_key,
    doc_lengths,
    block_size,
):
    cut = tokens.shape[1]
    row, col = lax.axis_index("row"), lax.axis_index("col")
    me = row * lax.axis_size("col") + col
    depth, hidden_half = weight_gate.shape
    q_half, kv_half = weight_query.shape[1], weight_key.shape[1]
    gain_block = jnp.pad(jnp.stack([gain_input, gain_attn, gain_pre, gain_post]), ((0, 4), (0, 0)))
    (
        w_hidden, w_attn, kv_all, bias, inputs, upstream, gains, query_pre, key_pre, log_total,
        cos_table, sin_table, head_bf, attn_out, residual, pre_normed,
    ) = attention_front(
        tokens.T, cotangent.T, gain_block, weight_query, weight_key, weight_value, weight_out.T,
        weight_gate, weight_up, weight_down.T, gain_query[None], gain_key[None], doc_lengths, block_size,
    )
    layer_rows, grad_g_post, grad_own, grad_parts, pre_t, grad_mlp_t, hidden, grad_gate, grad_up = mlp(
        pre_normed, residual, upstream, gains, w_hidden
    )
    sum_gate, sum_up, sum_down, attn_sum, layer_cut, token_cut, gain_sums = attention_back(
        grad_parts, pre_t, grad_mlp_t, hidden, grad_gate, grad_up, grad_own, layer_rows, attn_out, upstream,
        inputs, head_bf, query_pre, key_pre, kv_all, bias, w_attn, gains, gain_query[None], gain_key[None],
        log_total, cos_table, sin_table, grad_g_post,
    )
    if lax.axis_size("dp") != 4:
        sum_gate, sum_up, sum_down, attn_sum, gain_sums = (
            lax.psum(v.astype(F32), "dp") for v in (sum_gate, sum_up, sum_down, attn_sum, gain_sums)
        )
    grad_gate, grad_up, grad_down, grad_query, grad_key, grad_value, grad_out, grad_tokens = finish(
        sum_gate, sum_up, sum_down, attn_sum, token_cut, hidden_half, (q_half, kv_half, kv_half, q_half)
    )
    my_gains = lax.dynamic_slice_in_dim(gain_sums[:4], me * cut, cut, 1)
    return (
        layer_cut.T,
        grad_tokens.T,
        grad_query,
        grad_key,
        grad_value,
        grad_out.T,
        grad_gate,
        grad_up,
        grad_down.T,
        my_gains[0],
        my_gains[1],
        my_gains[2],
        my_gains[3],
        gain_sums[4, :HD],
        gain_sums[5, :HD],
    )


def solution(mesh):
    in_specs = (
        P("dp", ("row", "col")),
        P("dp", ("row", "col")),
        P("row", "col"),
        P("row", "col"),
        P("row", "col"),
        P("col", "row"),
        P("row", "col"),
        P("row", "col"),
        P("col", "row"),
        P(("row", "col")),
        P(("row", "col")),
        P(("row", "col")),
        P(("row", "col")),
        P(),
        P(),
        P("dp", None),
        P(),
    )
    out_specs = (
        P("dp", ("row", "col")),
        P("dp", ("row", "col")),
        P("row", "col"),
        P("row", "col"),
        P("row", "col"),
        P("col", "row"),
        P("row", "col"),
        P("row", "col"),
        P("col", "row"),
        P(("row", "col")),
        P(("row", "col")),
        P(("row", "col")),
        P(("row", "col")),
        P(),
        P(),
    )
    return jax.shard_map(body, mesh=mesh, in_specs=in_specs, out_specs=out_specs, check_vma=False)
```

```python
import functools
import math

import jax
import jax.numpy as jnp
from jax import lax
from jax.experimental import pallas as pl
from jax.experimental.pallas import tpu as pltpu
from jax.sharding import PartitionSpec as P

HD = 256
EPS = 1e-06
ROPE_BASE = 1000000.0
GELU_C = 0.7978845608028654
BF = jnp.bfloat16
F32 = jnp.float32
PLANE = ("row", "col")


def dot(left, right, dims):
    return lax.dot_general(left, right, (dims, ((), ())), preferred_element_type=F32)


def nn(left, right):
    return dot(left, right, ((1,), (0,)))


def nt(left, right):
    return dot(left, right, ((1,), (1,)))


def tn(left, right):
    return dot(left, right, ((0,), (0,)))


MESH = pl.DeviceIdType.MESH
TILE = 256
KV_SLOTS = (0, 1, 4, 5)
LEAD = 4
VMEM_LIMIT = 64 * 1024 * 1024 - 512 * 1024


def whereabouts():
    place, row, col = lax.axis_index("dp"), lax.axis_index("row"), lax.axis_index("col")
    return place, row, col, row // 2, row % 2


def peers():
    place, row, col, high, core = whereabouts()
    far = row + 2 - 4 * high
    return (
        (place, row, 1 - col),
        (place, far, col),
        (place, far, 1 - col),
        (place, row + 1 - 2 * core, col),
    )


def remote(src, dst, send, recv, device):
    return pltpu.make_async_remote_copy(
        src_ref=src, dst_ref=dst, send_sem=send, recv_sem=recv, device_id=device, device_id_type=MESH
    )


def greet(devices):
    barrier = pltpu.get_barrier_semaphore()
    for device in devices:
        pl.semaphore_signal(barrier, inc=1, device_id=device, device_id_type=MESH)
    pl.semaphore_wait(barrier, len(devices))


def any_spec():
    return pl.BlockSpec(memory_space=pl.ANY)


def vmem_spec():
    return pl.BlockSpec(memory_space=pltpu.VMEM)


def params(number):
    return pltpu.CompilerParams(
        collective_id=number, has_side_effects=True, vmem_limit_bytes=VMEM_LIMIT
    )


def token_places(lengths, span, tokens):
    inverse = 1.0 / jnp.full((1, 1), span[0], jnp.int32).astype(F32)
    document = jnp.zeros_like(tokens)
    first = jnp.zeros_like(tokens)
    end = jnp.int32(0)
    for i in range(lengths.shape[1]):
        end = end + lengths[0, i]
        past = tokens >= end
        document = jnp.where(past, i + 1, document)
        first = jnp.where(past, end, first)
    position = (tokens - first).astype(F32)
    return document, jnp.floor((position + 0.5) * inverse), position


def mask_bias(lengths, span, bias, me, slots):
    local = bias.shape[1]
    query_doc, query_block, _ = token_places(
        lengths, span, me * local + lax.broadcasted_iota(jnp.int32, (1, local), 1)
    )
    for s, owner in enumerate(slots):
        key_doc, key_block, _ = token_places(
            lengths, span, owner * local + lax.broadcasted_iota(jnp.int32, (local, 1), 0)
        )
        seen = (key_doc == query_doc) & (key_block <= query_block)
        bias[s * local : (s + 1) * local, :] = jnp.where(seen, 0.0, -1e30).astype(BF)


def slot_owners():
    place, row, col, high, core = whereabouts()
    owners = []
    for s in range(8):
        r2 = (high + s // 4) % 2 * 2 + (core + s // 2) % 2
        owners.append(2 * r2 + (col + s) % 2)
    return owners


def sent_to_all(index):
    place, row, col, high, core = whereabouts()
    others = []
    for s in range(1, 8):
        r2, c2 = (high + s // 4) % 2 * 2 + (core + s // 2) % 2, (col + s) % 2
        others.append((2 * r2 + c2, (place, r2, c2)))
    return others


def head_forward(values, scales, cos, sin):
    half = values.shape[1] // 2
    inverse = lax.rsqrt(jnp.mean(values * values, axis=1, keepdims=True) + EPS)
    scaled = values * inverse * (1.0 + scales)
    first, second = scaled[:, :half], scaled[:, half:]
    return jnp.concatenate([first * cos - second * sin, second * cos + first * sin], axis=1)


def front_kernel(
    tok, ct, gain_block, wq, wk, wv, wo, wg, wu, wd, gq, gk, lengths, span,
    wm_out, wa_out, kv_out, bias_out, x_out, ct_out, gains, q_pre, k_pre, lse, cos, sin, heads, ao, res, pre,
    wm, wa, tok_all, ct_all, gain_all, q_out, kv, v_t, bias, probs,
    wm_l, wa_l, tk_s, tk_r, ct_s, ct_r, gn_s, gn_r, wa_s, wa_r, wb_s, wb_r, wy_s, wy_r, wu_s, wd_s, wz_r, wc_s, wc_r, wo_s, wo_r, kv_s, kv_r, loc_s,
):
    place, row, col, high, core = whereabouts()
    me = 2 * row + col
    px, py, pd, pc = peers()
    others = sent_to_all(me)
    depth, hidden = wg.shape
    slab = wm_out.shape[2]
    cut = tok.shape[0]
    loc = x_out.shape[0]
    head_count = heads.shape[1] // HD
    half = HD // 2
    members = len(others) + 1
    share = lax.axis_size("dp") == 4
    far_row = row + 2 - 4 * high
    friends = [device for _, device in others]
    if share:
        friends += [((place + i) % 4, row, col) for i in range(1, 4)]

    loads = [
        pltpu.make_async_copy(src, wm.at[m, :, pl.ds(0, hidden)], wm_l.at[m]) for m, src in enumerate((wg, wu, wd))
    ]
    rows = pl.ds(row * depth, depth)
    far_rows = pl.ds(far_row * depth, depth)
    spots, at = [], 0
    for src in (wq, wk, wv, wo):
        spots.append(pl.ds(at, src.shape[1]))
        at += src.shape[1]
    qkv = at - wo.shape[1]
    own = [
        pltpu.make_async_copy(src, wa.at[col, rows, spot], wa_l.at[i])
        for i, (src, spot) in enumerate(zip((wq, wk, wv, wo), spots))
    ]
    tok_own = pltpu.make_async_copy(
        tok.at[:, pl.ds(pl.multiple_of(me * loc, 128), loc)], tok_all.at[pl.ds(me * cut, cut)], loc_s.at[0]
    )
    ct_own = pltpu.make_async_copy(
        ct.at[:, pl.ds(pl.multiple_of(me * loc, 128), loc)], ct_all.at[pl.ds(me * cut, cut)], loc_s.at[1]
    )
    gain_own = pltpu.make_async_copy(gain_block, gain_all.at[me], loc_s.at[2])
    for copy in [tok_own, gain_own] + own + [ct_own] + loads:
        copy.start()
    greet(friends)

    def scatter(src, dst, send, recv):
        copies = [
            remote(
                src.at[:, pl.ds(pl.multiple_of(index * loc, 128), loc)],
                dst.at[pl.ds(me * cut, cut)],
                send.at[j],
                recv.at[j],
                device,
            )
            for j, (index, device) in enumerate(others)
        ]
        for copy in copies:
            copy.start()
        return copies

    tok_copies = scatter(tok, tok_all, tk_s, tk_r)
    gain_copies = [
        remote(gain_block, gain_all.at[me], gn_s.at[j], gn_r.at[j], device) for j, (_, device) in enumerate(others)
    ]
    for copy in gain_copies:
        copy.start()
    attn_copies = {}

    def hand_out(which):
        for i in ((0, 1, 2), (3,))[which]:
            for j, device in enumerate((px, py, pd, pc)):
                attn_copies[i, j] = remote(
                    (wq, wk, wv, wo)[i], wa.at[col, rows, spots[i]], wa_s.at[i, j], wa_r.at[i, j], device
                )
                attn_copies[i, j].start()

    for copy in loads:
        copy.wait()
    for m in range(3):
        wm[m, :, hidden:] = jnp.zeros((depth, 2 * slab - hidden), BF)
    mine = pl.ds(pl.multiple_of(high * slab, 128), slab)
    away = pl.ds(pl.multiple_of((1 - high) * slab, 128), slab)
    unit = depth // 6
    groups, rounds = 18, 4

    def group(start, g):
        return g // 6, pl.ds(pl.multiple_of(start + g % 6 * unit, 16), unit)

    def over(g):
        m, at = group(0, g)
        return remote(wm.at[m, at, away], wm_out.at[group(row * depth, g)], wy_s.at[g], wy_r.at[g], py)

    def along(g, step):
        spot = wm_out.at[group(far_row * depth, g)]
        return remote(spot, spot, (wu_s if step > 0 else wd_s).at[g], wz_r.at[g], ((place + step) % 4, row, col))

    def between(g):
        spot = wm_out.at[group(far_row * depth, g)]
        return remote(spot, spot, wc_s.at[g], wc_r.at[g], pc)

    own_hidden = [pltpu.make_async_copy(wm.at[m, :, mine], wm_out.at[m, rows], wm_l.at[m]) for m in range(3)]
    beside = [remote(wm.at[m, :, mine], wm_out.at[m, rows], wo_s.at[m], wo_r.at[m], pc) for m in range(3)]
    extra = 16 + place % 2
    for m in range(3):
        own_hidden[m].start()
        beside[m].start()
    fetched = [rounds * r + place for r in range(rounds)] + [extra] if share else list(range(groups))
    for g in fetched[:rounds]:
        over(g).start()
    hand_out(0)
    for g in fetched[rounds:]:
        over(g).start()

    def travel(distance, r, act_up, act_down):
        if distance == 0:
            g = rounds * r + place
            pl.when(place < 3)(lambda: act_up(g))
            pl.when(place > 0)(lambda: act_down(g))
        else:
            below, above = rounds * r + place - distance, rounds * r + place + distance
            pl.when(jnp.logical_and(place >= distance, place < 3))(lambda: act_up(below))
            pl.when(jnp.logical_and(place + distance <= 3, place > 0))(lambda: act_down(above))

    def arrive(distance, r):
        if distance == 0:
            g = rounds * r + place
            over(g).wait_recv()
            between(g).start()
        else:
            for g, there in (
                (rounds * r + place - distance, place >= distance),
                (rounds * r + place + distance, place + distance <= 3),
            ):

                @pl.when(there)
                def _(g=g):
                    along(g, 1).wait_recv()
                    between(g).start()

        travel(distance, r, lambda g: along(g, 1).start(), lambda g: along(g, -1).start())

    def arrive_extra():
        over(extra).wait_recv()
        between(extra).start()
        pl.when(place % 2 == 0)(lambda: along(extra, 1).start())
        pl.when(place % 2 == 1)(lambda: along(extra, -1).start())

    def arrive_whole():
        for g in fetched:
            over(g).wait_recv()
            between(g).start()

    if share:
        events = [
            functools.partial(arrive, distance, r)
            for distance, r in (
                (0, 0), (0, 1), (0, 2), (1, 0), (0, 3), (1, 1), (2, 0), (1, 2), (2, 1), (3, 0), (1, 3), (2, 2), (3, 1),
                (2, 3), (3, 2), (3, 3),
            )
        ]
        events.insert(7, arrive_extra)
    else:
        events = [arrive_whole]

    def poll(count):
        for _ in range(min(count, len(events))):
            events.pop(0)()

    def arrived():
        if share:
            other = 33 - extra
            along(other, 1).wait_recv()
            between(other).start()
            pl.when(place % 2 == 0)(lambda: along(extra, 1).wait_send())
            pl.when(place % 2 == 1)(lambda: along(extra, -1).wait_send())
            for distance in range(4):
                for r in range(rounds):
                    travel(distance, r, lambda g: along(g, 1).wait_send(), lambda g: along(g, -1).wait_send())
        for g in fetched:
            over(g).wait_send()
        for g in range(groups):
            between(g).wait()
        for m in range(3):
            beside[m].wait()
            own_hidden[m].wait()

    doc, _, position = token_places(lengths, span, me * loc + lax.broadcasted_iota(jnp.int32, (loc, 1), 0))
    steps = lax.broadcasted_iota(jnp.int32, (1, half), 1).astype(F32)
    phases = position * jnp.exp(steps * (-2.0 * math.log(ROPE_BASE) / HD))
    cos[...] = jnp.cos(phases)
    sin[...] = jnp.sin(phases)
    mask_bias(lengths, span, bias, me, slot_owners())
    bias_copy = pltpu.make_async_copy(bias, bias_out, loc_s.at[3])
    bias_copy.start()

    tok_own.wait()
    gain_own.wait()
    for copy in tok_copies + gain_copies:
        copy.wait_recv()
    for f in range(members):
        gains[:, f * cut : (f + 1) * cut] = gain_all[f]
    x_out[...] = tok_all[...].T
    inputs = x_out[...].astype(F32)
    inverse = lax.rsqrt(jnp.mean(inputs * inputs, axis=1, keepdims=True) + EPS)
    normed = (inputs * inverse * (1.0 + gains[0:1, :])).astype(BF)

    corners = ((row, 1 - col), (far_row, col), (far_row, 1 - col))
    part_spots = (pl.ds(0, qkv), pl.ds(qkv, wo.shape[1]))
    passed = {}

    def pass_on(which):
        for j, (r2, c2) in enumerate(corners):
            for i in ((0, 1, 2), (3,))[which]:
                attn_copies[i, j].wait_recv()
            slot = wa.at[c2, pl.ds(r2 * depth, depth), part_spots[which]]
            passed[which, j] = remote(slot, slot, wb_s.at[which, j], wb_r.at[which, j], pc)
            passed[which, j].start()

    def settled(which):
        for i in ((0, 1, 2), (3,))[which]:
            own[i].wait()
            attn_copies[i, 3].wait_recv()
        for j in range(3):
            passed[which, j].wait_recv()

    poll(5)
    pass_on(0)
    poll(1)
    settled(0)
    poll(1)
    q_half, kv_half = wq.shape[1], wk.shape[1]
    for j in range(2):
        found = nn(normed, wa[j, :, q_half:qkv])
        k_pre[:, j * kv_half : (j + 1) * kv_half] = found[:, :kv_half]
        kv[:loc, HD + j * kv_half : HD + (j + 1) * kv_half] = found[:, kv_half:].astype(BF)
    kv[:loc, :HD] = head_forward(k_pre[...], gk[...], cos[...], sin[...]).astype(BF)
    kv_first = [
        remote(kv.at[pl.ds(0, loc)], kv.at[pl.ds(slot * loc, loc)], kv_s.at[i], kv_r.at[i], device)
        for i, (slot, device) in enumerate(((1, px), (4, py), (5, pd), (2, pc)))
    ]
    for copy in kv_first:
        copy.start()
    hand_out(1)
    for j in range(2):
        q_pre[:, j * q_half : (j + 1) * q_half] = nn(normed, wa[j, :, :q_half])
    ct_copies = scatter(ct, ct_all, ct_s, ct_r)
    for h in range(head_count):
        cols = slice(h * HD, (h + 1) * HD)
        q_out[:, cols] = (head_forward(q_pre[:, cols], gq[...], cos[...], sin[...]) * (1.0 / math.sqrt(HD))).astype(BF)
    lse[...] = jnp.zeros_like(lse)
    poll(1)

    def slot_scores(slot):
        keys = slice(slot * loc, (slot + 1) * loc)
        v_t[:, keys] = kv[keys, HD:].T
        for h in range(head_count):
            grown = jnp.exp(nt(kv[keys, :HD], q_out[:, h * HD : (h + 1) * HD]) + bias[keys, :].astype(F32))
            probs[h, keys, :] = grown
            lse[h : h + 1, :] += jnp.sum(grown, axis=0, keepdims=True)

    slot_scores(0)
    poll(2)
    kv_relay = []
    for i, slot in enumerate((1, 4, 5)):
        kv_first[i].wait_recv()
        keys = pl.ds(slot * loc, loc)
        copy = remote(kv.at[keys], kv.at[pl.ds((slot + 2) * loc, loc)], kv_s.at[4 + i], kv_r.at[4 + i], pc)
        copy.start()
        kv_relay.append(copy)
        slot_scores(slot)
        poll(1)
        if i == 0:
            kv_first[3].wait_recv()
            slot_scores(2)
            poll(1)
    for i, slot in enumerate((3, 6, 7)):
        kv_relay[i].wait_recv()
        slot_scores(slot)
        poll(1)
    kv_copy = pltpu.make_async_copy(kv, kv_out, loc_s.at[4])
    kv_copy.start()
    for h in range(head_count):
        inverse = 1.0 / lse[h : h + 1, :]
        total = nn(v_t[...], (probs[h] * inverse).astype(BF))
        heads[:, h * HD : (h + 1) * HD] = total.T.astype(BF)
        poll(1)
    lse[...] = jnp.log(lse[...])
    pass_on(1)
    poll(1)
    settled(1)
    wa_copy = pltpu.make_async_copy(wa, wa_out, loc_s.at[5])
    wa_copy.start()
    feats = wo.shape[1]
    ao[...] = nt(heads[:, :feats], wa[0, :, qkv:]) + nt(heads[:, feats:], wa[1, :, qkv:])

    def norm_rows(values, scales):
        inverse = lax.rsqrt(jnp.mean(values * values, axis=1, keepdims=True) + EPS)
        return values * inverse * (1.0 + scales)

    res[...] = inputs + norm_rows(ao[...], gains[1:2, :])
    pre[...] = norm_rows(res[...], gains[2:3, :]).astype(BF)
    ct_own.wait()
    for copy in ct_copies:
        copy.wait_recv()
    ct_out[...] = ct_all[...].T
    poll(len(events))
    arrived()
    for copy in tok_copies + gain_copies + ct_copies + kv_first:
        copy.wait_send()
    for copy in kv_relay + list(passed.values()) + list(attn_copies.values()):
        copy.wait_send()
    bias_copy.wait()
    kv_copy.wait()
    wa_copy.wait()


def attention_front(*args):
    tok, _, gain_block, wq, wk, wv, wo, wg = args[:8]
    cut, tok_count = tok.shape
    members = 8
    width, loc = cut * members, tok_count // members
    depth, hidden = wg.shape
    slab = -(-hidden // (2 * TILE)) * TILE
    feats = wq.shape[1] + wk.shape[1] + wv.shape[1] + wo.shape[1]
    q_width = 2 * wq.shape[1]
    dma = pltpu.SemaphoreType.DMA
    struct = jax.ShapeDtypeStruct
    smem = pl.BlockSpec(memory_space=pltpu.SMEM)
    return pl.pallas_call(
        front_kernel,
        out_shape=(
            struct((3, width, slab), BF),
            struct((2, width, feats), BF),
            struct((tok_count, 2 * HD), BF),
            struct((tok_count, loc), BF),
            struct((loc, width), BF),
            struct((loc, width), BF),
            struct((8, width), F32),
            struct((loc, q_width), F32),
            struct((loc, HD), F32),
            struct((q_width // HD, loc), F32),
            struct((loc, HD // 2), F32),
            struct((loc, HD // 2), F32),
            struct((loc, q_width), BF),
            struct((loc, width), F32),
            struct((loc, width), F32),
            struct((loc, width), BF),
        ),
        in_specs=[any_spec()] * 10 + [vmem_spec()] * 2 + [smem] * 2,
        out_specs=[any_spec()] * 4 + [vmem_spec()] * 12,
        scratch_shapes=[
            pltpu.VMEM((3, depth, 2 * slab), BF),
            pltpu.VMEM((2, width, feats), BF),
            pltpu.VMEM((width, loc), BF),
            pltpu.VMEM((width, loc), BF),
            pltpu.VMEM((members,) + gain_block.shape, F32),
            pltpu.VMEM((loc, q_width), BF),
            pltpu.VMEM((tok_count, 2 * HD), BF),
            pltpu.VMEM((HD, tok_count), BF),
            pltpu.VMEM((tok_count, loc), BF),
            pltpu.VMEM((q_width // HD, tok_count, loc), F32),
            dma((3,)), dma((4,)), dma((7,)), dma((7,)), dma((7,)), dma((7,)), dma((7,)), dma((7,)),
            dma((4, 4)), dma((4, 4)), dma((2, 3)), dma((2, 3)), dma((18,)), dma((18,)), dma((18,)), dma((18,)),
            dma((18,)), dma((18,)), dma((18,)), dma((3,)), dma((3,)), dma((7,)), dma((7,)), dma((6,)),
        ],
        compiler_params=params(1),
        name="attention_front",
    )(*args)


def mlp_kernel(
    pre, res, ct, gains, w_h,
    lo, dgpost, dpre, dparts, pre_t_out, gm_t_out, hh_out, bb_out, aa_out,
    wg, wu, wd, pre_all, pre_t, gm_all, gm_t, aa, bb, hh, acc, own, parts, prc,
    w_sem, ag_s, ag_r, rs_s, rs_r, gs_s, gs_r, st_s,
):
    place, row, col, high, core = whereabouts()
    px, py, pd, pc = peers()
    quad = (px, py, pd)
    loc, width = pre.shape
    slab = wg.shape[1]
    tiles = slab // TILE

    def store(kind, j, src, dst):
        rows = chunk_rows(j)
        return pltpu.make_async_copy(src.at[rows], dst.at[rows], st_s.at[kind, j])

    loads = [
        pltpu.make_async_copy(src, dst, w_sem.at[i])
        for i, (src, dst) in enumerate(((w_h.at[0], wg), (w_h.at[1], wu), (w_h.at[2], wd)))
    ]
    for copy in loads:
        copy.start()
    greet((px, py, pd, pc))

    def spread(src, buffer, send, recv):
        copies = [remote(src, buffer.at[i + 1], send.at[i], recv.at[i], p) for i, p in enumerate(quad)]
        for copy in copies:
            copy.start()
        return copies

    gathers = spread(pre, pre_all, ag_s, ag_r)
    pre_all[0] = pre[...]
    for copy in loads:
        copy.wait()

    def chunk_rows(j):
        return pl.ds(pl.multiple_of(j * loc, 256), loc)

    def chunk_device(j):
        return (place, (row + j // 2 * 2) % 4, (col + j) % 2)

    def give_part(j):
        return remote(parts.at[j - 1], prc.at[j - 1], rs_s.at[j - 1], rs_r.at[j - 1], chunk_device(j))

    def got_chunk(j, buffer, send, recv):
        pl.when(j > 0)(lambda: remote(pre, buffer.at[j], send.at[j - 1], recv.at[j - 1], chunk_device(j)).wait_recv())

    def forward(j, carry):
        got_chunk(j, pre_all, ag_s, ag_r)
        rows = chunk_rows(j)
        for n in range(tiles):
            at = slice(n * TILE, (n + 1) * TILE)
            x = pre_all[j]
            gate = nn(x, wg[:, at])
            up = nn(x, wu[:, at])
            square = gate * gate
            bend = jnp.tanh(GELU_C * gate * (1.0 + 0.044715 * square))
            half = 0.5 * (1.0 + bend)
            gelu = gate * half
            slope = half + 0.5 * gate * (1.0 - bend * bend) * (GELU_C * (1.0 + 0.134145 * square))
            hidden = (gelu * up).astype(BF)
            aa[rows, at] = gelu.astype(BF)
            bb[rows, at] = (up * slope).astype(BF)
            hh[rows, at] = hidden
        acc[...] = nt(hh[rows, :], wd[...])
        store(0, j, hh, hh_out).start()

        @pl.when(j == 0)
        def _():
            own[...] = acc[...]

        @pl.when(j > 0)
        def _():
            parts[j - 1] = acc[...].astype(BF)
            give_part(j).start()

        return carry

    lax.fori_loop(0, 4, forward, 0)
    for j in range(4):
        pre_t[:, j * loc : (j + 1) * loc] = pre_all[j].T
    pre_copy = pltpu.make_async_copy(pre_t, pre_t_out, st_s.at[3, 0])
    pre_copy.start()
    for j in range(1, 4):
        give_part(j).wait()
    out = own[...] + prc[0].astype(F32) + prc[1].astype(F32) + prc[2].astype(F32)
    scale = 1.0 + gains[3:4, :]
    inverse = lax.rsqrt(jnp.mean(out * out, axis=1, keepdims=True) + EPS)
    lo[...] = (res[...] + out * inverse * scale).astype(BF)
    upstream = ct[...].astype(F32)
    scaled = upstream * scale
    inner = jnp.mean(scaled * out, axis=1, keepdims=True)
    gm_all[0] = (scaled * inverse - out * (inverse * inverse * inverse * inner)).astype(BF)
    dgpost[...] = jnp.sum(upstream * out * inverse, axis=0, keepdims=True)

    gathers2 = spread(gm_all.at[0], gm_all, gs_s, gs_r)
    def backward(j, carry):
        got_chunk(j, gm_all, gs_s, gs_r)
        rows = chunk_rows(j)
        for n in range(tiles):
            at = slice(n * TILE, (n + 1) * TILE)
            grad_hidden = nn(gm_all[j], wd[:, at])
            grad_gate = (grad_hidden * bb[rows, at].astype(F32)).astype(BF)
            grad_up = (grad_hidden * aa[rows, at].astype(F32)).astype(BF)
            bb[rows, at] = grad_gate
            aa[rows, at] = grad_up
        acc[...] = nt(bb[rows, :], wg[...]) + nt(aa[rows, :], wu[...])
        gm_t[:, rows] = gm_all[j].T
        store(1, j, bb, bb_out).start()
        store(2, j, aa, aa_out).start()

        @pl.when(j == 0)
        def _():
            dpre[...] = acc[...]

        @pl.when(j > 0)
        def _():
            dparts[j - 1] = acc[...].astype(BF)

        return carry

    lax.fori_loop(0, 4, backward, 0)
    gm_copy = pltpu.make_async_copy(gm_t, gm_t_out, st_s.at[3, 1])
    gm_copy.start()
    for j in range(4):
        store(0, j, hh, hh_out).wait()
        store(1, j, bb, bb_out).wait()
        store(2, j, aa, aa_out).wait()
    pre_copy.wait()
    gm_copy.wait()
    for copy in gathers + gathers2:
        copy.wait_send()


def mlp(pre, res, ct, gains, weights):
    loc, width = pre.shape
    slab = weights.shape[2]
    dma = pltpu.SemaphoreType.DMA
    struct = jax.ShapeDtypeStruct
    return pl.pallas_call(
        mlp_kernel,
        out_shape=(
            struct((loc, width), BF),
            struct((1, width), F32),
            struct((loc, width), F32),
            struct((3, loc, width), BF),
            struct((width, 4 * loc), BF),
            struct((width, 4 * loc), BF),
            struct((4 * loc, slab), BF),
            struct((4 * loc, slab), BF),
            struct((4 * loc, slab), BF),
        ),
        in_specs=[vmem_spec()] * 4 + [any_spec()],
        out_specs=[vmem_spec()] * 4 + [any_spec()] * 5,
        scratch_shapes=[
            pltpu.VMEM((width, slab), BF),
            pltpu.VMEM((width, slab), BF),
            pltpu.VMEM((width, slab), BF),
            pltpu.VMEM((4, loc, width), BF),
            pltpu.VMEM((width, 4 * loc), BF),
            pltpu.VMEM((4, loc, width), BF),
            pltpu.VMEM((width, 4 * loc), BF),
            pltpu.VMEM((4 * loc, slab), BF),
            pltpu.VMEM((4 * loc, slab), BF),
            pltpu.VMEM((4 * loc, slab), BF),
            pltpu.VMEM((loc, width), F32),
            pltpu.VMEM((loc, width), F32),
            pltpu.VMEM((3, loc, width), BF),
            pltpu.VMEM((3, loc, width), BF),
            dma((3,)),
            dma((3,)), dma((3,)), dma((3,)), dma((3,)), dma((3,)), dma((3,)), dma((4, 4)),
        ],
        compiler_params=params(3),
        name="feed_forward",
    )(pre, res, ct, gains, weights)


class Line:
    def __init__(self, mine, inbox, middle, turned, out, sems, turns):
        self.mine, self.inbox, self.middle, self.turned, self.out = mine, inbox, middle, turned, out
        self.in_s, self.in_r, self.mid_s, self.mid_r, self.x_s, self.x_r, self.o_s, self.o_r, self.l_s, self.y_s, self.y_r = sems
        place, row, col, high, core = whereabouts()
        self.turns = turns
        self.end = (place % 3) == 0
        self.inner = (jnp.where(place == 0, 1, 2), row, col)
        self.outer = ((place - 1) * 3 % 6, row, col)
        self.across = (3 - place, row, col)
        self.beside = (place, row + 2 - 4 * high, col)
        self.place = place

    def root(self, k):
        return (k + self.place + 1) % 2

    def inward(self, k, h):
        return remote(self.mine.at[k, h], self.inbox.at[k, h], self.in_s.at[k, h], self.in_r.at[k, h], self.inner)

    def partial(self, k):
        return remote(
            self.mine.at[k, 1 - self.root(k)], self.middle.at[k], self.mid_s.at[k], self.mid_r.at[k], self.across
        )

    def turn(self, k):
        return remote(self.mine.at[k, 1], self.turned.at[k // 2], self.y_s.at[k], self.y_r.at[k], self.beside)

    def spot(self, k, h):
        return self.out(k, h) if isinstance(k, int) else self.mine.at[k, h]

    def exchange(self, k, h, source):
        return remote(source, self.spot(k, h), self.x_s.at[k], self.x_r.at[k], self.across)

    def outward(self, k, h, source):
        return remote(source, self.spot(k, h), self.o_s.at[k, h], self.o_r.at[k, h], self.outer)

    def keep(self, k, h, source):
        return pltpu.make_async_copy(source, self.spot(k, h), self.l_s.at[k])

    def inside(self, act):
        pl.when(jnp.logical_not(self.end))(act)

    def turns_here(self, k):
        return jnp.logical_and(k < self.turns, self.root(k) == 1)

    def send(self, k):
        @pl.when(self.end)
        def _():
            for h in range(2):
                self.inward(k, h).start()

    def sent(self, k):
        @pl.when(self.end)
        def _():
            for h in range(2):
                self.inward(k, h).wait_send()

    def add(self, k):
        def act():
            other = 1 - self.root(k)
            self.inward(k, other).wait_recv()
            self.mine[k, other] = (
                self.mine[k, other].astype(F32) + self.inbox[k, other].astype(F32)
            ).astype(BF)
            self.partial(k).start()

        self.inside(act)

    def share(self, k, h, source):
        self.outward(k, h, source).start()
        self.exchange(k, h, source).start()
        self.keep(k, h, source).start()

    def total(self, k):
        def act():
            root = self.root(k)
            self.inward(k, root).wait_recv()
            self.partial(k).wait_recv()
            self.mine[k, root] = (
                self.mine[k, root].astype(F32) + self.inbox[k, root].astype(F32) + self.middle[k].astype(F32)
            ).astype(BF)

            if isinstance(k, int) and k >= self.turns:
                self.share(k, root, self.mine.at[k, root])
                return

            @pl.when(self.turns_here(k))
            def _():
                self.turn(k).start()

            @pl.when(jnp.logical_not(self.turns_here(k)))
            def _():
                self.share(k, root, self.mine.at[k, root])

        self.inside(act)

    def spread(self, k):
        @pl.when(jnp.logical_and(jnp.logical_not(self.end), self.turns_here(k)))
        def _():
            self.turn(k).wait_recv()
            self.share(k, 1, self.turned.at[k // 2])

    def forward(self, k, late):
        def act():
            other = 1 - self.root(k)
            source = self.out(k, other)
            self.exchange(k, other, self.mine.at[k, other]).wait_recv()
            self.outward(k, other, source).start()

        if k >= self.turns:
            if not late:
                self.inside(act)
        else:
            pl.when(jnp.logical_and(jnp.logical_not(self.end), self.root(k) == (0 if late else 1)))(act)

    def drain(self, k):
        @pl.when(self.end)
        def _():
            for h in range(2):
                self.outward(k, h, self.mine.at[k, h]).wait_recv()

        def act():
            root = self.root(k)
            self.partial(k).wait_send()
            self.exchange(k, root, self.mine.at[k, root]).wait_send()
            self.keep(k, root, self.mine.at[k, root]).wait()
            for h in range(2):
                self.outward(k, h, self.mine.at[k, h]).wait_send()

            if not isinstance(k, int):
                pl.when(self.turns_here(k))(lambda: self.turn(k).wait_send())

        self.inside(act)


class Alone:
    def __init__(self, mine, inbox, middle, turned, out, sems, turns):
        self.mine, self.out, self.turns = mine, out, turns
        self.l_s, self.y_s, self.y_r = sems[0], sems[9], sems[10]
        place, row, col, high, core = whereabouts()
        self.beside = (place, row + 2 - 4 * high, col)

    def send(self, k):
        pass

    def sent(self, k):
        pass

    def add(self, k):
        pass

    def spread(self, k):
        pass

    def forward(self, k, late):
        pass

    def copy(self, k, h):
        spot = self.out(k, h) if isinstance(k, int) else self.mine.at[k, h]
        return pltpu.make_async_copy(self.mine.at[k, h], spot, self.l_s.at[k, h])

    def turn(self, k):
        spot = self.out(k, 0) if isinstance(k, int) else self.mine.at[k, 1]
        return remote(self.mine.at[k, 1], spot, self.y_s.at[k], self.y_r.at[k], self.beside)

    def total(self, k):
        self.copy(k, 0).start()
        if isinstance(k, int):
            (self.turn(k) if k < self.turns else self.copy(k, 1)).start()
        else:
            pl.when(k < self.turns)(lambda: self.turn(k).start())
            pl.when(k >= self.turns)(lambda: self.copy(k, 1).start())

    def drain(self, k):
        self.copy(k, 0).wait()
        if isinstance(k, int):
            (self.turn(k) if k < self.turns else self.copy(k, 1)).wait()
        else:
            pl.when(k < self.turns)(lambda: self.turn(k).wait())
            pl.when(k >= self.turns)(lambda: self.copy(k, 1).wait())


def line_sems(count):
    dma = pltpu.SemaphoreType.DMA
    return [
        dma((count, 2)), dma((count, 2)), dma((count,)), dma((count,)), dma((count,)), dma((count,)),
        dma((count, 2)), dma((count, 2)), dma((count,)), dma((count,)), dma((count,)),
    ]


EARLY, AHEAD, SPREAD, LATE = 5, 3, 4, 6


def back_kernel(
    dparts, pre_t_h, gm_t_h, hh_h, bb_h, aa_h, own_h, lo_h, ao_h, ct_h, x_h, heads_h, q_pre_h, k_pre_h, kv_h,
    bias_h, wa_h, gains, gq, gk, lse, cos, sin, dgpost,
    gate_out, up_out, down_out, a_out, lo_out, gt_out, gain_out,
    mine, inbox, middle, turned, a_mine, a_in, a_mid, parts, cr, summed, qr, rsr, lefts, ring, halves,
    own, ga, ao, ct, x, heads, q_pre, k_pre, kv, bias,
    k_t, gh, dk, dv, kv_cr, kv_qr, dh, cut_t, gain_buf, gain_in,
    in_s, t_s, big_s, wa_l, rs_s, rs_r, c_s, c_r, kc_s, kc_r, kq_s, kq_r, pc_s, pc_r, pq_s, pq_r,
    lo_s, lo_r, gt_s, gt_r, gn_s, gn_r, loc_s, *line_refs,
):
    place, row, col, high, core = whereabouts()
    me = 2 * row + col
    px, py, pd, pc = peers()
    quad = (px, py, pd)
    others = sent_to_all(me)
    on_line = lax.axis_size("dp") == 4
    make = Line if on_line else Alone
    hidden_pairs = mine.shape[0] - 2
    slab = gate_out.shape[1] // 2

    def place_of(k, h):
        if k >= hidden_pairs:
            return a_out.at[:, pl.ds((0 if k > hidden_pairs else qkv) + h * TILE, TILE)]
        start = (high + h) % 2 * slab + k // 3 * TILE
        return (gate_out, up_out, down_out)[k % 3].at[:, pl.ds(pl.multiple_of(start, TILE), TILE)]

    def place_of_small(k, h):
        return a_out.at[pl.ds(h * (depth // 2), depth // 2), pl.ds(qkv - TILE, TILE)]

    line = make(mine, inbox, middle, turned, place_of, line_refs[:11], hidden_pairs)
    small = make(a_mine, a_in, a_mid, turned, place_of_small, line_refs[11:], 0)
    tiles = hidden_pairs // 3
    pairs = mine.shape[0]
    loc, width = x.shape
    depth = mine.shape[2]
    cut = width // 8
    all_tok = pre_t_h.shape[1]
    head_count = q_pre.shape[1] // HD
    half = HD // 2
    out_half = heads.shape[1] // 2
    feats = parts.shape[2]
    qkv = feats - out_half

    big = [
        pltpu.make_async_copy(src, lefts.at[i], big_s.at[i]) for i, src in enumerate((pre_t_h, gm_t_h))
    ]
    sources = (bb_h, aa_h, hh_h)

    def lanes(index):
        return pl.ds(pl.multiple_of(index * TILE, TILE), TILE)

    def load(n, m):
        return pltpu.make_async_copy(sources[m].at[:, lanes(n)], ring.at[m], t_s.at[m])

    for m in range(3):
        load(0, m).start()
        if m < 2:
            big[m].start()
    whole_wa = pltpu.make_async_copy(wa_h, parts, wa_l)
    smalls = [
        pltpu.make_async_copy(src, dst, in_s.at[i])
        for i, (src, dst) in enumerate(
            (
                (lo_h, ga), (own_h, own), (ao_h, ao), (ct_h, ct), (heads_h, heads),
                (kv_h, kv), (bias_h, bias), (q_pre_h, q_pre), (k_pre_h, k_pre), (x_h, x),
            )
        )
    ]
    for copy in smalls + [whole_wa]:
        copy.start()
    friends = [device for _, device in others]
    if on_line:
        friends += [((place + i) % 4, row, col) for i in range(1, 4)]
    greet(friends)
    scatters = [remote(dparts.at[i], rsr.at[i], rs_s.at[i], rs_r.at[i], device) for i, device in enumerate(quad)]
    for copy in scatters:
        copy.start()

    def to_core(k, m):
        return (
            remote(halves.at[m, 2 * high + 1 - core], mine.at[k, 0], c_s.at[m, 0], c_r.at[k, 0], pc),
            remote(halves.at[m, 3 - 2 * high - core], mine.at[k, 1], c_s.at[m, 1], c_r.at[k, 1], pc),
        )

    def produce(n):
        for m in range(3):
            load(n, m).wait()

        def one(m, carry):
            product = nn(lefts[m // 2], ring[m]).astype(BF)
            for b in range(4):
                halves[m, b] = product[b * depth : (b + 1) * depth]
            for copy in to_core(3 * n + m, m):
                copy.start()
            return carry

        lax.fori_loop(0, 3, one, 0)
        if n + 1 < tiles:
            for m in range(3):
                load(n + 1, m).start()

    def settle(n):
        def one(m, carry):
            k = 3 * n + m
            for copy in to_core(k, m):
                copy.wait()
            mine[k, 0] = (mine[k, 0].astype(F32) + halves[m, 2 * high + core].astype(F32)).astype(BF)
            mine[k, 1] = (mine[k, 1].astype(F32) + halves[m, 2 - 2 * high + core].astype(F32)).astype(BF)
            return carry

        lax.fori_loop(0, 3, one, 0)

    order = list(range(14)) + [hidden_pairs] + list(range(14, 18)) + [hidden_pairs + 1] + list(range(18, hidden_pairs))

    def line_rest(p):
        if 0 <= p - 1 < pairs:
            line.total(order[p - 1])
        if 0 <= p - SPREAD < pairs and order[p - SPREAD] < hidden_pairs:
            line.spread(order[p - SPREAD])
        if 0 <= p - 3 < pairs:
            line.forward(order[p - 3], False)
        if 0 <= p - LATE < pairs:
            line.forward(order[p - LATE], True)

    def line_step(p):
        line.sent(order[p])
        if p + AHEAD < pairs:
            line.send(order[p + AHEAD])
        elif p + AHEAD == pairs:
            small.send(0)
        line.add(order[p])
        line_rest(p)

    for copy in big:
        copy.wait()
    produce(0)
    for n in range(1, EARLY):
        settle(n - 1)
        for i in range(3 * n - 3, min(3 * n, AHEAD)):
            line.send(i)
        produce(n)
        if n >= EARLY - 2:
            line_step(n + 2 - EARLY)

    here = pl.ds(pl.multiple_of(me * loc, 128), loc)

    def give(src, dst, send, recv, local):
        copies = [
            remote(src.at[pl.ds(i * cut, cut)], dst.at[:, here], send.at[j], recv.at[j], d)
            for j, (i, d) in enumerate(others)
        ]
        for copy in copies:
            copy.start()
        stays = pltpu.make_async_copy(src.at[pl.ds(me * cut, cut)], dst.at[:, here], local)
        stays.start()
        return copies, stays

    def norm_grad(values, scales, upstream):
        inverse = lax.rsqrt(jnp.mean(values * values, axis=1, keepdims=True) + EPS)
        scaled = upstream * (1.0 + scales)
        inner = jnp.mean(scaled * values, axis=1, keepdims=True)
        grad = scaled * inverse - values * (inverse * inverse * inverse * inner)
        return grad, jnp.sum(upstream * values * inverse, axis=0, keepdims=True)

    smalls[0].wait()
    cut_t[...] = ga[...].T
    lo_copies, lo_own = give(cut_t, lo_out, lo_s, lo_r, loc_s.at[0])
    gain_buf[...] = jnp.zeros_like(gain_buf)
    for copy in smalls[1:] + [whole_wa]:
        copy.wait()
    k_t[...] = kv[:, :HD].T
    settle(EARLY - 1)
    produce(EARLY)
    line_step(2)
    for copy in scatters:
        copy.wait()
    grad_pre = own[...] + rsr[0].astype(F32) + rsr[1].astype(F32) + rsr[2].astype(F32)
    inverse = lax.rsqrt(jnp.mean(ao[...] * ao[...], axis=1, keepdims=True) + EPS)
    residual = x[...].astype(F32) + ao[...] * inverse * (1.0 + gains[1:2, :])
    grad, gain_buf[0, 2:3, :] = norm_grad(residual, gains[2:3, :], grad_pre)
    own[...] = grad + ct[...].astype(F32)
    grad, gain_buf[0, 1:2, :] = norm_grad(ao[...], gains[1:2, :], own[...])
    ga[...] = grad.astype(BF)
    gain_buf[0, 3:4, :] = dgpost[...]
    for j in range(2):
        gh[:, j * out_half : (j + 1) * out_half] = nn(ga[...], parts[j, :, qkv:]).astype(BF)
    line_step(3)

    wanted = ((1 - col, 1 - high, pd), (1 - col, high, px), (col, 1 - high, py), (col, high, None))

    def block(ref, index, columns):
        return ref.at[pl.ds(pl.multiple_of(index * depth, 16), depth), columns]

    class PlaneSum:
        def __init__(self, which, start, size):
            self.columns = pl.ds(start, size)
            self.core = [
                remote(
                    block(parts.at[c2], 2 * y2 + 1 - core, self.columns),
                    block(cr, 2 * c2 + y2, self.columns),
                    pc_s.at[which, i],
                    pc_r.at[which, 2 * c2 + y2],
                    pc,
                )
                for i, (c2, y2, _) in enumerate(wanted)
            ]
            self.sends = [
                remote(block(summed, i, self.columns), qr.at[i, :, self.columns], pq_s.at[which, i], pq_r.at[which, i], d)
                for i, (_, _, d) in enumerate(wanted[:3])
            ]

        def begin(self):
            for copy in self.core:
                copy.start()

        def added(self, i):
            c2, y2, _ = wanted[i]
            self.core[i].wait_recv()
            return block(parts.at[c2], 2 * y2 + core, self.columns)[...].astype(F32) + block(
                cr, 2 * c2 + y2, self.columns
            )[...].astype(F32)

        def spread(self):
            for i in range(3):
                block(summed, i, self.columns)[...] = self.added(i).astype(BF)
                self.sends[i].start()

        def result(self):
            total = self.added(3)
            for i in range(3):
                self.sends[i].wait()
                total = total + qr[i, :, self.columns].astype(F32)
            for copy in self.core:
                copy.wait_send()
            return total.astype(BF)

    ga_t = ga[...].T
    for j in range(2):
        for n in range(out_half // TILE):
            parts[j, :, qkv + n * TILE : qkv + (n + 1) * TILE] = nn(
                ga_t, heads[:, j * out_half + n * TILE : j * out_half + (n + 1) * TILE]
            ).astype(BF)
    out_sum = PlaneSum(0, qkv, out_half)
    out_sum.begin()
    line_step(4)

    step_keys = 512
    for h in range(head_count):
        cols = slice(h * HD, (h + 1) * HD)
        query = head_forward(q_pre[:, cols], gq[...], cos[...], sin[...]) * (1.0 / math.sqrt(HD))
        query, grad_head = query.astype(BF), gh[:, cols]
        delta = jnp.sum((grad_head.astype(F32) * heads[:, cols].astype(F32)).T, axis=0, keepdims=True)

        def keys(c, total, h=h, query=query, grad_head=grad_head, delta=delta):
            rows = pl.ds(pl.multiple_of(c * step_keys, step_keys), step_keys)
            scores = nt(kv[rows, :HD], query) + bias[rows, :].astype(F32)
            probs = jnp.exp(scores - lse[h : h + 1, :])
            grad_probs = nt(kv[rows, HD:], grad_head)
            grad_scores = (probs * (grad_probs - delta)).astype(BF)
            add_v = nn(probs.astype(BF), grad_head)
            add_k = nn(grad_scores, query)
            if h:
                dv[rows, :] += add_v
                dk[rows, :] += add_k
            else:
                dv[rows, :] = add_v
                dk[rows, :] = add_k
            return total + nn(k_t[:, rows], grad_scores)

        total = lax.fori_loop(0, kv.shape[0] // step_keys, keys, jnp.zeros((HD, loc), F32))
        grad_query = total.T * (1.0 / math.sqrt(HD))
        first, second = grad_query[:, :half], grad_query[:, half:]
        turned = jnp.concatenate(
            [first * cos[...] + second * sin[...], second * cos[...] - first * sin[...]], axis=1
        )
        grad, gain = norm_grad(q_pre[:, cols], gq[...], turned)
        gain_buf[0, 4:5, :HD] += gain
        dh[h // 2, :, (h % 2) * HD : (h % 2 + 1) * HD] = grad.astype(BF)
        if h == 0:
            out_sum.spread()
        if h % 2:
            line_step(3 + 2 * (h // 2 + 1))
            line_step(4 + 2 * (h // 2 + 1))

    stage = [rsr.at[i // 2, :, pl.ds(i % 2 * 2 * HD, 2 * HD)] for i in range(4)]
    for i, slot in enumerate(KV_SLOTS):
        rows = slice((slot + 2) * loc, (slot + 3) * loc)
        stage[i][:, :HD] = dk[rows, :].astype(BF)
        stage[i][:, HD:] = dv[rows, :].astype(BF)
    kv_core = [remote(stage[i], kv_cr.at[i], kc_s.at[i], kc_r.at[i], pc) for i in range(4)]
    for copy in kv_core:
        copy.start()
    inputs = x[...].astype(F32)
    inverse = lax.rsqrt(jnp.mean(inputs * inputs, axis=1, keepdims=True) + EPS)
    normed_t = (inputs * inverse * (1.0 + gains[0:1, :])).astype(BF).T
    feat_q = dh.shape[2] - HD
    ao[...] = nt(dh[0, :, :feat_q], parts[0, :, :feat_q]) + nt(dh[1, :, :feat_q], parts[1, :, :feat_q])
    kv_sums = (ct.at[:, pl.ds(0, 2 * HD)], ct.at[:, pl.ds(2 * HD, 2 * HD)], rsr.at[2, :, pl.ds(0, 2 * HD)])
    kv_sends = []
    for i, device in ((3, pd), (1, px), (2, py)):
        kv_core[i].wait_recv()
        rows = slice(KV_SLOTS[i] * loc, (KV_SLOTS[i] + 1) * loc)
        kv_sums[i - 1][:, :HD] = (dk[rows, :] + kv_cr[i, :, :HD].astype(F32)).astype(BF)
        kv_sums[i - 1][:, HD:] = (dv[rows, :] + kv_cr[i, :, HD:].astype(F32)).astype(BF)
        copy = remote(kv_sums[i - 1], kv_qr.at[i - 1], kq_s.at[i - 1], kq_r.at[i - 1], device)
        copy.start()
        kv_sends.append(copy)
    kv_core[0].wait_recv()
    for j in range(2):
        for n in range(feat_q // TILE):
            parts[j, :, n * TILE : (n + 1) * TILE] = nn(normed_t, dh[j, :, n * TILE : (n + 1) * TILE]).astype(BF)
    query_sum = PlaneSum(1, 0, feat_q)
    query_sum.begin()
    settle(EARLY)
    produce(EARLY + 1)
    query_sum.spread()
    line_step(9)
    line_step(10)
    total = out_sum.result()
    for i in range(2):
        mine[hidden_pairs, i] = total[:, i * TILE : (i + 1) * TILE]
    for copy in kv_sends:
        copy.wait()
    got = kv_qr[0].astype(F32) + kv_qr[1].astype(F32) + kv_qr[2].astype(F32) + kv_cr[0].astype(F32)
    grad_key = dk[:loc, :] + got[:, :HD]
    grad_value = dv[:loc, :] + got[:, HD:]
    first, second = grad_key[:, :half], grad_key[:, half:]
    turned_key = jnp.concatenate(
        [first * cos[...] + second * sin[...], second * cos[...] - first * sin[...]], axis=1
    )
    grad, gain_buf[0, 5:6, :HD] = norm_grad(k_pre[...], gk[...], turned_key)
    for j in range(2):
        dh[j, :, feat_q : feat_q + half] = grad[:, j * half : (j + 1) * half].astype(BF)
        dh[j, :, feat_q + half :] = grad_value[:, j * half : (j + 1) * half].astype(BF)
    ao[...] += nt(dh[0, :, feat_q:], parts[0, :, feat_q:qkv]) + nt(dh[1, :, feat_q:], parts[1, :, feat_q:qkv])
    for j in range(2):
        parts[j, :, feat_q:qkv] = nn(normed_t, dh[j, :, feat_q:]).astype(BF)
    key_sum = PlaneSum(2, feat_q, HD)
    key_sum.begin()
    grad, gain_buf[0, 0:1, :] = norm_grad(x[...].astype(F32), gains[0:1, :], ao[...])
    key_sum.spread()
    for copy in lo_copies:
        copy.wait_send()
    lo_own.wait()
    cut_t[...] = (grad + own[...]).astype(BF).T
    gt_copies, gt_own = give(cut_t, gt_out, gt_s, gt_r, loc_s.at[1])
    gain_copies = [
        remote(gain_buf.at[0], gain_in.at[j], gn_s.at[j], gn_r.at[j], d) for j, (_, d) in enumerate(others)
    ]
    for copy in gain_copies:
        copy.start()
    settle(EARLY + 1)
    line_step(11)
    line_step(12)
    line_step(13)
    total = query_sum.result()
    for i in range(2):
        mine[hidden_pairs + 1, i] = total[:, i * TILE : (i + 1) * TILE]
    line_step(14)
    line_step(15)
    total = key_sum.result()
    for i in range(2):
        a_mine[0, i] = total[i * depth // 2 : (i + 1) * depth // 2]
    for copy in gain_copies:
        copy.wait()
    gain_buf[1] = gain_buf[0] + sum(gain_in[j] for j in range(7))
    gain_copies = [
        remote(gain_buf.at[1], gain_in.at[7 + i], gn_s.at[7 + i], gn_r.at[7 + i], ((place + i + 1) % 4, row, col))
        for i in range(3 if on_line else 0)
    ]
    for copy in gain_copies:
        copy.start()

    for p in range(16, pairs):
        line_step(p)
    small.sent(0)
    small.add(0)
    line_rest(pairs)
    small.total(0)
    for p in range(pairs + 1, pairs + 4):
        line_rest(p)
    small.forward(0, False)
    for p in range(pairs + 4, pairs + LATE):
        line_rest(p)

    def drain(k, carry):
        line.drain(k)
        return carry

    lax.fori_loop(0, pairs, drain, 0)
    small.drain(0)
    for copy in gain_copies:
        copy.wait()
    gain_out[...] = gain_buf[1]
    for i in range(len(gain_copies)):
        gain_out[...] += gain_in[7 + i]
    for copy in lo_copies:
        copy.wait_recv()
    for copy in gt_copies:
        copy.wait()
    gt_own.wait()
    for copy in kv_core:
        copy.wait_send()


def attention_back(*args):
    dparts, pre_t, hh, lo, heads, q_pre, kv, bias, wa = (args[i] for i in (0, 1, 3, 7, 11, 12, 14, 15, 16))
    loc, width = lo.shape
    depth, feats = width // 4, wa.shape[2]
    hidden_pairs = 3 * hh.shape[1] // TILE
    pairs = hidden_pairs + 2
    keys = kv.shape[0]
    cut = width // 8
    dma = pltpu.SemaphoreType.DMA
    piece = (depth, TILE)
    rest = (depth // 2, TILE)
    struct = jax.ShapeDtypeStruct
    vmem = pltpu.VMEM
    return pl.pallas_call(
        back_kernel,
        out_shape=(
            struct((depth, 2 * hh.shape[1]), BF),
            struct((depth, 2 * hh.shape[1]), BF),
            struct((depth, 2 * hh.shape[1]), BF),
            struct((depth, feats), BF),
            struct((cut, keys), BF),
            struct((cut, keys), BF),
            struct((8, width), F32),
        ),
        in_specs=[any_spec()] * 17 + [vmem_spec()] * 7,
        out_specs=[any_spec()] * 6 + [vmem_spec()],
        scratch_shapes=[
            vmem((pairs, 2) + piece, BF),
            vmem((pairs, 2) + piece, BF),
            vmem((pairs,) + piece, BF),
            vmem(((hidden_pairs + 1) // 2,) + piece, BF),
            vmem((1, 2) + rest, BF),
            vmem((1, 2) + rest, BF),
            vmem((1,) + rest, BF),
            vmem((2, width, feats), BF),
            vmem((width, feats), BF),
            vmem((3 * depth, feats), BF),
            vmem((3, depth, feats), BF),
            vmem(dparts.shape, BF),
            vmem((2,) + pre_t.shape, BF),
            vmem((3, pre_t.shape[1], TILE), BF),
            vmem((3, 4) + piece, BF),
        ]
        + [vmem(args[i].shape, args[i].dtype) for i in (6, 7, 8, 9, 10, 11, 12, 13, 14, 15)]
        + [
            vmem((HD, keys), BF),
            vmem(heads.shape, BF),
            vmem((keys, HD), F32),
            vmem((keys, HD), F32),
            vmem((4, loc, 2 * HD), BF),
            vmem((3, loc, 2 * HD), BF),
            vmem((2, loc, feats - heads.shape[1] // 2), BF),
            vmem((width, loc), BF),
            vmem((2, 8, width), F32),
            vmem((10, 8, width), F32),
            dma((12,)), dma((3,)), dma((2,)), dma(()), dma((3,)), dma((3,)), dma((3, 2)), dma((hidden_pairs, 2)),
            dma((4,)), dma((4,)), dma((3,)), dma((3,)),
            dma((3, 4)), dma((3, 4)), dma((3, 3)), dma((3, 3)),
            dma((7,)), dma((7,)), dma((7,)), dma((7,)), dma((10,)), dma((10,)), dma((2,)),
        ]
        + line_sems(pairs)
        + line_sems(1),
        compiler_params=params(6),
        name="attention_back",
    )(*args)


def finish_kernel(gate_in, up_in, down_in, attn_in, tok_in, gate, up, down, wq, wk, wv, wo, tok):
    for src, dst in ((gate_in, gate), (up_in, up), (down_in, down)):
        dst[...] = src[:, : dst.shape[1]].astype(F32)
    at = 0
    for dst in (wq, wk, wv, wo):
        dst[...] = attn_in[:, at : at + dst.shape[1]].astype(F32)
        at += dst.shape[1]
    tok[...] = tok_in[...].astype(F32)


def finish(gate, up, down, attn, tok, hidden, widths):
    depth, cut = gate.shape[0], tok.shape[0]
    steps = cut // 16
    outs = [(depth, hidden)] * 3 + [(depth, width) for width in widths] + [tok.shape]

    def rows(shape):
        return pl.BlockSpec((shape[0] // steps, shape[1]), lambda i: (i, 0))

    return pl.pallas_call(
        finish_kernel,
        grid=(steps,),
        in_specs=[rows(array.shape) for array in (gate, up, down, attn, tok)],
        out_specs=[rows(shape) for shape in outs],
        out_shape=[jax.ShapeDtypeStruct(shape, F32) for shape in outs],
        compiler_params=pltpu.CompilerParams(vmem_limit_bytes=VMEM_LIMIT),
        name="finish",
    )(gate, up, down, attn, tok)


def body(
    tokens,
    cotangent,
    weight_query,
    weight_key,
    weight_value,
    weight_out,
    weight_gate,
    weight_up,
    weight_down,
    gain_input,
    gain_attn,
    gain_pre,
    gain_post,
    gain_query,
    gain_key,
    doc_lengths,
    block_size,
):
    cut = tokens.shape[1]
    row, col = lax.axis_index("row"), lax.axis_index("col")
    me = row * lax.axis_size("col") + col
    depth, hidden_half = weight_gate.shape
    q_half, kv_half = weight_query.shape[1], weight_key.shape[1]
    gain_block = jnp.pad(jnp.stack([gain_input, gain_attn, gain_pre, gain_post]), ((0, 4), (0, 0)))
    (
        w_hidden, w_attn, kv_all, bias, inputs, upstream, gains, query_pre, key_pre, log_total,
        cos_table, sin_table, head_bf, attn_out, residual, pre_normed,
    ) = attention_front(
        tokens.T, cotangent.T, gain_block, weight_query, weight_key, weight_value, weight_out.T,
        weight_gate, weight_up, weight_down.T, gain_query[None], gain_key[None], doc_lengths, block_size,
    )
    layer_rows, grad_g_post, grad_own, grad_parts, pre_t, grad_mlp_t, hidden, grad_gate, grad_up = mlp(
        pre_normed, residual, upstream, gains, w_hidden
    )
    sum_gate, sum_up, sum_down, attn_sum, layer_cut, token_cut, gain_sums = attention_back(
        grad_parts, pre_t, grad_mlp_t, hidden, grad_gate, grad_up, grad_own, layer_rows, attn_out, upstream,
        inputs, head_bf, query_pre, key_pre, kv_all, bias, w_attn, gains, gain_query[None], gain_key[None],
        log_total, cos_table, sin_table, grad_g_post,
    )
    if lax.axis_size("dp") != 4:
        sum_gate, sum_up, sum_down, attn_sum, gain_sums = (
            lax.psum(v.astype(F32), "dp") for v in (sum_gate, sum_up, sum_down, attn_sum, gain_sums)
        )
    grad_gate, grad_up, grad_down, grad_query, grad_key, grad_value, grad_out, grad_tokens = finish(
        sum_gate, sum_up, sum_down, attn_sum, token_cut, hidden_half, (q_half, kv_half, kv_half, q_half)
    )
    my_gains = lax.dynamic_slice_in_dim(gain_sums[:4], me * cut, cut, 1)
    return (
        layer_cut.T,
        grad_tokens.T,
        grad_query,
        grad_key,
        grad_value,
        grad_out.T,
        grad_gate,
        grad_up,
        grad_down.T,
        my_gains[0],
        my_gains[1],
        my_gains[2],
        my_gains[3],
        gain_sums[4, :HD],
        gain_sums[5, :HD],
    )


def solution(mesh):
    in_specs = (
        P("dp", ("row", "col")),
        P("dp", ("row", "col")),
        P("row", "col"),
        P("row", "col"),
        P("row", "col"),
        P("col", "row"),
        P("row", "col"),
        P("row", "col"),
        P("col", "row"),
        P(("row", "col")),
        P(("row", "col")),
        P(("row", "col")),
        P(("row", "col")),
        P(),
        P(),
        P("dp", None),
        P(),
    )
    out_specs = (
        P("dp", ("row", "col")),
        P("dp", ("row", "col")),
        P("row", "col"),
        P("row", "col"),
        P("row", "col"),
        P("col", "row"),
        P("row", "col"),
        P("row", "col"),
        P("col", "row"),
        P(("row", "col")),
        P(("row", "col")),
        P(("row", "col")),
        P(("row", "col")),
        P(),
        P(),
    )
    return jax.shard_map(body, mesh=mesh, in_specs=in_specs, out_specs=out_specs, check_vma=False)
```

```python
import functools
import math

import jax
import jax.numpy as jnp
from jax import lax
from jax.experimental import pallas as pl
from jax.experimental.pallas import tpu as pltpu
from jax.sharding import PartitionSpec as P

HD = 256
EPS = 1e-06
ROPE_BASE = 1000000.0
GELU_C = 0.7978845608028654
BF = jnp.bfloat16
F32 = jnp.float32
PLANE = ("row", "col")


def dot(left, right, dims):
    return lax.dot_general(left, right, (dims, ((), ())), preferred_element_type=F32)


def nn(left, right):
    return dot(left, right, ((1,), (0,)))


def nt(left, right):
    return dot(left, right, ((1,), (1,)))


def tn(left, right):
    return dot(left, right, ((0,), (0,)))


MESH = pl.DeviceIdType.MESH
TILE = 256
KV_SLOTS = (0, 1, 4, 5)
LEAD = 4
VMEM_LIMIT = 64 * 1024 * 1024 - 512 * 1024


def whereabouts():
    place, row, col = lax.axis_index("dp"), lax.axis_index("row"), lax.axis_index("col")
    return place, row, col, row // 2, row % 2


def peers():
    place, row, col, high, core = whereabouts()
    far = row + 2 - 4 * high
    return (
        (place, row, 1 - col),
        (place, far, col),
        (place, far, 1 - col),
        (place, row + 1 - 2 * core, col),
    )


def remote(src, dst, send, recv, device):
    return pltpu.make_async_remote_copy(
        src_ref=src, dst_ref=dst, send_sem=send, recv_sem=recv, device_id=device, device_id_type=MESH
    )


def greet(devices):
    barrier = pltpu.get_barrier_semaphore()
    for device in devices:
        pl.semaphore_signal(barrier, inc=1, device_id=device, device_id_type=MESH)
    pl.semaphore_wait(barrier, len(devices))


def any_spec():
    return pl.BlockSpec(memory_space=pl.ANY)


def vmem_spec():
    return pl.BlockSpec(memory_space=pltpu.VMEM)


def params(number):
    return pltpu.CompilerParams(
        collective_id=number, has_side_effects=True, vmem_limit_bytes=VMEM_LIMIT
    )


def token_places(lengths, span, tokens):
    inverse = 1.0 / jnp.full((1, 1), span[0], jnp.int32).astype(F32)
    document = jnp.zeros_like(tokens)
    first = jnp.zeros_like(tokens)
    end = jnp.int32(0)
    for i in range(lengths.shape[1]):
        end = end + lengths[0, i]
        past = tokens >= end
        document = jnp.where(past, i + 1, document)
        first = jnp.where(past, end, first)
    position = (tokens - first).astype(F32)
    return document, jnp.floor((position + 0.5) * inverse), position


def mask_bias(lengths, span, bias, me, slots):
    local = bias.shape[1]
    query_doc, query_block, _ = token_places(
        lengths, span, me * local + lax.broadcasted_iota(jnp.int32, (1, local), 1)
    )
    for s, owner in enumerate(slots):
        key_doc, key_block, _ = token_places(
            lengths, span, owner * local + lax.broadcasted_iota(jnp.int32, (local, 1), 0)
        )
        seen = (key_doc == query_doc) & (key_block <= query_block)
        bias[s * local : (s + 1) * local, :] = jnp.where(seen, 0.0, -1e30).astype(BF)


def slot_owners():
    place, row, col, high, core = whereabouts()
    owners = []
    for s in range(8):
        r2 = (high + s // 4) % 2 * 2 + (core + s // 2) % 2
        owners.append(2 * r2 + (col + s) % 2)
    return owners


def sent_to_all(index):
    place, row, col, high, core = whereabouts()
    others = []
    for s in range(1, 8):
        r2, c2 = (high + s // 4) % 2 * 2 + (core + s // 2) % 2, (col + s) % 2
        others.append((2 * r2 + c2, (place, r2, c2)))
    return others


def head_forward(values, scales, cos, sin):
    half = values.shape[1] // 2
    inverse = lax.rsqrt(jnp.mean(values * values, axis=1, keepdims=True) + EPS)
    scaled = values * inverse * (1.0 + scales)
    first, second = scaled[:, :half], scaled[:, half:]
    return jnp.concatenate([first * cos - second * sin, second * cos + first * sin], axis=1)


def front_kernel(
    tok, ct, gain_block, wq, wk, wv, wo, wg, wu, wd, gq, gk, lengths, span,
    wm_out, wa_out, kv_out, bias_out, x_out, ct_out, gains, q_pre, k_pre, lse, cos, sin, heads, ao, res, pre,
    wm, wa, tok_all, ct_all, gain_all, q_out, kv, v_t, bias, probs,
    wm_l, wa_l, tk_s, tk_r, ct_s, ct_r, gn_s, gn_r, wa_s, wa_r, wb_s, wb_r, wy_s, wy_r, wu_s, wd_s, wz_r, wc_s, wc_r, wo_s, wo_r, kv_s, kv_r, loc_s,
):
    place, row, col, high, core = whereabouts()
    me = 2 * row + col
    px, py, pd, pc = peers()
    others = sent_to_all(me)
    depth, hidden = wg.shape
    slab = wm_out.shape[2]
    cut = tok.shape[0]
    loc = x_out.shape[0]
    head_count = heads.shape[1] // HD
    half = HD // 2
    members = len(others) + 1
    share = lax.axis_size("dp") == 4
    far_row = row + 2 - 4 * high
    friends = [device for _, device in others]
    if share:
        friends += [((place + i) % 4, row, col) for i in range(1, 4)]

    loads = [
        pltpu.make_async_copy(src, wm.at[m, :, pl.ds(0, hidden)], wm_l.at[m]) for m, src in enumerate((wg, wu, wd))
    ]
    rows = pl.ds(row * depth, depth)
    far_rows = pl.ds(far_row * depth, depth)
    spots, at = [], 0
    for src in (wq, wk, wv, wo):
        spots.append(pl.ds(at, src.shape[1]))
        at += src.shape[1]
    qkv = at - wo.shape[1]
    own = [
        pltpu.make_async_copy(src, wa.at[col, rows, spot], wa_l.at[i])
        for i, (src, spot) in enumerate(zip((wq, wk, wv, wo), spots))
    ]
    tok_own = pltpu.make_async_copy(
        tok.at[:, pl.ds(pl.multiple_of(me * loc, 128), loc)], tok_all.at[pl.ds(me * cut, cut)], loc_s.at[0]
    )
    ct_own = pltpu.make_async_copy(
        ct.at[:, pl.ds(pl.multiple_of(me * loc, 128), loc)], ct_all.at[pl.ds(me * cut, cut)], loc_s.at[1]
    )
    gain_own = pltpu.make_async_copy(gain_block, gain_all.at[me], loc_s.at[2])
    for copy in [tok_own, gain_own] + own + [ct_own] + loads:
        copy.start()
    greet(friends)

    def scatter(src, dst, send, recv):
        copies = [
            remote(
                src.at[:, pl.ds(pl.multiple_of(index * loc, 128), loc)],
                dst.at[pl.ds(me * cut, cut)],
                send.at[j],
                recv.at[j],
                device,
            )
            for j, (index, device) in enumerate(others)
        ]
        for copy in copies:
            copy.start()
        return copies

    tok_copies = scatter(tok, tok_all, tk_s, tk_r)
    gain_copies = [
        remote(gain_block, gain_all.at[me], gn_s.at[j], gn_r.at[j], device) for j, (_, device) in enumerate(others)
    ]
    for copy in gain_copies:
        copy.start()
    attn_copies = {}

    def hand_out(which):
        for i in ((0, 1, 2), (3,))[which]:
            for j, device in enumerate((px, py, pd, pc)):
                attn_copies[i, j] = remote(
                    (wq, wk, wv, wo)[i], wa.at[col, rows, spots[i]], wa_s.at[i, j], wa_r.at[i, j], device
                )
                attn_copies[i, j].start()

    for copy in loads:
        copy.wait()
    for m in range(3):
        wm[m, :, hidden:] = jnp.zeros((depth, 2 * slab - hidden), BF)
    mine = pl.ds(pl.multiple_of(high * slab, 128), slab)
    away = pl.ds(pl.multiple_of((1 - high) * slab, 128), slab)
    unit = depth // 6
    groups, rounds = 18, 4

    def group(start, g):
        return g // 6, pl.ds(pl.multiple_of(start + g % 6 * unit, 16), unit)

    def over(g):
        m, at = group(0, g)
        return remote(wm.at[m, at, away], wm_out.at[group(row * depth, g)], wy_s.at[g], wy_r.at[g], py)

    def along(g, step):
        spot = wm_out.at[group(far_row * depth, g)]
        return remote(spot, spot, (wu_s if step > 0 else wd_s).at[g], wz_r.at[g], ((place + step) % 4, row, col))

    def between(g):
        spot = wm_out.at[group(far_row * depth, g)]
        return remote(spot, spot, wc_s.at[g], wc_r.at[g], pc)

    own_hidden = [pltpu.make_async_copy(wm.at[m, :, mine], wm_out.at[m, rows], wm_l.at[m]) for m in range(3)]
    beside = [remote(wm.at[m, :, mine], wm_out.at[m, rows], wo_s.at[m], wo_r.at[m], pc) for m in range(3)]
    extra = 16 + place % 2
    for m in range(3):
        own_hidden[m].start()
        beside[m].start()
    fetched = [rounds * r + place for r in range(rounds)] + [extra] if share else list(range(groups))
    for g in fetched[:rounds]:
        over(g).start()
    hand_out(0)
    for g in fetched[rounds:]:
        over(g).start()

    def travel(distance, r, act_up, act_down):
        if distance == 0:
            g = rounds * r + place
            pl.when(place < 3)(lambda: act_up(g))
            pl.when(place > 0)(lambda: act_down(g))
        else:
            below, above = rounds * r + place - distance, rounds * r + place + distance
            pl.when(jnp.logical_and(place >= distance, place < 3))(lambda: act_up(below))
            pl.when(jnp.logical_and(place + distance <= 3, place > 0))(lambda: act_down(above))

    def arrive(distance, r):
        if distance == 0:
            g = rounds * r + place
            over(g).wait_recv()
            between(g).start()
        else:
            for g, there in (
                (rounds * r + place - distance, place >= distance),
                (rounds * r + place + distance, place + distance <= 3),
            ):

                @pl.when(there)
                def _(g=g):
                    along(g, 1).wait_recv()
                    between(g).start()

        travel(distance, r, lambda g: along(g, 1).start(), lambda g: along(g, -1).start())

    def arrive_extra():
        over(extra).wait_recv()
        between(extra).start()
        pl.when(place % 2 == 0)(lambda: along(extra, 1).start())
        pl.when(place % 2 == 1)(lambda: along(extra, -1).start())

    def arrive_whole():
        for g in fetched:
            over(g).wait_recv()
            between(g).start()

    if share:
        events = [
            functools.partial(arrive, distance, r)
            for distance, r in (
                (0, 0), (0, 1), (0, 2), (1, 0), (0, 3), (1, 1), (2, 0), (1, 2), (2, 1), (3, 0), (1, 3), (2, 2), (3, 1),
                (2, 3), (3, 2), (3, 3),
            )
        ]
        events.insert(7, arrive_extra)
    else:
        events = [arrive_whole]

    def poll(count):
        for _ in range(min(count, len(events))):
            events.pop(0)()

    def arrived():
        if share:
            other = 33 - extra
            along(other, 1).wait_recv()
            between(other).start()
            pl.when(place % 2 == 0)(lambda: along(extra, 1).wait_send())
            pl.when(place % 2 == 1)(lambda: along(extra, -1).wait_send())
            for distance in range(4):
                for r in range(rounds):
                    travel(distance, r, lambda g: along(g, 1).wait_send(), lambda g: along(g, -1).wait_send())
        for g in fetched:
            over(g).wait_send()
        for g in range(groups):
            between(g).wait()
        for m in range(3):
            beside[m].wait()
            own_hidden[m].wait()

    doc, _, position = token_places(lengths, span, me * loc + lax.broadcasted_iota(jnp.int32, (loc, 1), 0))
    steps = lax.broadcasted_iota(jnp.int32, (1, half), 1).astype(F32)
    phases = position * jnp.exp(steps * (-2.0 * math.log(ROPE_BASE) / HD))
    cos[...] = jnp.cos(phases)
    sin[...] = jnp.sin(phases)
    mask_bias(lengths, span, bias, me, slot_owners())
    bias_copy = pltpu.make_async_copy(bias, bias_out, loc_s.at[3])
    bias_copy.start()

    tok_own.wait()
    gain_own.wait()
    for copy in tok_copies + gain_copies:
        copy.wait_recv()
    for f in range(members):
        gains[:, f * cut : (f + 1) * cut] = gain_all[f]
    x_out[...] = tok_all[...].T
    inputs = x_out[...].astype(F32)
    inverse = lax.rsqrt(jnp.mean(inputs * inputs, axis=1, keepdims=True) + EPS)
    normed = (inputs * inverse * (1.0 + gains[0:1, :])).astype(BF)

    corners = ((row, 1 - col), (far_row, col), (far_row, 1 - col))
    part_spots = (pl.ds(0, qkv), pl.ds(qkv, wo.shape[1]))
    passed = {}

    def pass_on(which):
        for j, (r2, c2) in enumerate(corners):
            for i in ((0, 1, 2), (3,))[which]:
                attn_copies[i, j].wait_recv()
            slot = wa.at[c2, pl.ds(r2 * depth, depth), part_spots[which]]
            passed[which, j] = remote(slot, slot, wb_s.at[which, j], wb_r.at[which, j], pc)
            passed[which, j].start()

    def settled(which):
        for i in ((0, 1, 2), (3,))[which]:
            own[i].wait()
            attn_copies[i, 3].wait_recv()
        for j in range(3):
            passed[which, j].wait_recv()

    poll(5)
    pass_on(0)
    poll(1)
    settled(0)
    poll(1)
    q_half, kv_half = wq.shape[1], wk.shape[1]
    for j in range(2):
        found = nn(normed, wa[j, :, q_half:qkv])
        k_pre[:, j * kv_half : (j + 1) * kv_half] = found[:, :kv_half]
        kv[:loc, HD + j * kv_half : HD + (j + 1) * kv_half] = found[:, kv_half:].astype(BF)
    kv[:loc, :HD] = head_forward(k_pre[...], gk[...], cos[...], sin[...]).astype(BF)
    kv_first = [
        remote(kv.at[pl.ds(0, loc)], kv.at[pl.ds(slot * loc, loc)], kv_s.at[i], kv_r.at[i], device)
        for i, (slot, device) in enumerate(((1, px), (4, py), (5, pd), (2, pc)))
    ]
    for copy in kv_first:
        copy.start()
    hand_out(1)
    for j in range(2):
        q_pre[:, j * q_half : (j + 1) * q_half] = nn(normed, wa[j, :, :q_half])
    ct_copies = scatter(ct, ct_all, ct_s, ct_r)
    for h in range(head_count):
        cols = slice(h * HD, (h + 1) * HD)
        q_out[:, cols] = (head_forward(q_pre[:, cols], gq[...], cos[...], sin[...]) * (1.0 / math.sqrt(HD))).astype(BF)
    lse[...] = jnp.zeros_like(lse)
    poll(1)

    def slot_scores(slot):
        keys = slice(slot * loc, (slot + 1) * loc)
        v_t[:, keys] = kv[keys, HD:].T
        for h in range(head_count):
            grown = jnp.exp(nt(kv[keys, :HD], q_out[:, h * HD : (h + 1) * HD]) + bias[keys, :].astype(F32))
            probs[h, keys, :] = grown
            lse[h : h + 1, :] += jnp.sum(grown, axis=0, keepdims=True)

    slot_scores(0)
    poll(2)
    kv_relay = []
    for i, slot in enumerate((1, 4, 5)):
        kv_first[i].wait_recv()
        keys = pl.ds(slot * loc, loc)
        copy = remote(kv.at[keys], kv.at[pl.ds((slot + 2) * loc, loc)], kv_s.at[4 + i], kv_r.at[4 + i], pc)
        copy.start()
        kv_relay.append(copy)
        slot_scores(slot)
        poll(1)
        if i == 0:
            kv_first[3].wait_recv()
            slot_scores(2)
            poll(1)
    for i, slot in enumerate((3, 6, 7)):
        kv_relay[i].wait_recv()
        slot_scores(slot)
        poll(1)
    kv_copy = pltpu.make_async_copy(kv, kv_out, loc_s.at[4])
    kv_copy.start()
    for h in range(head_count):
        inverse = 1.0 / lse[h : h + 1, :]
        total = nn(v_t[...], (probs[h] * inverse).astype(BF))
        heads[:, h * HD : (h + 1) * HD] = total.T.astype(BF)
        poll(1)
    lse[...] = jnp.log(lse[...])
    pass_on(1)
    poll(1)
    settled(1)
    wa_copy = pltpu.make_async_copy(wa, wa_out, loc_s.at[5])
    wa_copy.start()
    feats = wo.shape[1]
    ao[...] = nt(heads[:, :feats], wa[0, :, qkv:]) + nt(heads[:, feats:], wa[1, :, qkv:])

    def norm_rows(values, scales):
        inverse = lax.rsqrt(jnp.mean(values * values, axis=1, keepdims=True) + EPS)
        return values * inverse * (1.0 + scales)

    res[...] = inputs + norm_rows(ao[...], gains[1:2, :])
    pre[...] = norm_rows(res[...], gains[2:3, :]).astype(BF)
    ct_own.wait()
    for copy in ct_copies:
        copy.wait_recv()
    ct_out[...] = ct_all[...].T
    poll(len(events))
    arrived()
    for copy in tok_copies + gain_copies + ct_copies + kv_first:
        copy.wait_send()
    for copy in kv_relay + list(passed.values()) + list(attn_copies.values()):
        copy.wait_send()
    bias_copy.wait()
    kv_copy.wait()
    wa_copy.wait()


def attention_front(*args):
    tok, _, gain_block, wq, wk, wv, wo, wg = args[:8]
    cut, tok_count = tok.shape
    members = 8
    width, loc = cut * members, tok_count // members
    depth, hidden = wg.shape
    slab = -(-hidden // (2 * TILE)) * TILE
    feats = wq.shape[1] + wk.shape[1] + wv.shape[1] + wo.shape[1]
    q_width = 2 * wq.shape[1]
    dma = pltpu.SemaphoreType.DMA
    struct = jax.ShapeDtypeStruct
    smem = pl.BlockSpec(memory_space=pltpu.SMEM)
    return pl.pallas_call(
        front_kernel,
        out_shape=(
            struct((3, width, slab), BF),
            struct((2, width, feats), BF),
            struct((tok_count, 2 * HD), BF),
            struct((tok_count, loc), BF),
            struct((loc, width), BF),
            struct((loc, width), BF),
            struct((8, width), F32),
            struct((loc, q_width), F32),
            struct((loc, HD), F32),
            struct((q_width // HD, loc), F32),
            struct((loc, HD // 2), F32),
            struct((loc, HD // 2), F32),
            struct((loc, q_width), BF),
            struct((loc, width), F32),
            struct((loc, width), F32),
            struct((loc, width), BF),
        ),
        in_specs=[any_spec()] * 10 + [vmem_spec()] * 2 + [smem] * 2,
        out_specs=[any_spec()] * 4 + [vmem_spec()] * 12,
        scratch_shapes=[
            pltpu.VMEM((3, depth, 2 * slab), BF),
            pltpu.VMEM((2, width, feats), BF),
            pltpu.VMEM((width, loc), BF),
            pltpu.VMEM((width, loc), BF),
            pltpu.VMEM((members,) + gain_block.shape, F32),
            pltpu.VMEM((loc, q_width), BF),
            pltpu.VMEM((tok_count, 2 * HD), BF),
            pltpu.VMEM((HD, tok_count), BF),
            pltpu.VMEM((tok_count, loc), BF),
            pltpu.VMEM((q_width // HD, tok_count, loc), F32),
            dma((3,)), dma((4,)), dma((7,)), dma((7,)), dma((7,)), dma((7,)), dma((7,)), dma((7,)),
            dma((4, 4)), dma((4, 4)), dma((2, 3)), dma((2, 3)), dma((18,)), dma((18,)), dma((18,)), dma((18,)),
            dma((18,)), dma((18,)), dma((18,)), dma((3,)), dma((3,)), dma((7,)), dma((7,)), dma((6,)),
        ],
        compiler_params=params(1),
        name="attention_front",
    )(*args)


def mlp_kernel(
    pre, res, ct, gains, w_h,
    lo, dgpost, dpre, dparts, pre_t_out, gm_t_out, hh_out, bb_out, aa_out,
    wg, wu, wd, pre_all, pre_t, gm_all, gm_t, aa, bb, hh, acc, own, parts, prc,
    w_sem, ag_s, ag_r, rs_s, rs_r, gs_s, gs_r, st_s,
):
    place, row, col, high, core = whereabouts()
    px, py, pd, pc = peers()
    quad = (px, py, pd)
    loc, width = pre.shape
    slab = wg.shape[1]
    tiles = slab // TILE

    def store(kind, j, src, dst):
        rows = chunk_rows(j)
        return pltpu.make_async_copy(src.at[rows], dst.at[rows], st_s.at[kind, j])

    loads = [
        pltpu.make_async_copy(src, dst, w_sem.at[i])
        for i, (src, dst) in enumerate(((w_h.at[0], wg), (w_h.at[1], wu), (w_h.at[2], wd)))
    ]
    for copy in loads:
        copy.start()
    greet((px, py, pd, pc))

    def spread(src, buffer, send, recv):
        copies = [remote(src, buffer.at[i + 1], send.at[i], recv.at[i], p) for i, p in enumerate(quad)]
        for copy in copies:
            copy.start()
        return copies

    gathers = spread(pre, pre_all, ag_s, ag_r)
    pre_all[0] = pre[...]
    for copy in loads:
        copy.wait()

    def chunk_rows(j):
        return pl.ds(pl.multiple_of(j * loc, 256), loc)

    def chunk_device(j):
        return (place, (row + j // 2 * 2) % 4, (col + j) % 2)

    def give_part(j):
        return remote(parts.at[j - 1], prc.at[j - 1], rs_s.at[j - 1], rs_r.at[j - 1], chunk_device(j))

    def got_chunk(j, buffer, send, recv):
        pl.when(j > 0)(lambda: remote(pre, buffer.at[j], send.at[j - 1], recv.at[j - 1], chunk_device(j)).wait_recv())

    def forward(j, carry):
        got_chunk(j, pre_all, ag_s, ag_r)
        rows = chunk_rows(j)
        for n in range(tiles):
            at = slice(n * TILE, (n + 1) * TILE)
            x = pre_all[j]
            gate = nn(x, wg[:, at])
            up = nn(x, wu[:, at])
            square = gate * gate
            bend = jnp.tanh(GELU_C * gate * (1.0 + 0.044715 * square))
            half = 0.5 * (1.0 + bend)
            gelu = gate * half
            slope = half + 0.5 * gate * (1.0 - bend * bend) * (GELU_C * (1.0 + 0.134145 * square))
            hidden = (gelu * up).astype(BF)
            aa[rows, at] = gelu.astype(BF)
            bb[rows, at] = (up * slope).astype(BF)
            hh[rows, at] = hidden
        acc[...] = nt(hh[rows, :], wd[...])
        store(0, j, hh, hh_out).start()

        @pl.when(j == 0)
        def _():
            own[...] = acc[...]

        @pl.when(j > 0)
        def _():
            parts[j - 1] = acc[...].astype(BF)
            give_part(j).start()

        return carry

    lax.fori_loop(0, 4, forward, 0)
    for j in range(4):
        pre_t[:, j * loc : (j + 1) * loc] = pre_all[j].T
    pre_copy = pltpu.make_async_copy(pre_t, pre_t_out, st_s.at[3, 0])
    pre_copy.start()
    for j in range(1, 4):
        give_part(j).wait()
    out = own[...] + prc[0].astype(F32) + prc[1].astype(F32) + prc[2].astype(F32)
    scale = 1.0 + gains[3:4, :]
    inverse = lax.rsqrt(jnp.mean(out * out, axis=1, keepdims=True) + EPS)
    lo[...] = (res[...] + out * inverse * scale).astype(BF)
    upstream = ct[...].astype(F32)
    scaled = upstream * scale
    inner = jnp.mean(scaled * out, axis=1, keepdims=True)
    gm_all[0] = (scaled * inverse - out * (inverse * inverse * inverse * inner)).astype(BF)
    dgpost[...] = jnp.sum(upstream * out * inverse, axis=0, keepdims=True)

    gathers2 = spread(gm_all.at[0], gm_all, gs_s, gs_r)
    def backward(j, carry):
        got_chunk(j, gm_all, gs_s, gs_r)
        rows = chunk_rows(j)
        for n in range(tiles):
            at = slice(n * TILE, (n + 1) * TILE)
            grad_hidden = nn(gm_all[j], wd[:, at])
            grad_gate = (grad_hidden * bb[rows, at].astype(F32)).astype(BF)
            grad_up = (grad_hidden * aa[rows, at].astype(F32)).astype(BF)
            bb[rows, at] = grad_gate
            aa[rows, at] = grad_up
        acc[...] = nt(bb[rows, :], wg[...]) + nt(aa[rows, :], wu[...])
        gm_t[:, rows] = gm_all[j].T
        store(1, j, bb, bb_out).start()
        store(2, j, aa, aa_out).start()

        @pl.when(j == 0)
        def _():
            dpre[...] = acc[...]

        @pl.when(j > 0)
        def _():
            dparts[j - 1] = acc[...].astype(BF)

        return carry

    lax.fori_loop(0, 4, backward, 0)
    gm_copy = pltpu.make_async_copy(gm_t, gm_t_out, st_s.at[3, 1])
    gm_copy.start()
    for j in range(4):
        store(0, j, hh, hh_out).wait()
        store(1, j, bb, bb_out).wait()
        store(2, j, aa, aa_out).wait()
    pre_copy.wait()
    gm_copy.wait()
    for copy in gathers + gathers2:
        copy.wait_send()


def mlp(pre, res, ct, gains, weights):
    loc, width = pre.shape
    slab = weights.shape[2]
    dma = pltpu.SemaphoreType.DMA
    struct = jax.ShapeDtypeStruct
    return pl.pallas_call(
        mlp_kernel,
        out_shape=(
            struct((loc, width), BF),
            struct((1, width), F32),
            struct((loc, width), F32),
            struct((3, loc, width), BF),
            struct((width, 4 * loc), BF),
            struct((width, 4 * loc), BF),
            struct((4 * loc, slab), BF),
            struct((4 * loc, slab), BF),
            struct((4 * loc, slab), BF),
        ),
        in_specs=[vmem_spec()] * 4 + [any_spec()],
        out_specs=[vmem_spec()] * 4 + [any_spec()] * 5,
        scratch_shapes=[
            pltpu.VMEM((width, slab), BF),
            pltpu.VMEM((width, slab), BF),
            pltpu.VMEM((width, slab), BF),
            pltpu.VMEM((4, loc, width), BF),
            pltpu.VMEM((width, 4 * loc), BF),
            pltpu.VMEM((4, loc, width), BF),
            pltpu.VMEM((width, 4 * loc), BF),
            pltpu.VMEM((4 * loc, slab), BF),
            pltpu.VMEM((4 * loc, slab), BF),
            pltpu.VMEM((4 * loc, slab), BF),
            pltpu.VMEM((loc, width), F32),
            pltpu.VMEM((loc, width), F32),
            pltpu.VMEM((3, loc, width), BF),
            pltpu.VMEM((3, loc, width), BF),
            dma((3,)),
            dma((3,)), dma((3,)), dma((3,)), dma((3,)), dma((3,)), dma((3,)), dma((4, 4)),
        ],
        compiler_params=params(3),
        name="feed_forward",
    )(pre, res, ct, gains, weights)


class Line:
    def __init__(self, mine, inbox, middle, turned, out, sems, turns):
        self.mine, self.inbox, self.middle, self.turned, self.out = mine, inbox, middle, turned, out
        self.in_s, self.in_r, self.mid_s, self.mid_r, self.x_s, self.x_r, self.o_s, self.o_r, self.l_s, self.y_s, self.y_r = sems
        place, row, col, high, core = whereabouts()
        self.turns = turns
        self.end = (place % 3) == 0
        self.inner = (jnp.where(place == 0, 1, 2), row, col)
        self.outer = ((place - 1) * 3 % 6, row, col)
        self.across = (3 - place, row, col)
        self.beside = (place, row + 2 - 4 * high, col)
        self.place = place

    def root(self, k):
        return (k + self.place + 1) % 2

    def inward(self, k, h):
        return remote(self.mine.at[k, h], self.inbox.at[k, h], self.in_s.at[k, h], self.in_r.at[k, h], self.inner)

    def partial(self, k):
        return remote(
            self.mine.at[k, 1 - self.root(k)], self.middle.at[k], self.mid_s.at[k], self.mid_r.at[k], self.across
        )

    def turn(self, k):
        return remote(self.mine.at[k, 1], self.turned.at[k // 2], self.y_s.at[k], self.y_r.at[k], self.beside)

    def spot(self, k, h):
        return self.out(k, h) if isinstance(k, int) else self.mine.at[k, h]

    def exchange(self, k, h, source):
        return remote(source, self.spot(k, h), self.x_s.at[k], self.x_r.at[k], self.across)

    def outward(self, k, h, source):
        return remote(source, self.spot(k, h), self.o_s.at[k, h], self.o_r.at[k, h], self.outer)

    def keep(self, k, h, source):
        return pltpu.make_async_copy(source, self.spot(k, h), self.l_s.at[k])

    def inside(self, act):
        pl.when(jnp.logical_not(self.end))(act)

    def turns_here(self, k):
        return jnp.logical_and(k < self.turns, self.root(k) == 1)

    def send(self, k):
        @pl.when(self.end)
        def _():
            for h in range(2):
                self.inward(k, h).start()

    def sent(self, k):
        @pl.when(self.end)
        def _():
            for h in range(2):
                self.inward(k, h).wait_send()

    def add(self, k):
        def act():
            other = 1 - self.root(k)
            self.inward(k, other).wait_recv()
            self.mine[k, other] = (
                self.mine[k, other].astype(F32) + self.inbox[k, other].astype(F32)
            ).astype(BF)
            self.partial(k).start()

        self.inside(act)

    def share(self, k, h, source):
        self.outward(k, h, source).start()
        self.exchange(k, h, source).start()
        self.keep(k, h, source).start()

    def total(self, k):
        def act():
            root = self.root(k)
            self.inward(k, root).wait_recv()
            self.partial(k).wait_recv()
            self.mine[k, root] = (
                self.mine[k, root].astype(F32) + self.inbox[k, root].astype(F32) + self.middle[k].astype(F32)
            ).astype(BF)

            if isinstance(k, int) and k >= self.turns:
                self.share(k, root, self.mine.at[k, root])
                return

            @pl.when(self.turns_here(k))
            def _():
                self.turn(k).start()

            @pl.when(jnp.logical_not(self.turns_here(k)))
            def _():
                self.share(k, root, self.mine.at[k, root])

        self.inside(act)

    def spread(self, k):
        @pl.when(jnp.logical_and(jnp.logical_not(self.end), self.turns_here(k)))
        def _():
            self.turn(k).wait_recv()
            self.share(k, 1, self.turned.at[k // 2])

    def forward(self, k, late):
        def act():
            other = 1 - self.root(k)
            source = self.out(k, other)
            self.exchange(k, other, self.mine.at[k, other]).wait_recv()
            self.outward(k, other, source).start()

        if k >= self.turns:
            if not late:
                self.inside(act)
        else:
            pl.when(jnp.logical_and(jnp.logical_not(self.end), self.root(k) == (0 if late else 1)))(act)

    def drain(self, k):
        @pl.when(self.end)
        def _():
            for h in range(2):
                self.outward(k, h, self.mine.at[k, h]).wait_recv()

        def act():
            root = self.root(k)
            self.partial(k).wait_send()
            self.exchange(k, root, self.mine.at[k, root]).wait_send()
            self.keep(k, root, self.mine.at[k, root]).wait()
            for h in range(2):
                self.outward(k, h, self.mine.at[k, h]).wait_send()

            if not isinstance(k, int):
                pl.when(self.turns_here(k))(lambda: self.turn(k).wait_send())

        self.inside(act)


class Alone:
    def __init__(self, mine, inbox, middle, turned, out, sems, turns):
        self.mine, self.out, self.turns = mine, out, turns
        self.l_s, self.y_s, self.y_r = sems[0], sems[9], sems[10]
        place, row, col, high, core = whereabouts()
        self.beside = (place, row + 2 - 4 * high, col)

    def send(self, k):
        pass

    def sent(self, k):
        pass

    def add(self, k):
        pass

    def spread(self, k):
        pass

    def forward(self, k, late):
        pass

    def copy(self, k, h):
        spot = self.out(k, h) if isinstance(k, int) else self.mine.at[k, h]
        return pltpu.make_async_copy(self.mine.at[k, h], spot, self.l_s.at[k, h])

    def turn(self, k):
        spot = self.out(k, 0) if isinstance(k, int) else self.mine.at[k, 1]
        return remote(self.mine.at[k, 1], spot, self.y_s.at[k], self.y_r.at[k], self.beside)

    def total(self, k):
        self.copy(k, 0).start()
        if isinstance(k, int):
            (self.turn(k) if k < self.turns else self.copy(k, 1)).start()
        else:
            pl.when(k < self.turns)(lambda: self.turn(k).start())
            pl.when(k >= self.turns)(lambda: self.copy(k, 1).start())

    def drain(self, k):
        self.copy(k, 0).wait()
        if isinstance(k, int):
            (self.turn(k) if k < self.turns else self.copy(k, 1)).wait()
        else:
            pl.when(k < self.turns)(lambda: self.turn(k).wait())
            pl.when(k >= self.turns)(lambda: self.copy(k, 1).wait())


def line_sems(count):
    dma = pltpu.SemaphoreType.DMA
    return [
        dma((count, 2)), dma((count, 2)), dma((count,)), dma((count,)), dma((count,)), dma((count,)),
        dma((count, 2)), dma((count, 2)), dma((count,)), dma((count,)), dma((count,)),
    ]


EARLY, AHEAD, SPREAD, LATE = 5, 3, 4, 6


def back_kernel(
    dparts, pre_t_h, gm_t_h, hh_h, bb_h, aa_h, own_h, lo_h, ao_h, ct_h, x_h, heads_h, q_pre_h, k_pre_h, kv_h,
    bias_h, wa_h, gains, gq, gk, lse, cos, sin, dgpost,
    gate_out, up_out, down_out, a_out, lo_out, gt_out, gain_out,
    mine, inbox, middle, turned, a_mine, a_in, a_mid, parts, cr, summed, qr, rsr, lefts, ring, halves,
    own, ga, ao, ct, x, heads, q_pre, k_pre, kv, bias,
    k_t, gh, dk, dv, kv_cr, kv_qr, dh, cut_t, gain_buf, gain_in,
    in_s, t_s, big_s, wa_l, rs_s, rs_r, c_s, c_r, kc_s, kc_r, kq_s, kq_r, pc_s, pc_r, pq_s, pq_r,
    lo_s, lo_r, gt_s, gt_r, gn_s, gn_r, loc_s, *line_refs,
):
    place, row, col, high, core = whereabouts()
    me = 2 * row + col
    px, py, pd, pc = peers()
    quad = (px, py, pd)
    others = sent_to_all(me)
    on_line = lax.axis_size("dp") == 4
    make = Line if on_line else Alone
    hidden_pairs = mine.shape[0] - 2
    slab = gate_out.shape[1] // 2

    def place_of(k, h):
        if k >= hidden_pairs:
            return a_out.at[:, pl.ds((0 if k > hidden_pairs else qkv) + h * TILE, TILE)]
        start = (high + h) % 2 * slab + k // 3 * TILE
        return (gate_out, up_out, down_out)[k % 3].at[:, pl.ds(pl.multiple_of(start, TILE), TILE)]

    def place_of_small(k, h):
        return a_out.at[pl.ds(h * (depth // 2), depth // 2), pl.ds(qkv - TILE, TILE)]

    line = make(mine, inbox, middle, turned, place_of, line_refs[:11], hidden_pairs)
    small = make(a_mine, a_in, a_mid, turned, place_of_small, line_refs[11:], 0)
    tiles = hidden_pairs // 3
    pairs = mine.shape[0]
    loc, width = x.shape
    depth = mine.shape[2]
    cut = width // 8
    all_tok = pre_t_h.shape[1]
    head_count = q_pre.shape[1] // HD
    half = HD // 2
    out_half = heads.shape[1] // 2
    feats = parts.shape[2]
    qkv = feats - out_half

    big = [
        pltpu.make_async_copy(src, lefts.at[i], big_s.at[i]) for i, src in enumerate((pre_t_h, gm_t_h))
    ]
    sources = (bb_h, aa_h, hh_h)

    def lanes(index):
        return pl.ds(pl.multiple_of(index * TILE, TILE), TILE)

    def load(n, m):
        return pltpu.make_async_copy(sources[m].at[:, lanes(n)], ring.at[m], t_s.at[m])

    for m in range(3):
        load(0, m).start()
        if m < 2:
            big[m].start()
    whole_wa = pltpu.make_async_copy(wa_h, parts, wa_l)
    smalls = [
        pltpu.make_async_copy(src, dst, in_s.at[i])
        for i, (src, dst) in enumerate(
            (
                (lo_h, ga), (own_h, own), (ao_h, ao), (ct_h, ct), (heads_h, heads),
                (kv_h, kv), (bias_h, bias), (q_pre_h, q_pre), (k_pre_h, k_pre), (x_h, x),
            )
        )
    ]
    for copy in smalls + [whole_wa]:
        copy.start()
    friends = [device for _, device in others]
    if on_line:
        friends += [((place + i) % 4, row, col) for i in range(1, 4)]
    greet(friends)
    scatters = [remote(dparts.at[i], rsr.at[i], rs_s.at[i], rs_r.at[i], device) for i, device in enumerate(quad)]
    for copy in scatters:
        copy.start()

    def to_core(k, m):
        return (
            remote(halves.at[m, 2 * high + 1 - core], mine.at[k, 0], c_s.at[m, 0], c_r.at[k, 0], pc),
            remote(halves.at[m, 3 - 2 * high - core], mine.at[k, 1], c_s.at[m, 1], c_r.at[k, 1], pc),
        )

    def produce(n):
        for m in range(3):
            load(n, m).wait()

        def one(m, carry):
            product = nn(lefts[m // 2], ring[m]).astype(BF)
            for b in range(4):
                halves[m, b] = product[b * depth : (b + 1) * depth]
            for copy in to_core(3 * n + m, m):
                copy.start()
            return carry

        lax.fori_loop(0, 3, one, 0)
        if n + 1 < tiles:
            for m in range(3):
                load(n + 1, m).start()

    def settle(n):
        def one(m, carry):
            k = 3 * n + m
            for copy in to_core(k, m):
                copy.wait()
            mine[k, 0] = (mine[k, 0].astype(F32) + halves[m, 2 * high + core].astype(F32)).astype(BF)
            mine[k, 1] = (mine[k, 1].astype(F32) + halves[m, 2 - 2 * high + core].astype(F32)).astype(BF)
            return carry

        lax.fori_loop(0, 3, one, 0)

    order = list(range(14)) + [hidden_pairs] + list(range(14, 18)) + [hidden_pairs + 1] + list(range(18, hidden_pairs))

    def line_rest(p):
        if 0 <= p - 1 < pairs:
            line.total(order[p - 1])
        if 0 <= p - SPREAD < pairs and order[p - SPREAD] < hidden_pairs:
            line.spread(order[p - SPREAD])
        if 0 <= p - 3 < pairs:
            line.forward(order[p - 3], False)
        if 0 <= p - LATE < pairs:
            line.forward(order[p - LATE], True)

    def line_step(p):
        line.sent(order[p])
        if p + AHEAD < pairs:
            line.send(order[p + AHEAD])
        elif p + AHEAD == pairs:
            small.send(0)
        line.add(order[p])
        line_rest(p)

    for copy in big:
        copy.wait()
    produce(0)
    for n in range(1, EARLY):
        settle(n - 1)
        for i in range(3 * n - 3, min(3 * n, AHEAD)):
            line.send(i)
        produce(n)
        if n >= EARLY - 3:
            line_step(n + 3 - EARLY)

    here = pl.ds(pl.multiple_of(me * loc, 128), loc)

    def give(src, dst, send, recv, local):
        copies = [
            remote(src.at[pl.ds(i * cut, cut)], dst.at[:, here], send.at[j], recv.at[j], d)
            for j, (i, d) in enumerate(others)
        ]
        for copy in copies:
            copy.start()
        stays = pltpu.make_async_copy(src.at[pl.ds(me * cut, cut)], dst.at[:, here], local)
        stays.start()
        return copies, stays

    def norm_grad(values, scales, upstream):
        inverse = lax.rsqrt(jnp.mean(values * values, axis=1, keepdims=True) + EPS)
        scaled = upstream * (1.0 + scales)
        inner = jnp.mean(scaled * values, axis=1, keepdims=True)
        grad = scaled * inverse - values * (inverse * inverse * inverse * inner)
        return grad, jnp.sum(upstream * values * inverse, axis=0, keepdims=True)

    smalls[0].wait()
    cut_t[...] = ga[...].T
    lo_copies, lo_own = give(cut_t, lo_out, lo_s, lo_r, loc_s.at[0])
    gain_buf[...] = jnp.zeros_like(gain_buf)
    for copy in smalls[1:] + [whole_wa]:
        copy.wait()
    k_t[...] = kv[:, :HD].T
    settle(EARLY - 1)
    produce(EARLY)
    for copy in scatters:
        copy.wait()
    grad_pre = own[...] + rsr[0].astype(F32) + rsr[1].astype(F32) + rsr[2].astype(F32)
    inverse = lax.rsqrt(jnp.mean(ao[...] * ao[...], axis=1, keepdims=True) + EPS)
    residual = x[...].astype(F32) + ao[...] * inverse * (1.0 + gains[1:2, :])
    grad, gain_buf[0, 2:3, :] = norm_grad(residual, gains[2:3, :], grad_pre)
    own[...] = grad + ct[...].astype(F32)
    grad, gain_buf[0, 1:2, :] = norm_grad(ao[...], gains[1:2, :], own[...])
    ga[...] = grad.astype(BF)
    gain_buf[0, 3:4, :] = dgpost[...]
    for j in range(2):
        gh[:, j * out_half : (j + 1) * out_half] = nn(ga[...], parts[j, :, qkv:]).astype(BF)
    line_step(3)

    wanted = ((1 - col, 1 - high, pd), (1 - col, high, px), (col, 1 - high, py), (col, high, None))

    def block(ref, index, columns):
        return ref.at[pl.ds(pl.multiple_of(index * depth, 16), depth), columns]

    class PlaneSum:
        def __init__(self, which, start, size):
            self.columns = pl.ds(start, size)
            self.core = [
                remote(
                    block(parts.at[c2], 2 * y2 + 1 - core, self.columns),
                    block(cr, 2 * c2 + y2, self.columns),
                    pc_s.at[which, i],
                    pc_r.at[which, 2 * c2 + y2],
                    pc,
                )
                for i, (c2, y2, _) in enumerate(wanted)
            ]
            self.sends = [
                remote(block(summed, i, self.columns), qr.at[i, :, self.columns], pq_s.at[which, i], pq_r.at[which, i], d)
                for i, (_, _, d) in enumerate(wanted[:3])
            ]

        def begin(self):
            for copy in self.core:
                copy.start()

        def added(self, i):
            c2, y2, _ = wanted[i]
            self.core[i].wait_recv()
            return block(parts.at[c2], 2 * y2 + core, self.columns)[...].astype(F32) + block(
                cr, 2 * c2 + y2, self.columns
            )[...].astype(F32)

        def spread(self):
            for i in range(3):
                block(summed, i, self.columns)[...] = self.added(i).astype(BF)
                self.sends[i].start()

        def result(self):
            total = self.added(3)
            for i in range(3):
                self.sends[i].wait()
                total = total + qr[i, :, self.columns].astype(F32)
            for copy in self.core:
                copy.wait_send()
            return total.astype(BF)

    ga_t = ga[...].T
    for j in range(2):
        for n in range(out_half // TILE):
            parts[j, :, qkv + n * TILE : qkv + (n + 1) * TILE] = nn(
                ga_t, heads[:, j * out_half + n * TILE : j * out_half + (n + 1) * TILE]
            ).astype(BF)
    out_sum = PlaneSum(0, qkv, out_half)
    out_sum.begin()
    line_step(4)

    step_keys = 512
    for h in range(head_count):
        cols = slice(h * HD, (h + 1) * HD)
        query = head_forward(q_pre[:, cols], gq[...], cos[...], sin[...]) * (1.0 / math.sqrt(HD))
        query, grad_head = query.astype(BF), gh[:, cols]
        delta = jnp.sum((grad_head.astype(F32) * heads[:, cols].astype(F32)).T, axis=0, keepdims=True)

        def keys(c, total, h=h, query=query, grad_head=grad_head, delta=delta):
            rows = pl.ds(pl.multiple_of(c * step_keys, step_keys), step_keys)
            scores = nt(kv[rows, :HD], query) + bias[rows, :].astype(F32)
            probs = jnp.exp(scores - lse[h : h + 1, :])
            grad_probs = nt(kv[rows, HD:], grad_head)
            grad_scores = (probs * (grad_probs - delta)).astype(BF)
            add_v = nn(probs.astype(BF), grad_head)
            add_k = nn(grad_scores, query)
            if h:
                dv[rows, :] += add_v
                dk[rows, :] += add_k
            else:
                dv[rows, :] = add_v
                dk[rows, :] = add_k
            return total + nn(k_t[:, rows], grad_scores)

        total = lax.fori_loop(0, kv.shape[0] // step_keys, keys, jnp.zeros((HD, loc), F32))
        grad_query = total.T * (1.0 / math.sqrt(HD))
        first, second = grad_query[:, :half], grad_query[:, half:]
        turned = jnp.concatenate(
            [first * cos[...] + second * sin[...], second * cos[...] - first * sin[...]], axis=1
        )
        grad, gain = norm_grad(q_pre[:, cols], gq[...], turned)
        gain_buf[0, 4:5, :HD] += gain
        dh[h // 2, :, (h % 2) * HD : (h % 2 + 1) * HD] = grad.astype(BF)
        if h == 0:
            out_sum.spread()
        if h % 2:
            line_step(3 + 2 * (h // 2 + 1))
            line_step(4 + 2 * (h // 2 + 1))

    stage = [rsr.at[i // 2, :, pl.ds(i % 2 * 2 * HD, 2 * HD)] for i in range(4)]
    for i, slot in enumerate(KV_SLOTS):
        rows = slice((slot + 2) * loc, (slot + 3) * loc)
        stage[i][:, :HD] = dk[rows, :].astype(BF)
        stage[i][:, HD:] = dv[rows, :].astype(BF)
    kv_core = [remote(stage[i], kv_cr.at[i], kc_s.at[i], kc_r.at[i], pc) for i in range(4)]
    for copy in kv_core:
        copy.start()
    inputs = x[...].astype(F32)
    inverse = lax.rsqrt(jnp.mean(inputs * inputs, axis=1, keepdims=True) + EPS)
    normed_t = (inputs * inverse * (1.0 + gains[0:1, :])).astype(BF).T
    feat_q = dh.shape[2] - HD
    ao[...] = nt(dh[0, :, :feat_q], parts[0, :, :feat_q]) + nt(dh[1, :, :feat_q], parts[1, :, :feat_q])
    kv_sums = (ct.at[:, pl.ds(0, 2 * HD)], ct.at[:, pl.ds(2 * HD, 2 * HD)], rsr.at[2, :, pl.ds(0, 2 * HD)])
    kv_sends = []
    for i, device in ((3, pd), (1, px), (2, py)):
        kv_core[i].wait_recv()
        rows = slice(KV_SLOTS[i] * loc, (KV_SLOTS[i] + 1) * loc)
        kv_sums[i - 1][:, :HD] = (dk[rows, :] + kv_cr[i, :, :HD].astype(F32)).astype(BF)
        kv_sums[i - 1][:, HD:] = (dv[rows, :] + kv_cr[i, :, HD:].astype(F32)).astype(BF)
        copy = remote(kv_sums[i - 1], kv_qr.at[i - 1], kq_s.at[i - 1], kq_r.at[i - 1], device)
        copy.start()
        kv_sends.append(copy)
    kv_core[0].wait_recv()
    for j in range(2):
        for n in range(feat_q // TILE):
            parts[j, :, n * TILE : (n + 1) * TILE] = nn(normed_t, dh[j, :, n * TILE : (n + 1) * TILE]).astype(BF)
    query_sum = PlaneSum(1, 0, feat_q)
    query_sum.begin()
    settle(EARLY)
    produce(EARLY + 1)
    query_sum.spread()
    line_step(9)
    line_step(10)
    total = out_sum.result()
    for i in range(2):
        mine[hidden_pairs, i] = total[:, i * TILE : (i + 1) * TILE]
    for copy in kv_sends:
        copy.wait()
    got = kv_qr[0].astype(F32) + kv_qr[1].astype(F32) + kv_qr[2].astype(F32) + kv_cr[0].astype(F32)
    grad_key = dk[:loc, :] + got[:, :HD]
    grad_value = dv[:loc, :] + got[:, HD:]
    first, second = grad_key[:, :half], grad_key[:, half:]
    turned_key = jnp.concatenate(
        [first * cos[...] + second * sin[...], second * cos[...] - first * sin[...]], axis=1
    )
    grad, gain_buf[0, 5:6, :HD] = norm_grad(k_pre[...], gk[...], turned_key)
    for j in range(2):
        dh[j, :, feat_q : feat_q + half] = grad[:, j * half : (j + 1) * half].astype(BF)
        dh[j, :, feat_q + half :] = grad_value[:, j * half : (j + 1) * half].astype(BF)
    ao[...] += nt(dh[0, :, feat_q:], parts[0, :, feat_q:qkv]) + nt(dh[1, :, feat_q:], parts[1, :, feat_q:qkv])
    for j in range(2):
        parts[j, :, feat_q:qkv] = nn(normed_t, dh[j, :, feat_q:]).astype(BF)
    key_sum = PlaneSum(2, feat_q, HD)
    key_sum.begin()
    grad, gain_buf[0, 0:1, :] = norm_grad(x[...].astype(F32), gains[0:1, :], ao[...])
    key_sum.spread()
    for copy in lo_copies:
        copy.wait_send()
    lo_own.wait()
    cut_t[...] = (grad + own[...]).astype(BF).T
    gt_copies, gt_own = give(cut_t, gt_out, gt_s, gt_r, loc_s.at[1])
    gain_copies = [
        remote(gain_buf.at[0], gain_in.at[j], gn_s.at[j], gn_r.at[j], d) for j, (_, d) in enumerate(others)
    ]
    for copy in gain_copies:
        copy.start()
    settle(EARLY + 1)
    line_step(11)
    line_step(12)
    line_step(13)
    total = query_sum.result()
    for i in range(2):
        mine[hidden_pairs + 1, i] = total[:, i * TILE : (i + 1) * TILE]
    line_step(14)
    line_step(15)
    total = key_sum.result()
    for i in range(2):
        a_mine[0, i] = total[i * depth // 2 : (i + 1) * depth // 2]
    for copy in gain_copies:
        copy.wait()
    gain_buf[1] = gain_buf[0] + sum(gain_in[j] for j in range(7))
    gain_copies = [
        remote(gain_buf.at[1], gain_in.at[7 + i], gn_s.at[7 + i], gn_r.at[7 + i], ((place + i + 1) % 4, row, col))
        for i in range(3 if on_line else 0)
    ]
    for copy in gain_copies:
        copy.start()

    for p in range(16, pairs):
        line_step(p)
    small.sent(0)
    small.add(0)
    line_rest(pairs)
    small.total(0)
    for p in range(pairs + 1, pairs + 4):
        line_rest(p)
    small.forward(0, False)
    for p in range(pairs + 4, pairs + LATE):
        line_rest(p)

    def drain(k, carry):
        line.drain(k)
        return carry

    lax.fori_loop(0, pairs, drain, 0)
    small.drain(0)
    for copy in gain_copies:
        copy.wait()
    gain_out[...] = gain_buf[1]
    for i in range(len(gain_copies)):
        gain_out[...] += gain_in[7 + i]
    for copy in lo_copies:
        copy.wait_recv()
    for copy in gt_copies:
        copy.wait()
    gt_own.wait()
    for copy in kv_core:
        copy.wait_send()


def attention_back(*args):
    dparts, pre_t, hh, lo, heads, q_pre, kv, bias, wa = (args[i] for i in (0, 1, 3, 7, 11, 12, 14, 15, 16))
    loc, width = lo.shape
    depth, feats = width // 4, wa.shape[2]
    hidden_pairs = 3 * hh.shape[1] // TILE
    pairs = hidden_pairs + 2
    keys = kv.shape[0]
    cut = width // 8
    dma = pltpu.SemaphoreType.DMA
    piece = (depth, TILE)
    rest = (depth // 2, TILE)
    struct = jax.ShapeDtypeStruct
    vmem = pltpu.VMEM
    return pl.pallas_call(
        back_kernel,
        out_shape=(
            struct((depth, 2 * hh.shape[1]), BF),
            struct((depth, 2 * hh.shape[1]), BF),
            struct((depth, 2 * hh.shape[1]), BF),
            struct((depth, feats), BF),
            struct((cut, keys), BF),
            struct((cut, keys), BF),
            struct((8, width), F32),
        ),
        in_specs=[any_spec()] * 17 + [vmem_spec()] * 7,
        out_specs=[any_spec()] * 6 + [vmem_spec()],
        scratch_shapes=[
            vmem((pairs, 2) + piece, BF),
            vmem((pairs, 2) + piece, BF),
            vmem((pairs,) + piece, BF),
            vmem(((hidden_pairs + 1) // 2,) + piece, BF),
            vmem((1, 2) + rest, BF),
            vmem((1, 2) + rest, BF),
            vmem((1,) + rest, BF),
            vmem((2, width, feats), BF),
            vmem((width, feats), BF),
            vmem((3 * depth, feats), BF),
            vmem((3, depth, feats), BF),
            vmem(dparts.shape, BF),
            vmem((2,) + pre_t.shape, BF),
            vmem((3, pre_t.shape[1], TILE), BF),
            vmem((3, 4) + piece, BF),
        ]
        + [vmem(args[i].shape, args[i].dtype) for i in (6, 7, 8, 9, 10, 11, 12, 13, 14, 15)]
        + [
            vmem((HD, keys), BF),
            vmem(heads.shape, BF),
            vmem((keys, HD), F32),
            vmem((keys, HD), F32),
            vmem((4, loc, 2 * HD), BF),
            vmem((3, loc, 2 * HD), BF),
            vmem((2, loc, feats - heads.shape[1] // 2), BF),
            vmem((width, loc), BF),
            vmem((2, 8, width), F32),
            vmem((10, 8, width), F32),
            dma((12,)), dma((3,)), dma((2,)), dma(()), dma((3,)), dma((3,)), dma((3, 2)), dma((hidden_pairs, 2)),
            dma((4,)), dma((4,)), dma((3,)), dma((3,)),
            dma((3, 4)), dma((3, 4)), dma((3, 3)), dma((3, 3)),
            dma((7,)), dma((7,)), dma((7,)), dma((7,)), dma((10,)), dma((10,)), dma((2,)),
        ]
        + line_sems(pairs)
        + line_sems(1),
        compiler_params=params(6),
        name="attention_back",
    )(*args)


def finish_kernel(gate_in, up_in, down_in, attn_in, tok_in, gate, up, down, wq, wk, wv, wo, tok):
    for src, dst in ((gate_in, gate), (up_in, up), (down_in, down)):
        dst[...] = src[:, : dst.shape[1]].astype(F32)
    at = 0
    for dst in (wq, wk, wv, wo):
        dst[...] = attn_in[:, at : at + dst.shape[1]].astype(F32)
        at += dst.shape[1]
    tok[...] = tok_in[...].astype(F32)


def finish(gate, up, down, attn, tok, hidden, widths):
    depth, cut = gate.shape[0], tok.shape[0]
    steps = cut // 48
    outs = [(depth, hidden)] * 3 + [(depth, width) for width in widths] + [tok.shape]

    def rows(shape):
        return pl.BlockSpec((shape[0] // steps, shape[1]), lambda i: (i, 0))

    return pl.pallas_call(
        finish_kernel,
        grid=(steps,),
        in_specs=[rows(array.shape) for array in (gate, up, down, attn, tok)],
        out_specs=[rows(shape) for shape in outs],
        out_shape=[jax.ShapeDtypeStruct(shape, F32) for shape in outs],
        compiler_params=pltpu.CompilerParams(vmem_limit_bytes=VMEM_LIMIT),
        name="finish",
    )(gate, up, down, attn, tok)


def body(
    tokens,
    cotangent,
    weight_query,
    weight_key,
    weight_value,
    weight_out,
    weight_gate,
    weight_up,
    weight_down,
    gain_input,
    gain_attn,
    gain_pre,
    gain_post,
    gain_query,
    gain_key,
    doc_lengths,
    block_size,
):
    cut = tokens.shape[1]
    row, col = lax.axis_index("row"), lax.axis_index("col")
    me = row * lax.axis_size("col") + col
    depth, hidden_half = weight_gate.shape
    q_half, kv_half = weight_query.shape[1], weight_key.shape[1]
    gain_block = jnp.pad(jnp.stack([gain_input, gain_attn, gain_pre, gain_post]), ((0, 4), (0, 0)))
    (
        w_hidden, w_attn, kv_all, bias, inputs, upstream, gains, query_pre, key_pre, log_total,
        cos_table, sin_table, head_bf, attn_out, residual, pre_normed,
    ) = attention_front(
        tokens.T, cotangent.T, gain_block, weight_query, weight_key, weight_value, weight_out.T,
        weight_gate, weight_up, weight_down.T, gain_query[None], gain_key[None], doc_lengths, block_size,
    )
    layer_rows, grad_g_post, grad_own, grad_parts, pre_t, grad_mlp_t, hidden, grad_gate, grad_up = mlp(
        pre_normed, residual, upstream, gains, w_hidden
    )
    sum_gate, sum_up, sum_down, attn_sum, layer_cut, token_cut, gain_sums = attention_back(
        grad_parts, pre_t, grad_mlp_t, hidden, grad_gate, grad_up, grad_own, layer_rows, attn_out, upstream,
        inputs, head_bf, query_pre, key_pre, kv_all, bias, w_attn, gains, gain_query[None], gain_key[None],
        log_total, cos_table, sin_table, grad_g_post,
    )
    if lax.axis_size("dp") != 4:
        sum_gate, sum_up, sum_down, attn_sum, gain_sums = (
            lax.psum(v.astype(F32), "dp") for v in (sum_gate, sum_up, sum_down, attn_sum, gain_sums)
        )
    grad_gate, grad_up, grad_down, grad_query, grad_key, grad_value, grad_out, grad_tokens = finish(
        sum_gate, sum_up, sum_down, attn_sum, token_cut, hidden_half, (q_half, kv_half, kv_half, q_half)
    )
    my_gains = lax.dynamic_slice_in_dim(gain_sums[:4], me * cut, cut, 1)
    return (
        layer_cut.T,
        grad_tokens.T,
        grad_query,
        grad_key,
        grad_value,
        grad_out.T,
        grad_gate,
        grad_up,
        grad_down.T,
        my_gains[0],
        my_gains[1],
        my_gains[2],
        my_gains[3],
        gain_sums[4, :HD],
        gain_sums[5, :HD],
    )


def solution(mesh):
    in_specs = (
        P("dp", ("row", "col")),
        P("dp", ("row", "col")),
        P("row", "col"),
        P("row", "col"),
        P("row", "col"),
        P("col", "row"),
        P("row", "col"),
        P("row", "col"),
        P("col", "row"),
        P(("row", "col")),
        P(("row", "col")),
        P(("row", "col")),
        P(("row", "col")),
        P(),
        P(),
        P("dp", None),
        P(),
    )
    out_specs = (
        P("dp", ("row", "col")),
        P("dp", ("row", "col")),
        P("row", "col"),
        P("row", "col"),
        P("row", "col"),
        P("col", "row"),
        P("row", "col"),
        P("row", "col"),
        P("col", "row"),
        P(("row", "col")),
        P(("row", "col")),
        P(("row", "col")),
        P(("row", "col")),
        P(),
        P(),
    )
    return jax.shard_map(body, mesh=mesh, in_specs=in_specs, out_specs=out_specs, check_vma=False)
```
